32 devices in a mesh: seq: 4 (over y, x), fsdp: 8 (over z, core).
Axes of the slice: x: 2, y: 2, z: 4, core: 2. Of those that a mesh axis runs over, the one named last changes fastest.
Arguments:
- tokens: bfloat16 [2, 2048, 2304], P(None, ('seq', 'fsdp')), may hold values from -6 to 6
- attn_weight: bfloat16 [6144, 2304], P('fsdp'), may hold values from -0.23570226 to 0.23570226
- norm_gains: bfloat16 [4, 2304], P(None, 'fsdp'), may hold values from 0.25 to 1.75
- ffn_weight: bfloat16 [9216, 3, 2304], P('fsdp'), may hold values from -0.125 to 0.125
- out_grad: bfloat16 [2, 2048, 2304], P(None, ('seq', 'fsdp')), may hold values from -6 to 6
Outputs:
- block_out: bfloat16 [2, 2048, 2304], P(None, ('seq', 'fsdp'))
- token_grad: float32 [2, 2048, 2304], P(None, ('seq', 'fsdp'))
- attn_weight_grad: float32 [6144, 2304], P('fsdp')
- gain_grad: float32 [4, 2304], P(None, 'fsdp')
- ffn_weight_grad: float32 [9216, 3, 2304], P('fsdp')
The draws below stay inside these ranges and needn't reach their ends.
All inputs are finite; a program needn't handle non-finite values.
Results may differ from the reference program's by a relative error of at most 0.025.
The reference program's roundings to bfloat16 on the way count: a program that leaves them out, or rounds other values in their place, can miss the bound.
Values may be sent and summed in bfloat16 or wider, within the bound.
No kernel may reach another device: no remote copies, remote signals or barrier semaphores. Data moves between devices by JAX's collectives and lax.ppermute only.
A program may use at most 320 MiB of HBM per device.

```python
import math
import jax
import jax.numpy as jnp
from jax import lax

D = 2304
HQ = 8
KVH = 4
HD = 256
FF = 9216
SEQS = 2
L = 2048
ATT_ROWS = 6144


def draw_attn_weight(key, part):
    key = jax.random.fold_in(key, 11)
    pick_key, value_key = jax.random.split(key)
    chosen = jax.random.randint(pick_key, (), 0, KVH)
    row_index = jnp.arange(ATT_ROWS, dtype=jnp.int32)
    head_of_row = row_index // HD
    group_size = HQ // KVH
    query_hit = (row_index < HQ * HD) & (head_of_row // group_size == chosen)
    key_hit = (row_index >= HQ * HD) & (row_index < HQ * HD + KVH * HD) & (head_of_row - HQ == chosen)
    factor = jnp.where(query_hit | key_hit, 2.0, 1.0).astype(jnp.float32)
    deviation = (D // 2) ** (-0.5)
    drawn_values = jnp.clip(jax.random.normal(value_key, (ATT_ROWS, D), jnp.float32), -4.0, 4.0)
    return (drawn_values * deviation * factor[:, None]).astype(jnp.bfloat16)


def steps_of(stream_key, shape, cuts, low, high):
    def one(position, shards_of):
        heights = jax.random.uniform(jax.random.fold_in(jax.random.fold_in(stream_key, 6), position), (shards_of,), jnp.float32, low / len(cuts), high / len(cuts))
        return jnp.repeat(jnp.exp(heights), shape[position] // shards_of).reshape((-1,) + (1,) * (len(shape) - position - 1))

    loudness = one(*cuts[0])
    for cut in cuts[1:]:
        loudness = loudness * one(*cut)
    return loudness


def gaussian(own_key, extent, spread, most, pieces=(), kind=jnp.bfloat16):
    entries = jax.random.normal(own_key, extent, jnp.float32) * spread
    if len(pieces) > 0:
        entries = steps_of(own_key, extent, pieces, -0.22, 0.18) * entries
    return jnp.clip(entries, min=-most, max=most).astype(kind)


def setup_inputs(seed: int = 0) -> dict:
    streams_of = jax.random.split(jax.random.key(seed), 6)
    return {
        "tokens": gaussian(streams_of[0], (SEQS, L, D), 1.0, 6.0, ((1, 32),)),
        "attn_weight": draw_attn_weight(jax.random.fold_in(streams_of[5], 71), 0),
        "norm_gains": jnp.clip(1.0 + 0.15 * jax.random.normal(streams_of[2], (4, D), jnp.float32), 0.25, 1.75).astype(jnp.bfloat16),
        "ffn_weight": gaussian(streams_of[3], (FF, 3, D), D ** -0.5, 0.125, ((0, 8),)),
        "out_grad": gaussian(streams_of[4], (SEQS, L, D), 1.0, 6.0, ((1, 32),)),
    }


@jax.custom_vjp
def low(v):
    return lax.optimization_barrier(v.astype(jnp.bfloat16)).astype(jnp.float32)

@jax.custom_vjp
def low_back(v):
    return v

def low_keep(v):
    return (low(v), None)

def low_pass(kept, grad):
    return (grad,)

def back_keep(v):
    return (v, None)

def back_low(kept, grad):
    return (low(grad),)
low.defvjp(low_keep, low_pass)
low_back.defvjp(back_keep, back_low)
soft_cap = 50.0
norm_eps = 1e-06
highest = lax.Precision.HIGHEST

def rms_scale(values, gain_row):
    return values * lax.rsqrt(lax.optimization_barrier(jnp.mean(values * values, axis=-1, keepdims=True)) + norm_eps) * gain_row

def attend_block(query_block, key_heads, value_heads, first_row):
    raw_scores = low_back(jnp.einsum('qhd,khd->hqk', query_block, key_heads, precision=highest) * HD ** (-0.5))
    capped = soft_cap * jnp.tanh(raw_scores / soft_cap)
    query_pos = first_row + jnp.arange(query_block.shape[0], dtype=jnp.int32)
    key_pos = jnp.arange(key_heads.shape[0], dtype=jnp.int32)
    causal = key_pos[None, :] <= query_pos[:, None]
    capped = jnp.where(causal[None], capped, -1e+30)
    row_max = lax.optimization_barrier(jnp.max(capped, axis=-1, keepdims=True))
    expanded = jnp.exp(capped - row_max)
    softmax_weights = low(expanded / lax.optimization_barrier(jnp.sum(expanded, axis=-1, keepdims=True)))
    return jnp.einsum('hqk,khd->qhd', softmax_weights, value_heads, precision=highest)

def attend_sequence(query_seq, key_seq, value_seq):
    length = query_seq.shape[0]
    block_size = math.gcd(length, 512)
    query_blocks = query_seq.reshape(length // block_size, block_size, HQ, HD)
    starts = jnp.arange(length // block_size, dtype=jnp.int32) * block_size
    checked = jax.checkpoint(attend_block)
    mixed_blocks = lax.map(lambda block_pair: checked(block_pair[0], key_seq, value_seq, block_pair[1]), (query_blocks, starts))
    return mixed_blocks.reshape(length, HQ, HD)

def forward(tokens, attn_weight, norm_gains, ffn_weight):
    query_width = HQ * HD
    kv_width = KVH * HD
    weight_q = attn_weight[:query_width]
    weight_k = attn_weight[query_width:query_width + kv_width]
    weight_v = attn_weight[query_width + kv_width:query_width + 2 * kv_width]
    weight_o = attn_weight[query_width + 2 * kv_width:]
    flat_tokens = tokens.reshape(-1, D)
    normed = low(rms_scale(flat_tokens, norm_gains[0]))

    def project(weight_rows):
        return low_back(low(jnp.dot(normed, weight_rows.T, precision=highest)))
    queries = project(weight_q).reshape(SEQS, L, HQ, HD)
    key_heads = project(weight_k).reshape(SEQS, L, KVH, HD)
    value_heads = project(weight_v).reshape(SEQS, L, KVH, HD)
    key_heads = jnp.repeat(key_heads, HQ // KVH, axis=2)
    value_heads = jnp.repeat(value_heads, HQ // KVH, axis=2)
    mixed_heads = lax.map(lambda triple: attend_sequence(triple[0], triple[1], triple[2]), (queries, key_heads, value_heads))
    mixed_heads = low_back(low(mixed_heads.reshape(-1, query_width)))
    attn_out = low_back(jnp.dot(mixed_heads, weight_o, precision=highest))
    residual = flat_tokens + rms_scale(attn_out, norm_gains[1])
    normed_ffn = low(rms_scale(residual, norm_gains[2]))
    gate_proj = low_back(jnp.dot(normed_ffn, ffn_weight[:, 0, :].T, precision=highest))
    up_proj = low_back(jnp.dot(normed_ffn, ffn_weight[:, 1, :].T, precision=highest))
    hidden = low(jax.nn.gelu(gate_proj, approximate=True) * up_proj)
    ffn_out = low_back(jnp.dot(hidden, ffn_weight[:, 2, :], precision=highest))
    result = residual + rms_scale(ffn_out, norm_gains[3])
    return result.reshape(SEQS, L, D)

def reference(tokens, attn_weight, norm_gains, ffn_weight, out_grad):
    inputs = (tokens.astype(jnp.float32), attn_weight.astype(jnp.float32), norm_gains.astype(jnp.float32), ffn_weight.astype(jnp.float32))
    result, pullback = jax.vjp(forward, *inputs)
    grads = pullback(out_grad.astype(jnp.float32))
    return (result.astype(jnp.bfloat16), grads[0], grads[1], grads[2], grads[3])
```

```python
import functools

import jax
import jax.numpy as jnp
import numpy as np
from jax import lax
from jax.experimental import pallas as pl
from jax.experimental.pallas import tpu as pltpu
from jax.sharding import PartitionSpec as P

HQ = 8
KVH = 4
HD = 256
GROUP = HQ // KVH
HALF = HD // 2

soft_cap = 50.0
norm_eps = 1e-06
bf16 = jnp.bfloat16
f32 = jnp.float32


def rms_scale(values, gain_row):
    return (
        values * lax.rsqrt(jnp.mean(values * values, axis=-1, keepdims=True) + norm_eps) * gain_row
    )


def norm_back(values, gain_row, cotangent):
    inverse = lax.rsqrt(jnp.mean(values * values, axis=-1, keepdims=True) + norm_eps)
    unit_rows = values * inverse
    scaled = cotangent * gain_row
    grad_values = inverse * (
        scaled - unit_rows * jnp.mean(scaled * unit_rows, axis=-1, keepdims=True)
    )
    return (grad_values, cotangent * unit_rows)


def gated_units(gate_proj, up_proj):
    return jax.nn.gelu(gate_proj, approximate=True) * up_proj


def dot_nt(a, b):
    return lax.dot_general(a, b, (((1,), (1,)), ((), ())), preferred_element_type=f32)


def dot_nn(a, b):
    return lax.dot_general(a, b, (((1,), (0,)), ((), ())), preferred_element_type=f32)


def dot_tn(a, b):
    return lax.dot_general(a, b, (((0,), (0,)), ((), ())), preferred_element_type=f32)


def stacked_heads(block):
    heads = block.shape[1] // HD
    return jnp.concatenate([block[:, h * HD : (h + 1) * HD] for h in range(heads)], axis=0)


def visible_of(block, own, shard, rows, keys, lines):
    shape = (lines, keys)
    row = lax.broadcasted_iota(jnp.int32, shape, 0) & (rows - 1)
    col = lax.broadcasted_iota(jnp.int32, shape, 1)
    return block * keys + col <= own * keys + shard * rows + row


def attend_kernel(shard_ref, q_ref, kv_ref, o_ref, lse_ref, score_ref):
    own = pl.program_id(1)
    shard = shard_ref[0]
    parts, _, _, rows, _ = kv_ref.shape
    keys = parts * rows
    queries = stacked_heads(q_ref[0, 0])
    lines = queries.shape[0]

    def score_step(block, top):
        key_block = kv_ref[:, block, 0, :, :HD].reshape(keys, HD)
        raw = dot_nt(queries, key_block) * HD ** (-0.5)
        capped = soft_cap * jnp.tanh(raw / soft_cap)
        capped = jnp.where(visible_of(block, own, shard, rows, keys, lines), capped, -1e30)
        score_ref[block] = capped
        return jnp.maximum(top, jnp.max(capped, axis=-1, keepdims=True))

    top = lax.fori_loop(0, own + 1, score_step, jnp.full((lines, 1), -3e38, f32))

    def sum_step(block, total):
        expanded = jnp.exp(score_ref[block] - top)
        score_ref[block] = expanded
        return total + jnp.sum(expanded, axis=-1, keepdims=True)

    total = lax.fori_loop(0, own + 1, sum_step, jnp.zeros((lines, 1), f32))
    inverse = 1.0 / total

    def mix_step(block, mixed):
        weights = (score_ref[block] * inverse).astype(bf16)
        value_block = kv_ref[:, block, 0, :, HD:].reshape(keys, HD)
        return mixed + dot_nn(weights, value_block)

    mixed = lax.fori_loop(0, own + 1, mix_step, jnp.zeros((lines, HD), f32))
    for h in range(lines // rows):
        o_ref[0, 0, :, h * HD : (h + 1) * HD] = mixed[h * rows : (h + 1) * rows].astype(bf16)
    lse_ref[0, 0] = jnp.broadcast_to(top + jnp.log(total), (lines, 128))


def attend_back_kernel(
    shard_ref, q_ref, do_ref, lse_ref, kv_ref, dq_ref, dkv_ref, weight_ref, dp_ref, acc_ref
):
    own = pl.program_id(1)
    shard = shard_ref[0]
    parts, blocks, _, rows, _ = kv_ref.shape
    keys = parts * rows
    queries = stacked_heads(q_ref[0, 0])
    grads = stacked_heads(do_ref[0, 0])
    lse = lse_ref[0, 0][:, :1]
    lines = queries.shape[0]

    @pl.when(own == 0)
    def _():
        acc_ref[...] = jnp.zeros_like(acc_ref)

    def first_step(block, delta):
        key_block = kv_ref[:, block, 0, :, :HD].reshape(keys, HD)
        value_block = kv_ref[:, block, 0, :, HD:].reshape(keys, HD)
        bounded = jnp.tanh(dot_nt(queries, key_block) * (HD ** (-0.5) / soft_cap))
        capped = jnp.where(
            visible_of(block, own, shard, rows, keys, lines), soft_cap * bounded, -1e30
        )
        weights = jnp.exp(capped - lse)
        grad_weights = dot_nt(grads, value_block)
        acc_ref[block, :, HD:] += dot_tn(weights.astype(bf16), grads)
        weight_ref[block] = weights * (1.0 - bounded * bounded)
        dp_ref[block] = grad_weights
        return delta + jnp.sum(weights * grad_weights, axis=-1, keepdims=True)

    delta = lax.fori_loop(0, own + 1, first_step, jnp.zeros((lines, 1), f32))

    def second_step(block, grad_query):
        key_block = kv_ref[:, block, 0, :, :HD].reshape(keys, HD)
        grad_raw = (weight_ref[block] * (dp_ref[block] - delta)).astype(bf16)
        acc_ref[block, :, :HD] += dot_tn(grad_raw, queries)
        return grad_query + dot_nn(grad_raw, key_block)

    grad_query = lax.fori_loop(
        0, own + 1, second_step, jnp.zeros((lines, HD), f32)
    ) * HD ** (-0.5)
    for h in range(lines // rows):
        dq_ref[0, 0, :, h * HD : (h + 1) * HD] = grad_query[h * rows : (h + 1) * rows].astype(bf16)

    @pl.when(own == blocks - 1)
    def _():
        for block in range(blocks):
            dkv_ref[:, block, 0, :, :HD] = (
                (acc_ref[block, :, :HD] * HD ** (-0.5)).astype(bf16).reshape(parts, rows, HD)
            )
            dkv_ref[:, block, 0, :, HD:] = (
                acc_ref[block, :, HD:].astype(bf16).reshape(parts, rows, HD)
            )


def attend(shard, queries, kv_all):
    blocks, seqs, rows, width = queries.shape
    lines = rows * width // HD
    parts = kv_all.shape[0]
    keys = parts * rows
    row_spec = pl.BlockSpec((1, 1, rows, width), lambda n, s, shard: (s, n, 0, 0))
    lse_spec = pl.BlockSpec((1, 1, lines, 128), lambda n, s, shard: (s, n, 0, 0))
    kv_spec = pl.BlockSpec((parts, blocks, 1, rows, 2 * HD), lambda n, s, shard: (0, 0, n, 0, 0))
    return pl.pallas_call(
        attend_kernel,
        grid_spec=pltpu.PrefetchScalarGridSpec(
            num_scalar_prefetch=1,
            grid=(seqs, blocks),
            in_specs=[row_spec, kv_spec],
            out_specs=[row_spec, lse_spec],
            scratch_shapes=[pltpu.VMEM((blocks, lines, keys), f32)],
        ),
        out_shape=[
            jax.ShapeDtypeStruct(queries.shape, bf16),
            jax.ShapeDtypeStruct((blocks, seqs, lines, 128), f32),
        ],
        compiler_params=pltpu.CompilerParams(vmem_limit_bytes=48 * 2**20),
        name="attend",
    )(shard, queries, kv_all)


def attend_back(shard, queries, grads, lse, kv_all):
    blocks, seqs, rows, width = queries.shape
    lines = rows * width // HD
    parts = kv_all.shape[0]
    keys = parts * rows
    row_spec = pl.BlockSpec((1, 1, rows, width), lambda n, s, shard: (s, n, 0, 0))
    lse_spec = pl.BlockSpec((1, 1, lines, 128), lambda n, s, shard: (s, n, 0, 0))
    deep = 2 if keys * blocks <= 4096 else 1
    kv_spec = pl.BlockSpec(
        (parts, blocks, 1, rows, 2 * HD),
        lambda n, s, shard: (0, 0, n, 0, 0),
        pipeline_mode=pl.Buffered(deep),
    )
    return pl.pallas_call(
        attend_back_kernel,
        grid_spec=pltpu.PrefetchScalarGridSpec(
            num_scalar_prefetch=1,
            grid=(seqs, blocks),
            in_specs=[row_spec, row_spec, lse_spec, kv_spec],
            out_specs=[row_spec, kv_spec],
            scratch_shapes=[
                pltpu.VMEM((blocks, lines, keys), f32),
                pltpu.VMEM((blocks, lines, keys), f32),
                pltpu.VMEM((blocks, keys, 2 * HD), f32),
            ],
        ),
        out_shape=[
            jax.ShapeDtypeStruct(queries.shape, bf16),
            jax.ShapeDtypeStruct(kv_all.shape, bf16),
        ],
        compiler_params=pltpu.CompilerParams(vmem_limit_bytes=56 * 2**20),
        name="attend_back",
    )(shard, queries, grads, lse, kv_all)


def widen_kernel(*refs):
    refs[-1][0] = refs[0][...].astype(f32)


def widen_plane(plane, index, planes, whole):
    rows, width = plane.shape
    step = rows // 4 if rows % 64 == 0 else rows
    specs = [pl.BlockSpec((step, width), lambda i: (i, 0))]
    args = [plane]
    aliases = {}
    if whole is not None:
        specs.append(pl.BlockSpec(memory_space=pl.ANY))
        args.append(whole)
        aliases = {1: 0}
    return pl.pallas_call(
        widen_kernel,
        grid=(rows // step,),
        in_specs=specs,
        out_specs=pl.BlockSpec((1, step, width), lambda i: (index, i, 0)),
        out_shape=jax.ShapeDtypeStruct((planes, rows, width), f32),
        input_output_aliases=aliases,
        compiler_params=pltpu.CompilerParams(vmem_limit_bytes=40 * 2**20),
        name="widen",
    )(*args)


def granules_of(column, columns):
    per = HQ // columns
    first = column * per
    return (
        [first + i for i in range(per)]
        + [HQ + first // GROUP, HQ + KVH + first // GROUP]
        + [HQ + 2 * KVH + first + i for i in range(per)]
    )


def route(columns, chips, per_chip):
    items = len(granules_of(0, columns))
    urgent = items - HQ // columns
    source = [[g // per_chip for g in granules_of(c, columns)] for c in range(columns)]
    held = [[{k for k in range(items) if source[c][k] == z} for z in range(chips)] for c in range(columns)]
    steps = []
    urgent_steps = None
    while any(len(held[c][z]) < items for c in range(columns) for z in range(chips)):
        moves = {}
        for c in range(columns):
            for z in range(chips):
                for core, way in ((0, 1), (1, -1)):
                    if not 0 <= z + way < chips:
                        continue
                    ready = [
                        k
                        for k in held[c][z]
                        if k not in held[c][z + way] and (source[c][k] - z) * way <= 0
                    ]
                    if ready:
                        moves[c, z, core] = min(
                            ready, key=lambda k: (k >= urgent, abs(source[c][k] - z), k)
                        )
        for (c, z, core), k in moves.items():
            held[c][z + (1, -1)[core]].add(k)
        steps.append(moves)
        done = all(k in held[c][z] for c in range(columns) for z in range(chips) for k in range(urgent))
        if done and urgent_steps is None:
            urgent_steps = len(steps)
    return steps, urgent_steps


def pick_kernel(cands, which_ref, slot_ref, *refs):
    out_ref = refs[-1]
    wanted = which_ref[pl.program_id(0)]
    for code in cands:

        @pl.when(wanted == code)
        def _(code=code):
            out_ref[...] = refs[code][...]


def pick(places, sources, device, devices):
    names = []
    which = np.zeros((devices, len(places)), np.int32)
    slot = np.zeros((devices, len(places)), np.int32)
    for k, place in enumerate(places):
        for d in range(devices):
            name, at = place.get(d, ("mine", 0))
            if name not in names:
                names.append(name)
            which[d, k] = names.index(name)
            slot[d, k] = at
    _, rows, width = sources["mine"].shape
    table = jnp.asarray(np.concatenate([which, slot], axis=1))[device]
    block = (1, rows // 4, width)

    def spec(code):
        def index(k, r, which_ref, slot_ref):
            hit = which_ref[k] == code
            return jnp.where(hit, slot_ref[k], 0), jnp.where(hit, r, 0), 0

        return pl.BlockSpec(block, index)

    return pl.pallas_call(
        functools.partial(pick_kernel, range(len(names))),
        grid_spec=pltpu.PrefetchScalarGridSpec(
            num_scalar_prefetch=2,
            grid=(len(places), 4),
            in_specs=[spec(code) for code in range(len(names))],
            out_specs=pl.BlockSpec(block, lambda k, r, which_ref, slot_ref: (k, r, 0)),
        ),
        out_shape=jax.ShapeDtypeStruct((len(places), rows, width), bf16),
        compiler_params=pltpu.CompilerParams(vmem_limit_bytes=40 * 2**20),
        name="pick",
    )(table[: len(places)], table[len(places) :], *[sources[name] for name in names])


def routed_weights(attn_weight, column, shard, columns, shards, between):
    rows, width = attn_weight.shape
    count = rows // HD
    chips = shards // 2
    devices = columns * shards
    device = column * shards + shard
    swap = [(f, f ^ 1) for f in range(shards)]
    items = len(granules_of(0, columns))
    urgent = items - HQ // columns
    steps, urgent_steps = route(columns, chips, 2 * count)
    mine = attn_weight.reshape(count, HD, width)
    sources = {"mine": mine, "theirs": lax.ppermute(mine, "fsdp", swap)}
    at = [{} for _ in range(items)]
    for c in range(columns):
        for f in range(shards):
            for k, g in enumerate(granules_of(c, columns)):
                if g // (2 * count) == f // 2:
                    at[k][c * shards + f] = ("mine" if g // count == f else "theirs", g % count)
    first = None
    for number, moves in enumerate(steps):
        place = {}
        pairs = []
        for (c, z, core), k in moves.items():
            here = c * shards + 2 * z + core
            to = here + (2, -2)[core]
            place[here] = at[k][here]
            pairs.append((here, to))
            at[k][to] = ("got%d" % number, 0)
            at[k][to ^ 1] = ("swapped%d" % number, 0)
        got = lax.ppermute(pick([place], sources, device, devices), ("seq", "fsdp"), pairs)
        got = between(number, got)
        if 0 < number < urgent_steps:
            before = "swapped%d" % (number - 1)
            got, sources[before] = lax.optimization_barrier((got, sources[before]))
        sources["got%d" % number] = got
        sources["swapped%d" % number] = lax.ppermute(got, "fsdp", swap)
        if number + 1 == urgent_steps:
            first = pick(at[:urgent], sources, device, devices)
            first, sources = between(None, (first, sources))
    return first, pick(at[urgent:], sources, device, devices)


def column_weights(attn_weight, column, shard, columns, shards, between):
    rows, width = attn_weight.shape
    per = HQ // columns
    if rows % HD == 0 and shards == 8 and columns == 4:
        return routed_weights(attn_weight, column, shard, columns, shards, between)
    whole = lax.all_gather(attn_weight, "fsdp", axis=0, tiled=True).reshape(-1, HD, width)
    table = np.array([granules_of(c, columns) for c in range(columns)], np.int32)
    place = jnp.asarray(table)[column]
    taken = jnp.concatenate(
        [lax.dynamic_slice_in_dim(whole, place[k], 1, 0) for k in range(table.shape[1])], axis=0
    )
    return taken[: per + 2], taken[per + 2 :]


def ring_of(chips):
    return [0] + list(range(1, chips, 2)) + [z for z in range(chips - 1, 0, -1) if z % 2 == 0]


def ring_tables(shards):
    chips = shards // 2
    order = ring_of(chips)
    spot = {z: p for p, z in enumerate(order)}
    pairs = [
        (2 * z + c, 2 * order[(spot[z] + 1) % chips] + c) for z in range(chips) for c in range(2)
    ]
    behind = np.array(
        [[order[(spot[f // 2] - t) % chips] for t in range(chips + 1)] for f in range(shards)],
        np.int32,
    )
    return chips, pairs, behind


def ring_gather(block, shard, shards):
    chips, pairs, behind = ring_tables(shards)
    swap = [(f, f ^ 1) for f in range(shards)]
    source = jnp.asarray(behind)[shard]
    core = shard % 2
    out = jnp.zeros((shards,) + block.shape, block.dtype)
    held = block
    for t in range(chips):
        if t:
            held = lax.ppermute(held, "fsdp", pairs)
        other = lax.ppermute(held, "fsdp", swap)
        out = lax.dynamic_update_index_in_dim(out, held, 2 * source[t] + core, 0)
        out = lax.dynamic_update_index_in_dim(out, other, 2 * source[t] + 1 - core, 0)
    return out


def ring_scatter(parts, shard, shards):
    chips, pairs, behind = ring_tables(shards)
    swap = [(f, f ^ 1) for f in range(shards)]
    target = jnp.asarray(behind)[shard]
    core = shard % 2
    paired = parts.reshape((chips, 2) + parts.shape[1:])
    mine = lax.dynamic_index_in_dim(paired, core, 1, keepdims=False)
    other = lax.ppermute(
        lax.dynamic_index_in_dim(paired, 1 - core, 1, keepdims=False), "fsdp", swap
    )

    def local_sum(t):
        return lax.dynamic_index_in_dim(mine, target[t], 0, keepdims=False).astype(
            f32
        ) + lax.dynamic_index_in_dim(other, target[t], 0, keepdims=False).astype(f32)

    total = local_sum(1)
    for t in range(1, chips):
        total = lax.ppermute(total.astype(bf16), "fsdp", pairs).astype(f32) + local_sum(t + 1)
    return total


def partners(columns, bit):
    return [(c, c ^ bit) for c in range(columns)]


def column_scatter(parts):
    half = parts.shape[-1] // 2
    done = []
    for first, second, cut in ((1, 2, slice(0, half)), (2, 1, slice(half, None))):
        low = parts[..., cut].astype(bf16)
        got = lax.ppermute(
            jnp.concatenate([low[first : first + 1], low[3:]], axis=0), "seq", partners(4, first)
        )
        keep = parts[0, ..., cut] + got[0].astype(f32)
        away = parts[second, ..., cut] + got[1].astype(f32)
        done.append(
            keep + lax.ppermute(away.astype(bf16), "seq", partners(4, second)).astype(f32)
        )
    return jnp.concatenate(done, axis=-1)


def sum_everywhere(value, columns, shards):
    for axis, count in (("fsdp", shards), ("seq", columns)):
        bit = 1
        while bit < count:
            value = value + lax.ppermute(value, axis, [(c, c ^ bit) for c in range(count)])
            bit *= 2
    return value


def local(tokens, attn_weight, norm_gains, ffn_weight, out_grad):
    seqs, rows, width = tokens.shape
    columns = lax.axis_size("seq")
    shards = lax.axis_size("fsdp")
    column = lax.axis_index("seq")
    shard = lax.axis_index("fsdp")
    core = shard % 2
    per = HQ // columns
    own_rows = seqs * rows
    swap = [(f, f ^ 1) for f in range(shards)]
    shard_arg = shard.astype(jnp.int32).reshape(1)

    def whole_weights(granules, near, far):
        cut = granules.shape[0] // 2
        come = {
            (0, 1): near[0],
            (0, 2): far[0][0],
            (0, 3): far[0][1],
            (1, 2): near[1],
            (1, 1): far[1][0],
            (1, 3): far[1][1],
        }
        outs = []
        for begin, end in ((0, per + 2), (per + 2, 2 * per + 2)):
            out = jnp.zeros((columns, end - begin, 2, HALF, width), bf16)
            full = granules[begin:end].reshape(1, end - begin, 2, HALF, width)
            outs.append(lax.dynamic_update_slice(out, full, (column, 0, 0, 0, 0)))
        for (part, hop), lane in come.items():
            other = lax.ppermute(lane, "fsdp", swap)
            for half, piece in ((core, lane), (1 - core, other)):
                for i, (begin, end) in enumerate(((0, per + 2), (per + 2, 2 * per + 2))):
                    low, high = max(begin, part * cut), min(end, (part + 1) * cut)
                    if low < high:
                        chosen = piece[low - part * cut : high - part * cut]
                        outs[i] = lax.dynamic_update_slice(
                            outs[i],
                            chosen.reshape(1, high - low, 1, HALF, width),
                            (column ^ hop, low - begin, half, 0, 0),
                        )
        return outs[0].reshape(-1, width), outs[1].reshape(-1, width)

    token_slices = lax.all_gather(tokens, "seq", axis=0)
    gain_rows = lax.all_gather(norm_gains, "fsdp", axis=1, tiled=True).astype(f32)
    normed_slices = rms_scale(
        token_slices.reshape(-1, width).astype(f32), gain_rows[0]
    ).astype(bf16)
    heads = None

    def between(step, value):
        nonlocal gain_rows, normed_slices, heads
        if step == 0:
            value, gain_rows = lax.optimization_barrier((value, gain_rows))
        if step == 2:
            value, normed_slices = lax.optimization_barrier((value, normed_slices))
        if step is None:
            heads = dot_nt(normed_slices, value[0].reshape(-1, width)).astype(bf16)
            heads, value = lax.optimization_barrier((heads, value))
        return value

    weight_in, weight_out = column_weights(
        attn_weight, column, shard, columns, shards, between
    )
    if heads is None:
        heads = dot_nt(normed_slices, weight_in.reshape(-1, width)).astype(bf16)
    heads = heads.reshape(columns, seqs, rows, (per + 2) * HD)
    queries = heads[..., : per * HD]
    kv_all = lax.all_gather(heads[..., per * HD :], "fsdp", axis=0)

    mixed, lse = attend(shard_arg, queries, kv_all)
    mixed_rows = lax.all_to_all(mixed, "seq", split_axis=0, concat_axis=0, tiled=True)
    mixed_rows = mixed_rows.transpose(1, 2, 0, 3).reshape(own_rows, HQ * HD)
    weight_out_rows = weight_out.reshape(-1, width)
    if columns == 4:
        by_partner = jnp.concatenate(
            [lax.dynamic_slice_in_dim(mixed, column ^ k, 1, 0) for k in range(columns)], axis=0
        ).reshape(columns * own_rows, per * HD)
        attn_out = column_scatter(
            dot_nn(by_partner, weight_out_rows).reshape(columns, own_rows, width)
        )
    else:
        attn_out = lax.psum_scatter(
            dot_nn(mixed.reshape(-1, per * HD), weight_out_rows).astype(bf16),
            "seq",
            scatter_dimension=0,
            tiled=True,
        ).astype(f32)
    flat_tokens = tokens.reshape(-1, width).astype(f32)
    flat_cot = out_grad.reshape(-1, width).astype(f32)
    residual = flat_tokens + rms_scale(attn_out, gain_rows[1])
    normed_ffn = rms_scale(residual, gain_rows[2]).astype(bf16)

    granules = jnp.concatenate([weight_in, weight_out], axis=0)
    if columns == 4:
        lanes = lax.dynamic_index_in_dim(
            granules.reshape(-1, 2, HALF, width), core, 1, keepdims=False
        )
        lanes, normed_ffn = lax.optimization_barrier((lanes, normed_ffn))
        cut = lanes.shape[0] // 2
        lanes = (lanes[:cut], lanes[cut:])
        near = tuple(
            lax.ppermute(lane, "seq", partners(4, bit)) for lane, bit in zip(lanes, (1, 2))
        )
    ffn_in = lax.all_gather(normed_ffn, "fsdp", axis=0, tiled=True)
    gate_up = jnp.einsum("td,fgd->tgf", ffn_in, ffn_weight[:, :2], preferred_element_type=f32)
    hidden = gated_units(gate_up[:, 0], gate_up[:, 1]).astype(bf16)
    if columns == 4:
        hidden, near = lax.optimization_barrier((hidden, near))
        far = tuple(
            lax.ppermute(jnp.stack([lane, got]), "seq", partners(4, bit))
            for lane, got, bit in zip(lanes, near, (2, 1))
        )
    branch = dot_nn(hidden, ffn_weight[:, 2])
    ffn_out = lax.psum_scatter(
        branch.astype(bf16), "fsdp", scatter_dimension=0, tiled=True
    ).astype(f32)
    if columns == 4:
        ffn_out, far = lax.optimization_barrier((ffn_out, far))
        weight_in_all, weight_out_all = whole_weights(granules, near, far)
    else:
        whole = lax.all_gather(granules, "seq", axis=0)
        weight_in_all = whole[:, : per + 2].reshape(-1, width)
        weight_out_all = whole[:, per + 2 :].reshape(-1, width)
    result = residual + rms_scale(ffn_out, gain_rows[3])
    block_out = result.astype(bf16).reshape(tokens.shape)
    grad_ffn, gain_terms = norm_back(ffn_out, gain_rows[3], flat_cot)
    gain_last = jnp.sum(gain_terms, axis=0)
    grad_ffn_all = lax.all_gather(grad_ffn.astype(bf16), "fsdp", axis=0, tiled=True)
    grad_ffn_all, weight_in_all, weight_out_all = lax.optimization_barrier(
        (grad_ffn_all, weight_in_all, weight_out_all)
    )
    down_part = dot_tn(hidden, grad_ffn_all).astype(bf16)
    grad_ffn_all, down_part = lax.optimization_barrier((grad_ffn_all, down_part))
    normed_own = rms_scale(flat_tokens, gain_rows[0]).astype(bf16)
    normed_own, grad_ffn_all = lax.optimization_barrier((normed_own, grad_ffn_all))
    normed_all = ring_gather(normed_own, shard, shards).reshape(-1, width)
    grad_hidden = dot_nt(grad_ffn_all, ffn_weight[:, 2])
    unused, gated_pull = jax.vjp(gated_units, gate_up[:, 0], gate_up[:, 1])
    grad_gate, grad_up = gated_pull(grad_hidden)
    grad_gate_up = jnp.stack([grad_gate, grad_up], axis=1).astype(bf16)
    gate_part = dot_tn(grad_gate_up[:, 0], ffn_in).astype(bf16)
    up_part = dot_tn(grad_gate_up[:, 1], ffn_in).astype(bf16)
    grad_gate_up, gate_part, up_part, normed_all = lax.optimization_barrier(
        (grad_gate_up, gate_part, up_part, normed_all)
    )
    gate_grad, up_grad, down_grad = lax.psum((gate_part, up_part, down_part), "seq")
    grad_in = jnp.einsum(
        "tgf,fgd->td", grad_gate_up, ffn_weight[:, :2], preferred_element_type=f32
    )
    grad_normed_ffn = ring_scatter(
        grad_in.astype(bf16).reshape(shards, own_rows, width), shard, shards
    )

    grad_mid, gain_pre_ffn = norm_back(residual, gain_rows[2], grad_normed_ffn)
    grad_residual = flat_cot + grad_mid
    grad_attn, gain_post_attn = norm_back(attn_out, gain_rows[1], grad_residual)
    grad_attn_low = grad_attn.astype(bf16)
    grad_mixed = (
        dot_nt(grad_attn_low, weight_out_all).astype(bf16).reshape(seqs, rows, columns, per * HD)
    )
    grad_heads = lax.all_to_all(
        grad_mixed.transpose(2, 0, 1, 3), "seq", split_axis=0, concat_axis=0, tiled=True
    )
    grad_attn_all = ring_gather(grad_attn_low, shard, shards).reshape(-1, width)
    grad_queries, grad_kv = attend_back(shard_arg, queries, grad_heads, lse, kv_all)
    grad_kv, grad_attn_all = lax.optimization_barrier((grad_kv, grad_attn_all))
    grad_kv_own = ring_scatter(
        grad_kv.reshape(shards, columns * own_rows, 2 * HD), shard, shards
    ).astype(bf16).reshape(columns, seqs, rows, 2 * HD)
    grad_proj = lax.all_to_all(
        jnp.concatenate([grad_queries, grad_kv_own], axis=-1),
        "seq",
        split_axis=0,
        concat_axis=0,
        tiled=True,
    )
    grad_rows = grad_proj.reshape(columns, own_rows, (per + 2) * HD).transpose(1, 0, 2)
    grad_normed = dot_nn(grad_rows.reshape(own_rows, -1), weight_in_all)
    grad_tokens, gain_pre_attn = norm_back(flat_tokens, gain_rows[0], grad_normed)
    token_grad = (grad_residual + grad_tokens).reshape(tokens.shape)


    def shared(copies):
        if columns == KVH:
            return copies.reshape(own_rows, -1)
        summed = copies.reshape(own_rows, KVH, columns // KVH, HD).astype(f32).sum(axis=2)
        return summed.astype(bf16).reshape(own_rows, -1)

    weight_cols = jnp.concatenate(
        [
            grad_rows[:, :, : per * HD].reshape(own_rows, -1),
            shared(grad_rows[:, :, per * HD : (per + 1) * HD]),
            shared(grad_rows[:, :, (per + 1) * HD :]),
            mixed_rows,
        ],
        axis=1,
    )
    shard_cols = attn_weight.shape[0]
    col_all = lax.all_to_all(
        weight_cols.reshape(own_rows, shards, shard_cols).transpose(1, 0, 2),
        "fsdp",
        split_axis=0,
        concat_axis=0,
        tiled=True,
    ).reshape(-1, shard_cols)
    is_out = (shard * shard_cols + jnp.arange(shard_cols)) >= (HQ + 2 * KVH) * HD
    attn_grad = dot_tn(jnp.where(is_out, 0, col_all), normed_all) + dot_tn(
        jnp.where(is_out, col_all, 0), grad_attn_all
    )
    attn_grad_low, gate_grad, up_grad, down_grad = lax.optimization_barrier(
        (attn_grad.astype(bf16), gate_grad, up_grad, down_grad)
    )
    attn_total = lax.psum(attn_grad_low, "seq").astype(f32)
    ffn_grad = widen_plane(down_grad, 2, 3, None)
    ffn_grad = widen_plane(gate_grad, 0, 3, ffn_grad)
    ffn_grad = widen_plane(up_grad, 1, 3, ffn_grad)
    ffn_grad = ffn_grad.transpose(1, 0, 2)
    gain_grad = jnp.stack(
        [
            jnp.sum(gain_pre_attn, axis=0),
            jnp.sum(gain_post_attn, axis=0),
            jnp.sum(gain_pre_ffn, axis=0),
            gain_last,
        ]
    )
    gain_total = lax.dynamic_slice_in_dim(
        sum_everywhere(gain_grad, columns, shards),
        shard * norm_gains.shape[1],
        norm_gains.shape[1],
        1,
    )
    return (block_out, token_grad, attn_total, gain_total, ffn_grad)


def solution(mesh):
    in_specs = (
        P(None, ("seq", "fsdp"), None),
        P("fsdp", None),
        P(None, "fsdp"),
        P("fsdp", None, None),
        P(None, ("seq", "fsdp"), None),
    )
    out_specs = (
        P(None, ("seq", "fsdp"), None),
        P(None, ("seq", "fsdp"), None),
        P("fsdp", None),
        P(None, "fsdp"),
        P("fsdp", None, None),
    )
    return jax.shard_map(local, mesh=mesh, in_specs=in_specs, out_specs=out_specs, check_vma=False)
```

```python
import functools

import jax
import jax.numpy as jnp
import numpy as np
from jax import lax
from jax.experimental import pallas as pl
from jax.experimental.pallas import tpu as pltpu
from jax.sharding import PartitionSpec as P

HQ = 8
KVH = 4
HD = 256
GROUP = HQ // KVH
HALF = HD // 2

soft_cap = 50.0
norm_eps = 1e-06
bf16 = jnp.bfloat16
f32 = jnp.float32


def rms_scale(values, gain_row):
    return (
        values * lax.rsqrt(jnp.mean(values * values, axis=-1, keepdims=True) + norm_eps) * gain_row
    )


def norm_back(values, gain_row, cotangent):
    inverse = lax.rsqrt(jnp.mean(values * values, axis=-1, keepdims=True) + norm_eps)
    unit_rows = values * inverse
    scaled = cotangent * gain_row
    grad_values = inverse * (
        scaled - unit_rows * jnp.mean(scaled * unit_rows, axis=-1, keepdims=True)
    )
    return (grad_values, cotangent * unit_rows)


def gated_units(gate_proj, up_proj):
    return jax.nn.gelu(gate_proj, approximate=True) * up_proj


def dot_nt(a, b):
    return lax.dot_general(a, b, (((1,), (1,)), ((), ())), preferred_element_type=f32)


def dot_nn(a, b):
    return lax.dot_general(a, b, (((1,), (0,)), ((), ())), preferred_element_type=f32)


def dot_tn(a, b):
    return lax.dot_general(a, b, (((0,), (0,)), ((), ())), preferred_element_type=f32)


def stacked_heads(block):
    heads = block.shape[1] // HD
    return jnp.concatenate([block[:, h * HD : (h + 1) * HD] for h in range(heads)], axis=0)


def visible_of(block, own, shard, rows, keys, lines):
    shape = (lines, keys)
    row = lax.broadcasted_iota(jnp.int32, shape, 0) & (rows - 1)
    col = lax.broadcasted_iota(jnp.int32, shape, 1)
    return block * keys + col <= own * keys + shard * rows + row


def attend_kernel(shard_ref, q_ref, kv_ref, o_ref, lse_ref, score_ref):
    own = pl.program_id(1)
    shard = shard_ref[0]
    parts, _, _, rows, _ = kv_ref.shape
    keys = parts * rows
    queries = stacked_heads(q_ref[0, 0])
    lines = queries.shape[0]

    def score_step(block, top):
        key_block = kv_ref[:, block, 0, :, :HD].reshape(keys, HD)
        raw = dot_nt(queries, key_block) * HD ** (-0.5)
        capped = soft_cap * jnp.tanh(raw / soft_cap)
        capped = jnp.where(visible_of(block, own, shard, rows, keys, lines), capped, -1e30)
        score_ref[block] = capped
        return jnp.maximum(top, jnp.max(capped, axis=-1, keepdims=True))

    top = lax.fori_loop(0, own + 1, score_step, jnp.full((lines, 1), -3e38, f32))

    def sum_step(block, total):
        expanded = jnp.exp(score_ref[block] - top)
        score_ref[block] = expanded
        return total + jnp.sum(expanded, axis=-1, keepdims=True)

    total = lax.fori_loop(0, own + 1, sum_step, jnp.zeros((lines, 1), f32))
    inverse = 1.0 / total

    def mix_step(block, mixed):
        weights = (score_ref[block] * inverse).astype(bf16)
        value_block = kv_ref[:, block, 0, :, HD:].reshape(keys, HD)
        return mixed + dot_nn(weights, value_block)

    mixed = lax.fori_loop(0, own + 1, mix_step, jnp.zeros((lines, HD), f32))
    for h in range(lines // rows):
        o_ref[0, 0, :, h * HD : (h + 1) * HD] = mixed[h * rows : (h + 1) * rows].astype(bf16)
    lse_ref[0, 0] = jnp.broadcast_to(top + jnp.log(total), (lines, 128))


def attend_back_kernel(
    shard_ref, q_ref, do_ref, lse_ref, kv_ref, dq_ref, dkv_ref, weight_ref, dp_ref, acc_ref
):
    own = pl.program_id(1)
    shard = shard_ref[0]
    parts, blocks, _, rows, _ = kv_ref.shape
    keys = parts * rows
    queries = stacked_heads(q_ref[0, 0])
    grads = stacked_heads(do_ref[0, 0])
    lse = lse_ref[0, 0][:, :1]
    lines = queries.shape[0]

    @pl.when(own == 0)
    def _():
        acc_ref[...] = jnp.zeros_like(acc_ref)

    def first_step(block, delta):
        key_block = kv_ref[:, block, 0, :, :HD].reshape(keys, HD)
        value_block = kv_ref[:, block, 0, :, HD:].reshape(keys, HD)
        bounded = jnp.tanh(dot_nt(queries, key_block) * (HD ** (-0.5) / soft_cap))
        capped = jnp.where(
            visible_of(block, own, shard, rows, keys, lines), soft_cap * bounded, -1e30
        )
        weights = jnp.exp(capped - lse)
        grad_weights = dot_nt(grads, value_block)
        acc_ref[block, :, HD:] += dot_tn(weights.astype(bf16), grads)
        weight_ref[block] = weights * (1.0 - bounded * bounded)
        dp_ref[block] = grad_weights
        return delta + jnp.sum(weights * grad_weights, axis=-1, keepdims=True)

    delta = lax.fori_loop(0, own + 1, first_step, jnp.zeros((lines, 1), f32))

    def second_step(block, grad_query):
        key_block = kv_ref[:, block, 0, :, :HD].reshape(keys, HD)
        grad_raw = (weight_ref[block] * (dp_ref[block] - delta)).astype(bf16)
        acc_ref[block, :, :HD] += dot_tn(grad_raw, queries)
        return grad_query + dot_nn(grad_raw, key_block)

    grad_query = lax.fori_loop(
        0, own + 1, second_step, jnp.zeros((lines, HD), f32)
    ) * HD ** (-0.5)
    for h in range(lines // rows):
        dq_ref[0, 0, :, h * HD : (h + 1) * HD] = grad_query[h * rows : (h + 1) * rows].astype(bf16)

    @pl.when(own == blocks - 1)
    def _():
        for block in range(blocks):
            dkv_ref[:, block, 0, :, :HD] = (
                (acc_ref[block, :, :HD] * HD ** (-0.5)).astype(bf16).reshape(parts, rows, HD)
            )
            dkv_ref[:, block, 0, :, HD:] = (
                acc_ref[block, :, HD:].astype(bf16).reshape(parts, rows, HD)
            )


def attend(shard, queries, kv_all):
    blocks, seqs, rows, width = queries.shape
    lines = rows * width // HD
    parts = kv_all.shape[0]
    keys = parts * rows
    row_spec = pl.BlockSpec((1, 1, rows, width), lambda n, s, shard: (s, n, 0, 0))
    lse_spec = pl.BlockSpec((1, 1, lines, 128), lambda n, s, shard: (s, n, 0, 0))
    kv_spec = pl.BlockSpec((parts, blocks, 1, rows, 2 * HD), lambda n, s, shard: (0, 0, n, 0, 0))
    return pl.pallas_call(
        attend_kernel,
        grid_spec=pltpu.PrefetchScalarGridSpec(
            num_scalar_prefetch=1,
            grid=(seqs, blocks),
            in_specs=[row_spec, kv_spec],
            out_specs=[row_spec, lse_spec],
            scratch_shapes=[pltpu.VMEM((blocks, lines, keys), f32)],
        ),
        out_shape=[
            jax.ShapeDtypeStruct(queries.shape, bf16),
            jax.ShapeDtypeStruct((blocks, seqs, lines, 128), f32),
        ],
        compiler_params=pltpu.CompilerParams(vmem_limit_bytes=48 * 2**20),
        name="attend",
    )(shard, queries, kv_all)


def attend_back(shard, queries, grads, lse, kv_all):
    blocks, seqs, rows, width = queries.shape
    lines = rows * width // HD
    parts = kv_all.shape[0]
    keys = parts * rows
    row_spec = pl.BlockSpec((1, 1, rows, width), lambda n, s, shard: (s, n, 0, 0))
    lse_spec = pl.BlockSpec((1, 1, lines, 128), lambda n, s, shard: (s, n, 0, 0))
    deep = 2 if keys * blocks <= 4096 else 1
    kv_spec = pl.BlockSpec(
        (parts, blocks, 1, rows, 2 * HD),
        lambda n, s, shard: (0, 0, n, 0, 0),
        pipeline_mode=pl.Buffered(deep),
    )
    return pl.pallas_call(
        attend_back_kernel,
        grid_spec=pltpu.PrefetchScalarGridSpec(
            num_scalar_prefetch=1,
            grid=(seqs, blocks),
            in_specs=[row_spec, row_spec, lse_spec, kv_spec],
            out_specs=[row_spec, kv_spec],
            scratch_shapes=[
                pltpu.VMEM((blocks, lines, keys), f32),
                pltpu.VMEM((blocks, lines, keys), f32),
                pltpu.VMEM((blocks, keys, 2 * HD), f32),
            ],
        ),
        out_shape=[
            jax.ShapeDtypeStruct(queries.shape, bf16),
            jax.ShapeDtypeStruct(kv_all.shape, bf16),
        ],
        compiler_params=pltpu.CompilerParams(vmem_limit_bytes=56 * 2**20),
        name="attend_back",
    )(shard, queries, grads, lse, kv_all)


def widen_kernel(*refs):
    refs[-1][0] = refs[0][...].astype(f32)


def widen_plane(plane, index, planes, whole):
    rows, width = plane.shape
    step = rows // 4 if rows % 64 == 0 else rows
    specs = [pl.BlockSpec((step, width), lambda i: (i, 0))]
    args = [plane]
    aliases = {}
    if whole is not None:
        specs.append(pl.BlockSpec(memory_space=pl.ANY))
        args.append(whole)
        aliases = {1: 0}
    return pl.pallas_call(
        widen_kernel,
        grid=(rows // step,),
        in_specs=specs,
        out_specs=pl.BlockSpec((1, step, width), lambda i: (index, i, 0)),
        out_shape=jax.ShapeDtypeStruct((planes, rows, width), f32),
        input_output_aliases=aliases,
        compiler_params=pltpu.CompilerParams(vmem_limit_bytes=40 * 2**20),
        name="widen",
    )(*args)


def granules_of(column, columns):
    per = HQ // columns
    first = column * per
    return (
        [first + i for i in range(per)]
        + [HQ + first // GROUP, HQ + KVH + first // GROUP]
        + [HQ + 2 * KVH + first + i for i in range(per)]
    )


def route(columns, chips, per_chip):
    items = len(granules_of(0, columns))
    urgent = items - HQ // columns
    source = [[g // per_chip for g in granules_of(c, columns)] for c in range(columns)]
    held = [[{k for k in range(items) if source[c][k] == z} for z in range(chips)] for c in range(columns)]
    steps = []
    urgent_steps = None
    while any(len(held[c][z]) < items for c in range(columns) for z in range(chips)):
        moves = {}
        for c in range(columns):
            for z in range(chips):
                for core, way in ((0, 1), (1, -1)):
                    if not 0 <= z + way < chips:
                        continue
                    ready = [
                        k
                        for k in held[c][z]
                        if k not in held[c][z + way] and (source[c][k] - z) * way <= 0
                    ]
                    if ready:
                        moves[c, z, core] = min(
                            ready, key=lambda k: (k >= urgent, abs(source[c][k] - z), k)
                        )
        for (c, z, core), k in moves.items():
            held[c][z + (1, -1)[core]].add(k)
        steps.append(moves)
        done = all(k in held[c][z] for c in range(columns) for z in range(chips) for k in range(urgent))
        if done and urgent_steps is None:
            urgent_steps = len(steps)
    return steps, urgent_steps


def chosen(places, devices):
    names = []
    which = np.zeros((devices, len(places)), np.int32)
    slot = np.zeros((devices, len(places)), np.int32)
    for k, place in enumerate(places):
        for d in range(devices):
            name, at = place.get(d, ("mine", 0))
            if name not in names:
                names.append(name)
            which[d, k] = names.index(name)
            slot[d, k] = at
    return names, which, slot


def fetch(cands, which_ref, slot_ref, sources, place, buffer, sem):
    for code in cands[place]:

        @pl.when(which_ref[place] == code)
        def _(code=code):
            pltpu.make_async_copy(sources[code].at[slot_ref[place]], buffer, sem).start()


def pick_kernel(cands, which_ref, slot_ref, *refs):
    out_ref, buffers, in_sems, out_sems = refs[-4:]
    count, deep = len(cands), buffers.shape[0]

    def begin(k):
        at = k % deep
        fetch(cands, which_ref, slot_ref, refs, k, buffers.at[at], in_sems.at[at])

    def leaving(k):
        at = k % deep
        return pltpu.make_async_copy(buffers.at[at], out_ref.at[k], out_sems.at[at])

    for k in range(min(deep, count)):
        begin(k)
    for k in range(count):
        at = k % deep
        pltpu.make_async_copy(buffers.at[at], buffers.at[at], in_sems.at[at]).wait()
        leaving(k).start()
        again = k - deep // 2
        if again >= 0 and again + deep < count:
            leaving(again).wait()
            begin(again + deep)
    for k in range(max(0, count - deep), count):
        leaving(k).wait()


def project_kernel(cands, which_ref, slot_ref, rows_ref, *refs):
    out_ref, buffers, sems = refs[-3:]
    rows = buffers.shape[1]
    for k in range(len(cands)):
        fetch(cands, which_ref, slot_ref, refs, k, buffers.at[k], sems.at[k])
    for k in range(len(cands)):
        pltpu.make_async_copy(buffers.at[k], buffers.at[k], sems.at[k]).wait()
        out_ref[:, k * rows : (k + 1) * rows] = dot_nt(rows_ref[...], buffers[k]).astype(bf16)


def apply_kernel(cands, which_ref, slot_ref, rows_ref, *refs):
    out_ref, buffers, sems = refs[-3:]
    _, rows, width = buffers.shape
    for k in range(len(cands)):
        fetch(cands, which_ref, slot_ref, refs, k, buffers.at[k], sems.at[k])
    for k in range(len(cands)):
        pltpu.make_async_copy(buffers.at[k], buffers.at[k], sems.at[k]).wait()
    step = width // 3 if width % 384 == 0 else width
    for low in range(0, width, step):
        total = dot_nn(rows_ref[:, :rows], buffers[0, :, low : low + step])
        for k in range(1, len(cands)):
            total += dot_nn(
                rows_ref[:, k * rows : (k + 1) * rows], buffers[k, :, low : low + step]
            )
        out_ref[:, low : low + step] = total.astype(bf16)


def pick(places, sources, device, devices, kind="pick", rows_in=None):
    names, which, slot = chosen(places, devices)
    _, rows, width = sources["mine"].shape
    table = jnp.asarray(np.concatenate([which, slot], axis=1))[device]
    count = len(places)
    cands = [sorted(set(which[:, k].tolist())) for k in range(count)]
    kernel = {"pick": pick_kernel, "project": project_kernel, "apply": apply_kernel}[kind]
    args = [sources[name] for name in names]
    in_specs = [pl.BlockSpec(memory_space=pl.ANY)] * len(names)
    if kind == "pick":
        deep = min(count, 8)
        out_spec = pl.BlockSpec(memory_space=pl.ANY)
        out_shape = (count, rows, width)
        sems = [pltpu.SemaphoreType.DMA((deep,)), pltpu.SemaphoreType.DMA((deep,))]
    else:
        deep = count
        args = [rows_in] + args
        in_specs = [pl.BlockSpec(memory_space=pltpu.VMEM)] + in_specs
        out_spec = pl.BlockSpec(memory_space=pltpu.VMEM)
        out_shape = (rows_in.shape[0], count * rows if kind == "project" else width)
        sems = [pltpu.SemaphoreType.DMA((deep,))]
    return pl.pallas_call(
        functools.partial(kernel, cands),
        grid_spec=pltpu.PrefetchScalarGridSpec(
            num_scalar_prefetch=2,
            grid=(1,),
            in_specs=in_specs,
            out_specs=out_spec,
            scratch_shapes=[pltpu.VMEM((deep, rows, width), bf16)] + sems,
        ),
        out_shape=jax.ShapeDtypeStruct(out_shape, bf16),
        compiler_params=pltpu.CompilerParams(vmem_limit_bytes=58 * 2**20),
        name=kind,
    )(table[:count], table[count:], *args)


def routed_weights(attn_weight, column, shard, columns, shards, between):
    rows, width = attn_weight.shape
    count = rows // HD
    chips = shards // 2
    devices = columns * shards
    device = column * shards + shard
    swap = [(f, f ^ 1) for f in range(shards)]
    items = len(granules_of(0, columns))
    urgent = items - HQ // columns
    steps, urgent_steps = route(columns, chips, 2 * count)
    mine = attn_weight.reshape(count, HD, width)
    theirs = between("start", lax.ppermute(mine, "fsdp", swap))
    sources = {"mine": mine, "theirs": theirs}
    at = [{} for _ in range(items)]
    for c in range(columns):
        for f in range(shards):
            for k, g in enumerate(granules_of(c, columns)):
                if g // (2 * count) == f // 2:
                    at[k][c * shards + f] = ("mine" if g // count == f else "theirs", g % count)
    sends = []
    for number, moves in enumerate(steps):
        own, passed, pairs = {}, {}, []
        for (c, z, core), k in moves.items():
            here = c * shards + 2 * z + core
            to = here + (2, -2)[core]
            name, slot = at[k][here]
            if name in ("mine", "theirs"):
                own[here] = (name, slot)
            else:
                passed[here] = name
            pairs.append((here, to))
            at[k][to] = ("got%d" % number, 0)
            at[k][to ^ 1] = ("swapped%d" % number, 0)
        sends.append((own, passed, pairs))
    with_own = [n for n in range(1, len(sends)) if sends[n][0]]
    own_first = pick([sends[0][0]], sources, device, devices)
    own_later = None
    for number, (own, passed, pairs) in enumerate(sends):
        if number == 0:
            piece = own_first
        else:
            names = sorted(set(passed.values()))
            code = np.zeros((devices,), np.int32)
            for d, name in passed.items():
                code[d] = 1 + names.index(name)
            here = jnp.asarray(code)[device]
            piece = sources[names[-1]]
            for i, name in enumerate(names[:-1]):
                piece = jnp.where(here == 1 + i, sources[name], piece)
            if number in with_own:
                place = with_own.index(number)
                piece = jnp.where(here == 0, own_later[place : place + 1], piece)
        got = lax.ppermute(piece, ("seq", "fsdp"), pairs)
        if number == 0:
            own_later = pick([sends[n][0] for n in with_own], sources, device, devices)
            got, own_later = lax.optimization_barrier((got, own_later))
        if number < urgent_steps:
            got = between(number, got)
        if 0 < number < urgent_steps:
            before = "swapped%d" % (number - 1)
            got, sources[before] = lax.optimization_barrier((got, sources[before]))
        sources["got%d" % number] = got
        if number < urgent_steps:
            sources["swapped%d" % number] = lax.ppermute(got, "fsdp", swap)
        if number + 1 == urgent_steps:
            ready = dict(sources)
            made = between(
                None,
                lambda times: pick(at[:urgent], ready, device, devices, "project", times),
            )

    def first(after):
        held, after = lax.optimization_barrier((ready, after))
        return pick(at[:urgent], held, device, devices)

    held = None

    def times_rest(rows_in):
        nonlocal held
        held, rows_in = lax.optimization_barrier((sources, rows_in))
        for number in range(urgent_steps, len(steps)):
            held["swapped%d" % number] = lax.ppermute(held["got%d" % number], "fsdp", swap)
        return pick(at[urgent:], held, device, devices, "apply", rows_in)

    def others(after):
        kept, after = lax.optimization_barrier((held, after))
        return pick(at[urgent:], kept, device, devices)

    return made, first, times_rest, others


def column_weights(attn_weight, column, shard, columns, shards, between):
    rows, width = attn_weight.shape
    per = HQ // columns
    if rows % HD == 0 and shards == 8 and columns == 4:
        return routed_weights(attn_weight, column, shard, columns, shards, between)
    whole = lax.all_gather(attn_weight, "fsdp", axis=0, tiled=True).reshape(-1, HD, width)
    table = np.array([granules_of(c, columns) for c in range(columns)], np.int32)
    place = jnp.asarray(table)[column]
    taken = jnp.concatenate(
        [lax.dynamic_slice_in_dim(whole, place[k], 1, 0) for k in range(table.shape[1])], axis=0
    )
    made = between(
        None, lambda times: dot_nt(times, taken[: per + 2].reshape(-1, width)).astype(bf16)
    )
    return (
        made,
        lambda after: taken[: per + 2],
        lambda rows_in: dot_nn(rows_in, taken[per + 2 :].reshape(-1, width)).astype(bf16),
        lambda after: taken[per + 2 :],
    )


def ring_of(chips):
    return [0] + list(range(1, chips, 2)) + [z for z in range(chips - 1, 0, -1) if z % 2 == 0]


def ring_tables(shards):
    chips = shards // 2
    order = ring_of(chips)
    spot = {z: p for p, z in enumerate(order)}
    pairs = [
        (2 * z + c, 2 * order[(spot[z] + 1) % chips] + c) for z in range(chips) for c in range(2)
    ]
    behind = np.array(
        [[order[(spot[f // 2] - t) % chips] for t in range(chips + 1)] for f in range(shards)],
        np.int32,
    )
    return chips, pairs, behind


def ring_gather(block, shard, shards, beside=None):
    chips, pairs, behind = ring_tables(shards)
    swap = [(f, f ^ 1) for f in range(shards)]
    source = jnp.asarray(behind)[shard]
    core = shard % 2
    out = jnp.zeros((shards,) + block.shape, block.dtype)
    held = block
    for t in range(chips):
        if t:
            held = lax.ppermute(held, "fsdp", pairs)
            held = beside(t, held) if beside else held
        other = lax.ppermute(held, "fsdp", swap)
        out = lax.dynamic_update_index_in_dim(out, held, 2 * source[t] + core, 0)
        out = lax.dynamic_update_index_in_dim(out, other, 2 * source[t] + 1 - core, 0)
    return out


def ring_scatter(parts, shard, shards):
    chips, pairs, behind = ring_tables(shards)
    swap = [(f, f ^ 1) for f in range(shards)]
    target = jnp.asarray(behind)[shard]
    core = shard % 2
    paired = parts.reshape((chips, 2) + parts.shape[1:])
    mine = lax.dynamic_index_in_dim(paired, core, 1, keepdims=False)
    other = lax.ppermute(
        lax.dynamic_index_in_dim(paired, 1 - core, 1, keepdims=False), "fsdp", swap
    )

    def local_sum(t):
        return lax.dynamic_index_in_dim(mine, target[t], 0, keepdims=False).astype(
            f32
        ) + lax.dynamic_index_in_dim(other, target[t], 0, keepdims=False).astype(f32)

    total = local_sum(1)
    for t in range(1, chips):
        total = lax.ppermute(total.astype(bf16), "fsdp", pairs).astype(f32) + local_sum(t + 1)
    return total


def partners(columns, bit):
    return [(c, c ^ bit) for c in range(columns)]


def column_scatter(parts):
    half = parts.shape[-1] // 2
    done = []
    for first, second, cut in ((1, 2, slice(0, half)), (2, 1, slice(half, None))):
        low = parts[..., cut]
        got = lax.ppermute(
            jnp.concatenate([low[first : first + 1], low[3:]], axis=0), "seq", partners(4, first)
        )
        keep = low[0].astype(f32) + got[0].astype(f32)
        away = low[second].astype(f32) + got[1].astype(f32)
        done.append(
            keep + lax.ppermute(away.astype(bf16), "seq", partners(4, second)).astype(f32)
        )
    return jnp.concatenate(done, axis=-1)


def sum_everywhere(value, columns, shards):
    for axis, count in (("fsdp", shards), ("seq", columns)):
        bit = 1
        while bit < count:
            value = value + lax.ppermute(value, axis, [(c, c ^ bit) for c in range(count)])
            bit *= 2
    return value


def local(tokens, attn_weight, norm_gains, ffn_weight, out_grad):
    seqs, rows, width = tokens.shape
    columns = lax.axis_size("seq")
    shards = lax.axis_size("fsdp")
    column = lax.axis_index("seq")
    shard = lax.axis_index("fsdp")
    core = shard % 2
    per = HQ // columns
    own_rows = seqs * rows
    swap = [(f, f ^ 1) for f in range(shards)]
    shard_arg = shard.astype(jnp.int32).reshape(1)

    def core_half(granules):
        return lax.dynamic_index_in_dim(
            granules.reshape(-1, 2, HALF, width), core, 1, keepdims=False
        )

    def round_start(granules):
        lanes = core_half(granules)
        cut = lanes.shape[0] // 2
        lanes = (lanes[:cut], lanes[cut:])
        near = tuple(
            lax.ppermute(lane, "seq", partners(4, bit)) for lane, bit in zip(lanes, (1, 2))
        )
        return lanes, near

    def round_on(lanes, near):
        return tuple(
            tuple(lax.ppermute(piece, "seq", partners(4, bit)) for piece in pieces)
            for pieces, bit in zip(zip(lanes, near), (2, 1))
        )

    def all_columns(granules, near, far):
        count = granules.shape[0]
        cut = count // 2
        come = {
            (0, 1): near[0],
            (0, 2): far[0][0],
            (0, 3): far[0][1],
            (1, 2): near[1],
            (1, 1): far[1][0],
            (1, 3): far[1][1],
        }
        sources = {"mine": granules.reshape(2 * count, HALF, width)}
        for (part, hop), lane in come.items():
            sources["own%d%d" % (part, hop)] = lane
            sources["other%d%d" % (part, hop)] = lax.ppermute(lane, "fsdp", swap)
        places = []
        for home in range(columns):
            for k in range(count):
                for half in range(2):
                    place = {}
                    for c in range(columns):
                        for f in range(shards):
                            part, hop = int(k >= cut), home ^ c
                            whose = "own" if f % 2 == half else "other"
                            place[c * shards + f] = (
                                ("%s%d%d" % (whose, part, hop), k - part * cut)
                                if hop
                                else ("mine", 2 * k + half)
                            )
                    places.append(place)
        device = column * shards + shard
        return pick(places, sources, device, columns * shards).reshape(-1, width)

    token_slices = lax.all_gather(tokens, "seq", axis=0)
    gain_rows = lax.all_gather(norm_gains, "fsdp", axis=1, tiled=True).astype(f32)
    normed_slices = None

    def between(step, value):
        nonlocal gain_rows, normed_slices
        if step == 1:
            value, gain_rows = lax.optimization_barrier((value, gain_rows))
            normed_slices = rms_scale(
                token_slices.reshape(-1, width).astype(f32), gain_rows[0]
            ).astype(bf16)
        if step == 2:
            value, normed_slices = lax.optimization_barrier((value, normed_slices))
        if step is None:
            if normed_slices is None:
                normed_slices = rms_scale(
                    token_slices.reshape(-1, width).astype(f32), gain_rows[0]
                ).astype(bf16)
            return value(normed_slices)
        return value

    heads, first_weights, times_out, out_weights = column_weights(
        attn_weight, column, shard, columns, shards, between
    )
    heads = heads.reshape(columns, seqs, rows, (per + 2) * HD)
    queries = heads[..., : per * HD]
    kv_all = lax.all_gather(heads[..., per * HD :], "fsdp", axis=0)
    weight_in = first_weights(heads)
    if columns == 4:
        in_lanes, in_near = round_start(weight_in)
        kv_all, in_lanes = lax.optimization_barrier((kv_all, in_lanes))

    mixed, lse = attend(shard_arg, queries, kv_all)
    if columns == 4:
        by_partner = jnp.concatenate(
            [lax.dynamic_slice_in_dim(mixed, column ^ k, 1, 0) for k in range(columns)], axis=0
        ).reshape(columns * own_rows, per * HD)
        attn_out = column_scatter(times_out(by_partner).reshape(columns, own_rows, width))
    else:
        attn_out = lax.psum_scatter(
            times_out(mixed.reshape(-1, per * HD)),
            "seq",
            scatter_dimension=0,
            tiled=True,
        ).astype(f32)
    flat_tokens = tokens.reshape(-1, width).astype(f32)
    flat_cot = out_grad.reshape(-1, width).astype(f32)
    residual = flat_tokens + rms_scale(attn_out, gain_rows[1])
    normed_ffn = rms_scale(residual, gain_rows[2]).astype(bf16)

    if columns == 4:
        normed_ffn, in_near = lax.optimization_barrier((normed_ffn, in_near))
        in_far = round_on(in_lanes, in_near)
    mixed_later, normed_ffn = lax.optimization_barrier((mixed, normed_ffn))
    weight_out = out_weights(normed_ffn)
    ffn_in = lax.all_gather(normed_ffn, "fsdp", axis=0, tiled=True)
    mixed_rows = lax.all_to_all(mixed_later, "seq", split_axis=0, concat_axis=0, tiled=True)
    mixed_rows = mixed_rows.transpose(1, 2, 0, 3).reshape(own_rows, HQ * HD)
    if columns == 4:
        out_lanes, out_near = round_start(weight_out)
        ffn_in, out_lanes, mixed_rows = lax.optimization_barrier((ffn_in, out_lanes, mixed_rows))
    gate_up = jnp.einsum("td,fgd->tgf", ffn_in, ffn_weight[:, :2], preferred_element_type=f32)
    hidden = gated_units(gate_up[:, 0], gate_up[:, 1]).astype(bf16)
    if columns == 4:
        hidden, out_near = lax.optimization_barrier((hidden, out_near))
        out_far = round_on(out_lanes, out_near)
    branch = dot_nn(hidden, ffn_weight[:, 2]).astype(bf16)
    if columns == 4:
        branch, in_far = lax.optimization_barrier((branch, in_far))
    ffn_out = lax.psum_scatter(branch, "fsdp", scatter_dimension=0, tiled=True).astype(f32)
    if columns == 4:
        weight_in_all = all_columns(weight_in, in_near, in_far)
        ffn_out, weight_in_all = lax.optimization_barrier((ffn_out, weight_in_all))
    else:
        weight_in_all = lax.all_gather(weight_in, "seq", axis=0).reshape(-1, width)
        weight_out_all = lax.all_gather(weight_out, "seq", axis=0).reshape(-1, width)
    result = residual + rms_scale(ffn_out, gain_rows[3])
    block_out = result.astype(bf16).reshape(tokens.shape)
    grad_ffn, gain_terms = norm_back(ffn_out, gain_rows[3], flat_cot)
    gain_last = jnp.sum(gain_terms, axis=0)
    grad_ffn_all = lax.all_gather(grad_ffn.astype(bf16), "fsdp", axis=0, tiled=True)
    if columns == 4:
        weight_out_all = all_columns(weight_out, out_near, out_far)
        grad_ffn_all, weight_out_all = lax.optimization_barrier((grad_ffn_all, weight_out_all))

    normed_own = rms_scale(flat_tokens, gain_rows[0]).astype(bf16)
    grad_ffn_all, normed_own = lax.optimization_barrier((grad_ffn_all, normed_own))
    kept = {}

    def beside(step, held):
        if step == 1:
            part = dot_tn(hidden, grad_ffn_all).astype(bf16)
            held, kept["down"], kept["all"] = lax.optimization_barrier((held, part, grad_ffn_all))
        if step == 2:
            grad_hidden = dot_nt(kept["all"], ffn_weight[:, 2])
            unused, gated_pull = jax.vjp(gated_units, gate_up[:, 0], gate_up[:, 1])
            grad_gate, grad_up = gated_pull(grad_hidden)
            part = jnp.stack([grad_gate, grad_up], axis=1).astype(bf16)
            held, kept["units"] = lax.optimization_barrier((held, part))
        if step == 3:
            parts = (
                dot_tn(kept["units"][:, 0], ffn_in).astype(bf16),
                dot_tn(kept["units"][:, 1], ffn_in).astype(bf16),
            )
            held, kept["up"], kept["units"] = lax.optimization_barrier(
                (held, parts, kept["units"])
            )
        return held

    normed_all = ring_gather(normed_own, shard, shards, beside).reshape(-1, width)
    grad_gate_up = kept["units"]
    gate_grad, up_grad, down_grad = lax.psum((*kept["up"], kept["down"]), "seq")

    def attention_back():
        grad_in = jnp.einsum(
            "tgf,fgd->td", grad_gate_up, ffn_weight[:, :2], preferred_element_type=f32
        )
        grad_normed_ffn = ring_scatter(
            grad_in.astype(bf16).reshape(shards, own_rows, width), shard, shards
        )
        grad_mid, gain_pre_ffn = norm_back(residual, gain_rows[2], grad_normed_ffn)
        grad_residual = flat_cot + grad_mid
        grad_attn, gain_post_attn = norm_back(attn_out, gain_rows[1], grad_residual)
        grad_attn_low = grad_attn.astype(bf16)
        grad_mixed = (
            dot_nt(grad_attn_low, weight_out_all)
            .astype(bf16)
            .reshape(seqs, rows, columns, per * HD)
        )
        grad_heads = lax.all_to_all(
            grad_mixed.transpose(2, 0, 1, 3), "seq", split_axis=0, concat_axis=0, tiled=True
        )
        grad_attn_all = ring_gather(grad_attn_low, shard, shards).reshape(-1, width)
        grad_queries, grad_kv = attend_back(shard_arg, queries, grad_heads, lse, kv_all)
        grad_kv, grad_attn_all = lax.optimization_barrier((grad_kv, grad_attn_all))
        grad_kv_own = (
            ring_scatter(grad_kv.reshape(shards, columns * own_rows, 2 * HD), shard, shards)
            .astype(bf16)
            .reshape(columns, seqs, rows, 2 * HD)
        )
        grad_proj = lax.all_to_all(
            jnp.concatenate([grad_queries, grad_kv_own], axis=-1),
            "seq",
            split_axis=0,
            concat_axis=0,
            tiled=True,
        )
        grad_rows = grad_proj.reshape(columns, own_rows, (per + 2) * HD).transpose(1, 0, 2)
        grad_normed = dot_nn(grad_rows.reshape(own_rows, -1), weight_in_all)
        grad_tokens, gain_pre_attn = norm_back(flat_tokens, gain_rows[0], grad_normed)
        token_grad = (grad_residual + grad_tokens).reshape(tokens.shape)

        def shared(copies):
            if columns == KVH:
                return copies.reshape(own_rows, -1)
            summed = copies.reshape(own_rows, KVH, columns // KVH, HD).astype(f32).sum(axis=2)
            return summed.astype(bf16).reshape(own_rows, -1)

        weight_cols = jnp.concatenate(
            [
                grad_rows[:, :, : per * HD].reshape(own_rows, -1),
                shared(grad_rows[:, :, per * HD : (per + 1) * HD]),
                shared(grad_rows[:, :, (per + 1) * HD :]),
                mixed_rows,
            ],
            axis=1,
        )
        shard_cols = attn_weight.shape[0]
        col_all = lax.all_to_all(
            weight_cols.reshape(own_rows, shards, shard_cols).transpose(1, 0, 2),
            "fsdp",
            split_axis=0,
            concat_axis=0,
            tiled=True,
        ).reshape(-1, shard_cols)
        is_out = (shard * shard_cols + jnp.arange(shard_cols)) >= (HQ + 2 * KVH) * HD
        attn_grad = dot_tn(jnp.where(is_out, 0, col_all), normed_all) + dot_tn(
            jnp.where(is_out, col_all, 0), grad_attn_all
        )
        gain_grad = jnp.stack(
            [
                jnp.sum(gain_pre_attn, axis=0),
                jnp.sum(gain_post_attn, axis=0),
                jnp.sum(gain_pre_ffn, axis=0),
                gain_last,
            ]
        )
        return attn_grad.astype(bf16), gain_grad, token_grad

    def nothing():
        return (
            jnp.zeros(attn_weight.shape, bf16),
            jnp.zeros((4, width), f32),
            jnp.zeros(tokens.shape, f32),
        )

    attn_grad, gain_grad, token_grad = lax.cond(
        shard < 2**20, attention_back, nothing
    )
    attn_grad, gate_grad, up_grad, down_grad = lax.optimization_barrier(
        (attn_grad, gate_grad, up_grad, down_grad)
    )
    attn_total = lax.psum(attn_grad, "seq").astype(f32)
    ffn_grad = widen_plane(down_grad, 2, 3, None)
    ffn_grad = widen_plane(gate_grad, 0, 3, ffn_grad)
    ffn_grad = widen_plane(up_grad, 1, 3, ffn_grad)
    ffn_grad = ffn_grad.transpose(1, 0, 2)
    gain_total = lax.dynamic_slice_in_dim(
        sum_everywhere(gain_grad, columns, shards),
        shard * norm_gains.shape[1],
        norm_gains.shape[1],
        1,
    )
    return (block_out, token_grad, attn_total, gain_total, ffn_grad)


def solution(mesh):
    in_specs = (
        P(None, ("seq", "fsdp"), None),
        P("fsdp", None),
        P(None, "fsdp"),
        P("fsdp", None, None),
        P(None, ("seq", "fsdp"), None),
    )
    out_specs = (
        P(None, ("seq", "fsdp"), None),
        P(None, ("seq", "fsdp"), None),
        P("fsdp", None),
        P(None, "fsdp"),
        P("fsdp", None, None),
    )
    return jax.shard_map(local, mesh=mesh, in_specs=in_specs, out_specs=out_specs, check_vma=False)
```

```python
import functools

import jax
import jax.numpy as jnp
import numpy as np
from jax import lax
from jax.experimental import pallas as pl
from jax.experimental.pallas import tpu as pltpu
from jax.sharding import PartitionSpec as P

HQ = 8
KVH = 4
HD = 256
GROUP = HQ // KVH
HALF = HD // 2

soft_cap = 50.0
norm_eps = 1e-06
bf16 = jnp.bfloat16
f32 = jnp.float32


def rms_scale(values, gain_row):
    return (
        values * lax.rsqrt(jnp.mean(values * values, axis=-1, keepdims=True) + norm_eps) * gain_row
    )


def norm_back(values, gain_row, cotangent):
    inverse = lax.rsqrt(jnp.mean(values * values, axis=-1, keepdims=True) + norm_eps)
    unit_rows = values * inverse
    scaled = cotangent * gain_row
    grad_values = inverse * (
        scaled - unit_rows * jnp.mean(scaled * unit_rows, axis=-1, keepdims=True)
    )
    return (grad_values, cotangent * unit_rows)


def gated_units(gate_proj, up_proj):
    return jax.nn.gelu(gate_proj, approximate=True) * up_proj


def dot_nt(a, b):
    return lax.dot_general(a, b, (((1,), (1,)), ((), ())), preferred_element_type=f32)


def dot_nn(a, b):
    return lax.dot_general(a, b, (((1,), (0,)), ((), ())), preferred_element_type=f32)


def dot_tn(a, b):
    return lax.dot_general(a, b, (((0,), (0,)), ((), ())), preferred_element_type=f32)


def stacked_heads(block):
    heads = block.shape[1] // HD
    return jnp.concatenate([block[:, h * HD : (h + 1) * HD] for h in range(heads)], axis=0)


def visible_of(block, own, shard, rows, keys, lines):
    shape = (lines, keys)
    row = lax.broadcasted_iota(jnp.int32, shape, 0) & (rows - 1)
    col = lax.broadcasted_iota(jnp.int32, shape, 1)
    return block * keys + col <= own * keys + shard * rows + row


def attend_kernel(shard_ref, q_ref, kv_ref, o_ref, lse_ref, score_ref):
    own = pl.program_id(1)
    shard = shard_ref[0]
    parts, _, _, rows, _ = kv_ref.shape
    keys = parts * rows
    queries = stacked_heads(q_ref[0, 0])
    lines = queries.shape[0]

    def score_step(block, top):
        key_block = kv_ref[:, block, 0, :, :HD].reshape(keys, HD)
        raw = dot_nt(queries, key_block) * HD ** (-0.5)
        capped = soft_cap * jnp.tanh(raw / soft_cap)
        capped = jnp.where(visible_of(block, own, shard, rows, keys, lines), capped, -1e30)
        score_ref[block] = capped
        return jnp.maximum(top, jnp.max(capped, axis=-1, keepdims=True))

    top = lax.fori_loop(0, own + 1, score_step, jnp.full((lines, 1), -3e38, f32))

    def sum_step(block, total):
        expanded = jnp.exp(score_ref[block] - top)
        score_ref[block] = expanded
        return total + jnp.sum(expanded, axis=-1, keepdims=True)

    total = lax.fori_loop(0, own + 1, sum_step, jnp.zeros((lines, 1), f32))
    inverse = 1.0 / total

    def mix_step(block, mixed):
        weights = (score_ref[block] * inverse).astype(bf16)
        value_block = kv_ref[:, block, 0, :, HD:].reshape(keys, HD)
        return mixed + dot_nn(weights, value_block)

    mixed = lax.fori_loop(0, own + 1, mix_step, jnp.zeros((lines, HD), f32))
    for h in range(lines // rows):
        o_ref[0, 0, :, h * HD : (h + 1) * HD] = mixed[h * rows : (h + 1) * rows].astype(bf16)
    lse_ref[0, 0] = jnp.broadcast_to(top + jnp.log(total), (lines, 128))


def attend_back_kernel(
    shard_ref, q_ref, do_ref, lse_ref, kv_ref, dq_ref, dkv_ref, weight_ref, dp_ref, acc_ref
):
    own = pl.program_id(1)
    shard = shard_ref[0]
    parts, blocks, _, rows, _ = kv_ref.shape
    keys = parts * rows
    queries = stacked_heads(q_ref[0, 0])
    grads = stacked_heads(do_ref[0, 0])
    lse = lse_ref[0, 0][:, :1]
    lines = queries.shape[0]

    @pl.when(own == 0)
    def _():
        acc_ref[...] = jnp.zeros_like(acc_ref)

    def first_step(block, delta):
        key_block = kv_ref[:, block, 0, :, :HD].reshape(keys, HD)
        value_block = kv_ref[:, block, 0, :, HD:].reshape(keys, HD)
        bounded = jnp.tanh(dot_nt(queries, key_block) * (HD ** (-0.5) / soft_cap))
        capped = jnp.where(
            visible_of(block, own, shard, rows, keys, lines), soft_cap * bounded, -1e30
        )
        weights = jnp.exp(capped - lse)
        grad_weights = dot_nt(grads, value_block)
        acc_ref[block, :, HD:] += dot_tn(weights.astype(bf16), grads)
        weight_ref[block] = weights * (1.0 - bounded * bounded)
        dp_ref[block] = grad_weights
        return delta + jnp.sum(weights * grad_weights, axis=-1, keepdims=True)

    delta = lax.fori_loop(0, own + 1, first_step, jnp.zeros((lines, 1), f32))

    def second_step(block, grad_query):
        key_block = kv_ref[:, block, 0, :, :HD].reshape(keys, HD)
        grad_raw = (weight_ref[block] * (dp_ref[block] - delta)).astype(bf16)
        acc_ref[block, :, :HD] += dot_tn(grad_raw, queries)
        return grad_query + dot_nn(grad_raw, key_block)

    grad_query = lax.fori_loop(
        0, own + 1, second_step, jnp.zeros((lines, HD), f32)
    ) * HD ** (-0.5)
    for h in range(lines // rows):
        dq_ref[0, 0, :, h * HD : (h + 1) * HD] = grad_query[h * rows : (h + 1) * rows].astype(bf16)

    @pl.when(own == blocks - 1)
    def _():
        for block in range(blocks):
            dkv_ref[:, block, 0, :, :HD] = (
                (acc_ref[block, :, :HD] * HD ** (-0.5)).astype(bf16).reshape(parts, rows, HD)
            )
            dkv_ref[:, block, 0, :, HD:] = (
                acc_ref[block, :, HD:].astype(bf16).reshape(parts, rows, HD)
            )


def attend(shard, queries, kv_all):
    blocks, seqs, rows, width = queries.shape
    lines = rows * width // HD
    parts = kv_all.shape[0]
    keys = parts * rows
    row_spec = pl.BlockSpec((1, 1, rows, width), lambda n, s, shard: (s, n, 0, 0))
    lse_spec = pl.BlockSpec((1, 1, lines, 128), lambda n, s, shard: (s, n, 0, 0))
    kv_spec = pl.BlockSpec((parts, blocks, 1, rows, 2 * HD), lambda n, s, shard: (0, 0, n, 0, 0))
    return pl.pallas_call(
        attend_kernel,
        grid_spec=pltpu.PrefetchScalarGridSpec(
            num_scalar_prefetch=1,
            grid=(seqs, blocks),
            in_specs=[row_spec, kv_spec],
            out_specs=[row_spec, lse_spec],
            scratch_shapes=[pltpu.VMEM((blocks, lines, keys), f32)],
        ),
        out_shape=[
            jax.ShapeDtypeStruct(queries.shape, bf16),
            jax.ShapeDtypeStruct((blocks, seqs, lines, 128), f32),
        ],
        compiler_params=pltpu.CompilerParams(vmem_limit_bytes=48 * 2**20),
        name="attend",
    )(shard, queries, kv_all)


def attend_back(shard, queries, grads, lse, kv_all):
    blocks, seqs, rows, width = queries.shape
    lines = rows * width // HD
    parts = kv_all.shape[0]
    keys = parts * rows
    row_spec = pl.BlockSpec((1, 1, rows, width), lambda n, s, shard: (s, n, 0, 0))
    lse_spec = pl.BlockSpec((1, 1, lines, 128), lambda n, s, shard: (s, n, 0, 0))
    deep = 2 if keys * blocks <= 4096 else 1
    kv_spec = pl.BlockSpec(
        (parts, blocks, 1, rows, 2 * HD),
        lambda n, s, shard: (0, 0, n, 0, 0),
        pipeline_mode=pl.Buffered(deep),
    )
    return pl.pallas_call(
        attend_back_kernel,
        grid_spec=pltpu.PrefetchScalarGridSpec(
            num_scalar_prefetch=1,
            grid=(seqs, blocks),
            in_specs=[row_spec, row_spec, lse_spec, kv_spec],
            out_specs=[row_spec, kv_spec],
            scratch_shapes=[
                pltpu.VMEM((blocks, lines, keys), f32),
                pltpu.VMEM((blocks, lines, keys), f32),
                pltpu.VMEM((blocks, keys, 2 * HD), f32),
            ],
        ),
        out_shape=[
            jax.ShapeDtypeStruct(queries.shape, bf16),
            jax.ShapeDtypeStruct(kv_all.shape, bf16),
        ],
        compiler_params=pltpu.CompilerParams(vmem_limit_bytes=56 * 2**20),
        name="attend_back",
    )(shard, queries, grads, lse, kv_all)


def widen_kernel(*refs):
    refs[-1][0] = refs[0][...].astype(f32)


def widen_plane(plane, index, planes, whole):
    rows, width = plane.shape
    step = rows // 4 if rows % 64 == 0 else rows
    specs = [pl.BlockSpec((step, width), lambda i: (i, 0))]
    args = [plane]
    aliases = {}
    if whole is not None:
        specs.append(pl.BlockSpec(memory_space=pl.ANY))
        args.append(whole)
        aliases = {1: 0}
    return pl.pallas_call(
        widen_kernel,
        grid=(rows // step,),
        in_specs=specs,
        out_specs=pl.BlockSpec((1, step, width), lambda i: (index, i, 0)),
        out_shape=jax.ShapeDtypeStruct((planes, rows, width), f32),
        input_output_aliases=aliases,
        compiler_params=pltpu.CompilerParams(vmem_limit_bytes=40 * 2**20),
        name="widen",
    )(*args)


def granules_of(column, columns):
    per = HQ // columns
    first = column * per
    return (
        [first + i for i in range(per)]
        + [HQ + first // GROUP, HQ + KVH + first // GROUP]
        + [HQ + 2 * KVH + first + i for i in range(per)]
    )


def route(columns, chips, per_chip):
    items = len(granules_of(0, columns))
    urgent = items - HQ // columns
    rank = [1] * (urgent - 2) + [0] * 2 + [2] * (items - urgent)
    source = [[g // per_chip for g in granules_of(c, columns)] for c in range(columns)]
    held = [[{k for k in range(items) if source[c][k] == z} for z in range(chips)] for c in range(columns)]
    steps = []
    urgent_steps = kv_steps = None
    while any(len(held[c][z]) < items for c in range(columns) for z in range(chips)):
        moves = {}
        for c in range(columns):
            for z in range(chips):
                for core, way in ((0, 1), (1, -1)):
                    if not 0 <= z + way < chips:
                        continue
                    ready = [
                        k
                        for k in held[c][z]
                        if k not in held[c][z + way] and (source[c][k] - z) * way <= 0
                    ]
                    if ready:
                        moves[c, z, core] = min(
                            ready, key=lambda k: (rank[k], abs(source[c][k] - z), k)
                        )
        for (c, z, core), k in moves.items():
            held[c][z + (1, -1)[core]].add(k)
        steps.append(moves)
        done = all(k in held[c][z] for c in range(columns) for z in range(chips) for k in range(urgent))
        if done and urgent_steps is None:
            urgent_steps = len(steps)
        done = all(
            k in held[c][z]
            for c in range(columns)
            for z in range(chips)
            for k in (urgent - 2, urgent - 1)
        )
        if done and kv_steps is None:
            kv_steps = len(steps)
    return steps, urgent_steps, kv_steps


def chosen(places, devices):
    names = []
    which = np.zeros((devices, len(places)), np.int32)
    slot = np.zeros((devices, len(places)), np.int32)
    for k, place in enumerate(places):
        for d in range(devices):
            name, at = place.get(d, ("mine", 0))
            if name not in names:
                names.append(name)
            which[d, k] = names.index(name)
            slot[d, k] = at
    return names, which, slot


def fetch(cands, which_ref, slot_ref, sources, place, buffer, sem):
    for code in cands[place]:

        @pl.when(which_ref[place] == code)
        def _(code=code):
            pltpu.make_async_copy(sources[code].at[slot_ref[place]], buffer, sem).start()


def pick_kernel(cands, which_ref, slot_ref, *refs):
    out_ref, buffers, in_sems, out_sems = refs[-4:]
    count, deep = len(cands), buffers.shape[0]

    def begin(k):
        at = k % deep
        fetch(cands, which_ref, slot_ref, refs, k, buffers.at[at], in_sems.at[at])

    def leaving(k):
        at = k % deep
        return pltpu.make_async_copy(buffers.at[at], out_ref.at[k], out_sems.at[at])

    for k in range(min(deep, count)):
        begin(k)
    for k in range(count):
        at = k % deep
        pltpu.make_async_copy(buffers.at[at], buffers.at[at], in_sems.at[at]).wait()
        leaving(k).start()
        again = k - deep // 2
        if again >= 0 and again + deep < count:
            leaving(again).wait()
            begin(again + deep)
    for k in range(max(0, count - deep), count):
        leaving(k).wait()


def project_kernel(cands, which_ref, slot_ref, rows_ref, *refs):
    out_ref, buffers, sems = refs[-3:]
    rows = buffers.shape[1]
    for k in range(len(cands)):
        fetch(cands, which_ref, slot_ref, refs, k, buffers.at[k], sems.at[k])
    for k in range(len(cands)):
        pltpu.make_async_copy(buffers.at[k], buffers.at[k], sems.at[k]).wait()
        out_ref[:, k * rows : (k + 1) * rows] = dot_nt(rows_ref[...], buffers[k]).astype(bf16)


def apply_kernel(cands, which_ref, slot_ref, rows_ref, *refs):
    out_ref, buffers, sems = refs[-3:]
    _, rows, width = buffers.shape
    for k in range(len(cands)):
        fetch(cands, which_ref, slot_ref, refs, k, buffers.at[k], sems.at[k])
    for k in range(len(cands)):
        pltpu.make_async_copy(buffers.at[k], buffers.at[k], sems.at[k]).wait()
    step = width // 3 if width % 384 == 0 else width
    for low in range(0, width, step):
        total = dot_nn(rows_ref[:, :rows], buffers[0, :, low : low + step])
        for k in range(1, len(cands)):
            total += dot_nn(
                rows_ref[:, k * rows : (k + 1) * rows], buffers[k, :, low : low + step]
            )
        out_ref[:, low : low + step] = total.astype(bf16)


def pick(places, sources, device, devices, kind="pick", rows_in=None):
    names, which, slot = chosen(places, devices)
    _, rows, width = sources["mine"].shape
    table = jnp.asarray(np.concatenate([which, slot], axis=1))[device]
    count = len(places)
    cands = [sorted(set(which[:, k].tolist())) for k in range(count)]
    kernel = {"pick": pick_kernel, "project": project_kernel, "apply": apply_kernel}[kind]
    args = [sources[name] for name in names]
    in_specs = [pl.BlockSpec(memory_space=pl.ANY)] * len(names)
    if kind == "pick":
        deep = min(count, 8)
        out_spec = pl.BlockSpec(memory_space=pl.ANY)
        out_shape = (count, rows, width)
        sems = [pltpu.SemaphoreType.DMA((deep,)), pltpu.SemaphoreType.DMA((deep,))]
    else:
        deep = count
        args = [rows_in] + args
        in_specs = [pl.BlockSpec(memory_space=pltpu.VMEM)] + in_specs
        out_spec = pl.BlockSpec(memory_space=pltpu.VMEM)
        out_shape = (rows_in.shape[0], count * rows if kind == "project" else width)
        sems = [pltpu.SemaphoreType.DMA((deep,))]
    return pl.pallas_call(
        functools.partial(kernel, cands),
        grid_spec=pltpu.PrefetchScalarGridSpec(
            num_scalar_prefetch=2,
            grid=(1,),
            in_specs=in_specs,
            out_specs=out_spec,
            scratch_shapes=[pltpu.VMEM((deep, rows, width), bf16)] + sems,
        ),
        out_shape=jax.ShapeDtypeStruct(out_shape, bf16),
        compiler_params=pltpu.CompilerParams(vmem_limit_bytes=58 * 2**20),
        name=kind,
    )(table[:count], table[count:], *args)


def routed_weights(attn_weight, column, shard, columns, shards, between):
    rows, width = attn_weight.shape
    count = rows // HD
    chips = shards // 2
    devices = columns * shards
    device = column * shards + shard
    swap = [(f, f ^ 1) for f in range(shards)]
    items = len(granules_of(0, columns))
    urgent = items - HQ // columns
    steps, urgent_steps, kv_steps = route(columns, chips, 2 * count)
    mine = attn_weight.reshape(count, HD, width)
    theirs = between("start", lax.ppermute(mine, "fsdp", swap))
    sources = {"mine": mine, "theirs": theirs}
    at = [{} for _ in range(items)]
    for c in range(columns):
        for f in range(shards):
            for k, g in enumerate(granules_of(c, columns)):
                if g // (2 * count) == f // 2:
                    at[k][c * shards + f] = ("mine" if g // count == f else "theirs", g % count)
    sends = []
    for number, moves in enumerate(steps):
        own, passed, pairs = {}, {}, []
        for (c, z, core), k in moves.items():
            here = c * shards + 2 * z + core
            to = here + (2, -2)[core]
            name, slot = at[k][here]
            if name in ("mine", "theirs"):
                own[here] = (name, slot)
            else:
                passed[here] = name
            pairs.append((here, to))
            at[k][to] = ("got%d" % number, 0)
            at[k][to ^ 1] = ("swapped%d" % number, 0)
        sends.append((own, passed, pairs))
    with_own = [n for n in range(1, len(sends)) if sends[n][0]]
    own_first = pick([sends[0][0]], sources, device, devices)
    own_later = None
    for number, (own, passed, pairs) in enumerate(sends):
        if number == 0:
            piece = own_first
        else:
            names = sorted(set(passed.values()))
            code = np.zeros((devices,), np.int32)
            for d, name in passed.items():
                code[d] = 1 + names.index(name)
            here = jnp.asarray(code)[device]
            piece = sources[names[-1]]
            for i, name in enumerate(names[:-1]):
                piece = jnp.where(here == 1 + i, sources[name], piece)
            if number in with_own:
                place = with_own.index(number)
                piece = jnp.where(here == 0, own_later[place : place + 1], piece)
        got = lax.ppermute(piece, ("seq", "fsdp"), pairs)
        if number == 0:
            own_later = pick([sends[n][0] for n in with_own], sources, device, devices)
            got, own_later = lax.optimization_barrier((got, own_later))
        if number < urgent_steps:
            got = between(number, got)
        if 0 < number < urgent_steps:
            before = "swapped%d" % (number - 1)
            got, sources[before] = lax.optimization_barrier((got, sources[before]))
        sources["got%d" % number] = got
        if number < urgent_steps:
            sources["swapped%d" % number] = lax.ppermute(got, "fsdp", swap)
        for name, wanted, count_of in (
            ("kv", (urgent - 2, urgent), kv_steps),
            ("q", (0, urgent - 2), urgent_steps),
        ):
            if number + 1 == count_of:
                ready = dict(sources)
                places = [dict(place) for place in at[slice(*wanted)]]
                between(
                    name,
                    lambda times, ready=ready, places=places: pick(
                        places, ready, device, devices, "project", times
                    ),
                )

    def first(after):
        held, after = lax.optimization_barrier((ready, after))
        return pick(at[:urgent], held, device, devices)

    held = None

    def times_rest(rows_in):
        nonlocal held
        held, rows_in = lax.optimization_barrier((sources, rows_in))
        for number in range(urgent_steps, len(steps)):
            held["swapped%d" % number] = lax.ppermute(held["got%d" % number], "fsdp", swap)
        return pick(at[urgent:], held, device, devices, "apply", rows_in)

    def others(after):
        kept, after = lax.optimization_barrier((held, after))
        return pick(at[urgent:], kept, device, devices)

    return first, times_rest, others


def column_weights(attn_weight, column, shard, columns, shards, between):
    rows, width = attn_weight.shape
    per = HQ // columns
    if rows % HD == 0 and shards == 8 and columns == 4:
        return routed_weights(attn_weight, column, shard, columns, shards, between)
    whole = lax.all_gather(attn_weight, "fsdp", axis=0, tiled=True).reshape(-1, HD, width)
    table = np.array([granules_of(c, columns) for c in range(columns)], np.int32)
    place = jnp.asarray(table)[column]
    taken = jnp.concatenate(
        [lax.dynamic_slice_in_dim(whole, place[k], 1, 0) for k in range(table.shape[1])], axis=0
    )
    for name, low, high in (("kv", per, per + 2), ("q", 0, per)):
        between(
            name,
            lambda times, low=low, high=high: dot_nt(
                times, taken[low:high].reshape(-1, width)
            ).astype(bf16),
        )
    return (
        lambda after: taken[: per + 2],
        lambda rows_in: dot_nn(rows_in, taken[per + 2 :].reshape(-1, width)).astype(bf16),
        lambda after: taken[per + 2 :],
    )


def ring_of(chips):
    return [0] + list(range(1, chips, 2)) + [z for z in range(chips - 1, 0, -1) if z % 2 == 0]


def ring_tables(shards):
    chips = shards // 2
    order = ring_of(chips)
    spot = {z: p for p, z in enumerate(order)}
    pairs = [
        (2 * z + c, 2 * order[(spot[z] + 1) % chips] + c) for z in range(chips) for c in range(2)
    ]
    behind = np.array(
        [[order[(spot[f // 2] - t) % chips] for t in range(chips + 1)] for f in range(shards)],
        np.int32,
    )
    return chips, pairs, behind


def ring_pieces(block, shard, shards, beside):
    chips, pairs, behind = ring_tables(shards)
    swap = [(f, f ^ 1) for f in range(shards)]
    source = jnp.asarray(behind)[shard]
    core = shard % 2
    pieces = []
    held = block
    for t in range(chips):
        if t:
            held = lax.ppermute(held, "fsdp", pairs)
            held = beside(t, held)
        pieces.append((held, 2 * source[t] + core))
        pieces.append((lax.ppermute(held, "fsdp", swap), 2 * source[t] + 1 - core))
    return pieces


def direct_pieces(block, shard, shards):
    chips = shards // 2
    swap = [(f, f ^ 1) for f in range(shards)]
    core = shard % 2
    come = [block] + [
        lax.ppermute(block, "fsdp", [(f, (f + 2 * hop) % shards) for f in range(shards)])
        for hop in range(1, chips)
    ]

    def finish(after):
        held, after = lax.optimization_barrier((come, after))
        pieces = []
        for hop, piece in enumerate(held):
            chip = (shard // 2 - hop) % chips
            pieces.append((piece, 2 * chip + core))
            pieces.append((lax.ppermute(piece, "fsdp", swap), 2 * chip + 1 - core))
        return pieces, after

    return finish


def weight_grad_kernel(half, place_ref, cols_ref, *refs):
    pieces = refs[: 2 * half]
    out_ref, rows_ref, turned_ref, sems = refs[2 * half :]
    lines = pieces[0].shape[0]
    for i, piece in enumerate(pieces):
        start = pl.multiple_of(place_ref[i] * lines, lines)
        pltpu.make_async_copy(
            piece, rows_ref.at[i // half, pl.ds(start, lines)], sems.at[i]
        ).start()
    limit = place_ref[2 * half]
    turned = cols_ref[...].T
    col = lax.broadcasted_iota(jnp.int32, turned.shape, 0)
    turned_ref[0] = jnp.where(col < limit, turned, 0)
    turned_ref[1] = jnp.where(col < limit, 0, turned)
    for i, piece in enumerate(pieces):
        pltpu.make_async_copy(piece, rows_ref.at[0, pl.ds(0, lines)], sems.at[i]).wait()
    width = out_ref.shape[1]
    step = width // 3 if width % 384 == 0 else width

    def chunk(n, carry):
        cut = pl.ds(pl.multiple_of(n * step, step), step)
        total = dot_nn(turned_ref[0], rows_ref[0, :, cut])
        total += dot_nn(turned_ref[1], rows_ref[1, :, cut])
        out_ref[:, cut] = total.astype(bf16)
        return carry

    lax.fori_loop(0, width // step, chunk, 0)


def weight_grad(cols, limit, first, second):
    lines, width = first[0][0].shape
    half = len(first)
    place = jnp.stack(
        [where.astype(jnp.int32) for _, where in first + second] + [limit.astype(jnp.int32)]
    )
    return pl.pallas_call(
        functools.partial(weight_grad_kernel, half),
        grid_spec=pltpu.PrefetchScalarGridSpec(
            num_scalar_prefetch=1,
            grid=(1,),
            in_specs=[pl.BlockSpec(memory_space=pltpu.VMEM)]
            + [pl.BlockSpec(memory_space=pl.ANY)] * (2 * half),
            out_specs=pl.BlockSpec(memory_space=pltpu.VMEM),
            scratch_shapes=[
                pltpu.VMEM((2, half * lines, width), bf16),
                pltpu.VMEM((2, cols.shape[1], cols.shape[0]), bf16),
                pltpu.SemaphoreType.DMA((2 * half,)),
            ],
        ),
        out_shape=jax.ShapeDtypeStruct((cols.shape[1], width), bf16),
        compiler_params=pltpu.CompilerParams(vmem_limit_bytes=58 * 2**20),
        name="weight_grad",
    )(place, cols, *[piece for piece, _ in first + second])


def ring_scatter(parts, shard, shards):
    chips, pairs, behind = ring_tables(shards)
    swap = [(f, f ^ 1) for f in range(shards)]
    target = jnp.asarray(behind)[shard]
    core = shard % 2
    paired = parts.reshape((chips, 2) + parts.shape[1:])
    mine = lax.dynamic_index_in_dim(paired, core, 1, keepdims=False)
    other = lax.ppermute(
        lax.dynamic_index_in_dim(paired, 1 - core, 1, keepdims=False), "fsdp", swap
    )

    def local_sum(t):
        return lax.dynamic_index_in_dim(mine, target[t], 0, keepdims=False).astype(
            f32
        ) + lax.dynamic_index_in_dim(other, target[t], 0, keepdims=False).astype(f32)

    total = local_sum(1)
    for t in range(1, chips):
        total = lax.ppermute(total.astype(bf16), "fsdp", pairs).astype(f32) + local_sum(t + 1)
    return total


def partners(columns, bit):
    return [(c, c ^ bit) for c in range(columns)]


def column_scatter(parts):
    half = parts.shape[-1] // 2
    done = []
    for first, second, cut in ((1, 2, slice(0, half)), (2, 1, slice(half, None))):
        low = parts[..., cut]
        got = lax.ppermute(
            jnp.concatenate([low[first : first + 1], low[3:]], axis=0), "seq", partners(4, first)
        )
        keep = low[0].astype(f32) + got[0].astype(f32)
        away = low[second].astype(f32) + got[1].astype(f32)
        done.append(
            keep + lax.ppermute(away.astype(bf16), "seq", partners(4, second)).astype(f32)
        )
    return jnp.concatenate(done, axis=-1)


def sum_everywhere(value, columns, shards):
    for axis, count in (("fsdp", shards), ("seq", columns)):
        bit = 1
        while bit < count:
            value = value + lax.ppermute(value, axis, [(c, c ^ bit) for c in range(count)])
            bit *= 2
    return value


def local(tokens, attn_weight, norm_gains, ffn_weight, out_grad):
    seqs, rows, width = tokens.shape
    columns = lax.axis_size("seq")
    shards = lax.axis_size("fsdp")
    column = lax.axis_index("seq")
    shard = lax.axis_index("fsdp")
    core = shard % 2
    per = HQ // columns
    own_rows = seqs * rows
    swap = [(f, f ^ 1) for f in range(shards)]
    shard_arg = shard.astype(jnp.int32).reshape(1)

    def core_half(granules):
        return lax.dynamic_index_in_dim(
            granules.reshape(-1, 2, HALF, width), core, 1, keepdims=False
        )

    def round_start(granules):
        lanes = core_half(granules)
        cut = lanes.shape[0] // 2
        lanes = (lanes[:cut], lanes[cut:])
        near = tuple(
            lax.ppermute(lane, "seq", partners(4, bit)) for lane, bit in zip(lanes, (1, 2))
        )
        return lanes, near

    def round_on(lanes, near):
        return tuple(
            tuple(lax.ppermute(piece, "seq", partners(4, bit)) for piece in pieces)
            for pieces, bit in zip(zip(lanes, near), (2, 1))
        )

    def all_columns(granules, near, far):
        count = granules.shape[0]
        cut = count // 2
        come = {
            (0, 1): near[0],
            (0, 2): far[0][0],
            (0, 3): far[0][1],
            (1, 2): near[1],
            (1, 1): far[1][0],
            (1, 3): far[1][1],
        }
        sources = {"mine": granules.reshape(2 * count, HALF, width)}
        for (part, hop), lane in come.items():
            sources["own%d%d" % (part, hop)] = lane
            sources["other%d%d" % (part, hop)] = lax.ppermute(lane, "fsdp", swap)
        places = []
        for home in range(columns):
            for k in range(count):
                for half in range(2):
                    place = {}
                    for c in range(columns):
                        for f in range(shards):
                            part, hop = int(k >= cut), home ^ c
                            whose = "own" if f % 2 == half else "other"
                            place[c * shards + f] = (
                                ("%s%d%d" % (whose, part, hop), k - part * cut)
                                if hop
                                else ("mine", 2 * k + half)
                            )
                    places.append(place)
        device = column * shards + shard
        return pick(places, sources, device, columns * shards).reshape(-1, width)

    token_slices = lax.all_gather(tokens, "seq", axis=0)
    gain_rows = lax.all_gather(norm_gains, "fsdp", axis=1, tiled=True).astype(f32)
    normed_slices = rms_scale(
        token_slices.reshape(-1, width).astype(f32), gain_rows[0]
    ).astype(bf16)
    made = {}

    def between(step, value):
        nonlocal normed_slices, gain_rows
        if step == "start":
            value, gain_rows = lax.optimization_barrier((value, gain_rows))
            normed_slices = rms_scale(
                token_slices.reshape(-1, width).astype(f32), gain_rows[0]
            ).astype(bf16)
        if step == 1:
            value, normed_slices = lax.optimization_barrier((value, normed_slices))
        if step == 2:
            value, made["kv"] = lax.optimization_barrier((value, made["kv"]))
        if step in ("kv", "q"):
            made[step] = value(normed_slices)
        return value

    first_weights, times_out, out_weights = column_weights(
        attn_weight, column, shard, columns, shards, between
    )
    kv_all = lax.all_gather(made["kv"].reshape(columns, seqs, rows, 2 * HD), "fsdp", axis=0)
    queries = made["q"].reshape(columns, seqs, rows, per * HD)
    weight_in = first_weights(queries)
    if columns == 4:
        in_lanes, in_near = round_start(weight_in)
        kv_all, in_lanes = lax.optimization_barrier((kv_all, in_lanes))

    mixed, lse = attend(shard_arg, queries, kv_all)
    if columns == 4:
        by_partner = jnp.concatenate(
            [lax.dynamic_slice_in_dim(mixed, column ^ k, 1, 0) for k in range(columns)], axis=0
        ).reshape(columns * own_rows, per * HD)
        attn_out = column_scatter(times_out(by_partner).reshape(columns, own_rows, width))
    else:
        attn_out = lax.psum_scatter(
            times_out(mixed.reshape(-1, per * HD)),
            "seq",
            scatter_dimension=0,
            tiled=True,
        ).astype(f32)
    flat_tokens = tokens.reshape(-1, width).astype(f32)
    flat_cot = out_grad.reshape(-1, width).astype(f32)
    residual = flat_tokens + rms_scale(attn_out, gain_rows[1])
    normed_ffn = rms_scale(residual, gain_rows[2]).astype(bf16)

    mixed_later, normed_ffn = lax.optimization_barrier((mixed, normed_ffn))
    weight_out = out_weights(normed_ffn)
    ffn_in = lax.all_gather(normed_ffn, "fsdp", axis=0, tiled=True)
    mixed_rows = lax.all_to_all(mixed_later, "seq", split_axis=0, concat_axis=0, tiled=True)
    mixed_rows = mixed_rows.transpose(1, 2, 0, 3).reshape(own_rows, HQ * HD)
    if columns == 4:
        out_lanes, out_near = round_start(weight_out)
        ffn_in, out_near, in_near, mixed_rows = lax.optimization_barrier(
            (ffn_in, out_near, in_near, mixed_rows)
        )
        in_far = round_on(in_lanes, in_near)
    gate_up = jnp.einsum("td,fgd->tgf", ffn_in, ffn_weight[:, :2], preferred_element_type=f32)
    hidden = gated_units(gate_up[:, 0], gate_up[:, 1]).astype(bf16)
    branch = dot_nn(hidden, ffn_weight[:, 2]).astype(bf16)
    ffn_out = lax.psum_scatter(branch, "fsdp", scatter_dimension=0, tiled=True).astype(f32)
    if columns == 4:
        ffn_out, in_far = lax.optimization_barrier((ffn_out, in_far))
        out_far = round_on(out_lanes, out_near)
        weight_in_all = all_columns(weight_in, in_near, in_far)
    else:
        weight_in_all = lax.all_gather(weight_in, "seq", axis=0).reshape(-1, width)
        weight_out_all = lax.all_gather(weight_out, "seq", axis=0).reshape(-1, width)
    result = residual + rms_scale(ffn_out, gain_rows[3])
    block_out = result.astype(bf16).reshape(tokens.shape)
    grad_ffn, gain_terms = norm_back(ffn_out, gain_rows[3], flat_cot)
    gain_last = jnp.sum(gain_terms, axis=0)
    grad_ffn_all = lax.all_gather(grad_ffn.astype(bf16), "fsdp", axis=0, tiled=True)
    if columns == 4:
        weight_out_all = all_columns(weight_out, out_near, out_far)
        grad_ffn_all, weight_out_all, weight_in_all = lax.optimization_barrier(
            (grad_ffn_all, weight_out_all, weight_in_all)
        )

    normed_own = rms_scale(flat_tokens, gain_rows[0]).astype(bf16)
    grad_ffn_all, normed_own = lax.optimization_barrier((grad_ffn_all, normed_own))
    kept = {}

    def beside(step, held):
        if step == 1:
            part = dot_tn(hidden, grad_ffn_all).astype(bf16)
            held, kept["down"], kept["all"] = lax.optimization_barrier((held, part, grad_ffn_all))
        if step == 2:
            grad_hidden = dot_nt(kept["all"], ffn_weight[:, 2])
            unused, gated_pull = jax.vjp(gated_units, gate_up[:, 0], gate_up[:, 1])
            grad_gate, grad_up = gated_pull(grad_hidden)
            part = jnp.stack([grad_gate, grad_up], axis=1).astype(bf16)
            held, kept["units"] = lax.optimization_barrier((held, part))
        if step == 3:
            parts = (
                dot_tn(kept["units"][:, 0], ffn_in).astype(bf16),
                dot_tn(kept["units"][:, 1], ffn_in).astype(bf16),
            )
            held, kept["up"], kept["units"] = lax.optimization_barrier(
                (held, parts, kept["units"])
            )
        return held

    normed_pieces = ring_pieces(normed_own, shard, shards, beside)
    grad_gate_up = kept["units"]
    gate_grad, up_grad, down_grad = lax.psum((*kept["up"], kept["down"]), "seq")

    def attention_back():
        grad_in = jnp.einsum(
            "tgf,fgd->td", grad_gate_up, ffn_weight[:, :2], preferred_element_type=f32
        )
        grad_normed_ffn = ring_scatter(
            grad_in.astype(bf16).reshape(shards, own_rows, width), shard, shards
        )
        grad_mid, gain_pre_ffn = norm_back(residual, gain_rows[2], grad_normed_ffn)
        grad_residual = flat_cot + grad_mid
        grad_attn, gain_post_attn = norm_back(attn_out, gain_rows[1], grad_residual)
        grad_attn_low = grad_attn.astype(bf16)
        grad_mixed = (
            dot_nt(grad_attn_low, weight_out_all)
            .astype(bf16)
            .reshape(seqs, rows, columns, per * HD)
        )
        grad_heads = lax.all_to_all(
            grad_mixed.transpose(2, 0, 1, 3), "seq", split_axis=0, concat_axis=0, tiled=True
        )
        later_pieces = direct_pieces(grad_attn_low, shard, shards)
        grad_queries, grad_kv = attend_back(shard_arg, queries, grad_heads, lse, kv_all)
        grad_kv_own = (
            ring_scatter(grad_kv.reshape(shards, columns * own_rows, 2 * HD), shard, shards)
            .astype(bf16)
            .reshape(columns, seqs, rows, 2 * HD)
        )
        grad_proj = lax.all_to_all(
            jnp.concatenate([grad_queries, grad_kv_own], axis=-1),
            "seq",
            split_axis=0,
            concat_axis=0,
            tiled=True,
        )
        attn_pieces, grad_proj = later_pieces(grad_proj)
        grad_rows = grad_proj.reshape(columns, own_rows, (per + 2) * HD).transpose(1, 0, 2)
        grad_normed = dot_nn(grad_rows.reshape(own_rows, -1), weight_in_all)
        grad_tokens, gain_pre_attn = norm_back(flat_tokens, gain_rows[0], grad_normed)
        token_grad = (grad_residual + grad_tokens).reshape(tokens.shape)

        def shared(copies):
            if columns == KVH:
                return copies.reshape(own_rows, -1)
            summed = copies.reshape(own_rows, KVH, columns // KVH, HD).astype(f32).sum(axis=2)
            return summed.astype(bf16).reshape(own_rows, -1)

        weight_cols = jnp.concatenate(
            [
                grad_rows[:, :, : per * HD].reshape(own_rows, -1),
                shared(grad_rows[:, :, per * HD : (per + 1) * HD]),
                shared(grad_rows[:, :, (per + 1) * HD :]),
                mixed_rows,
            ],
            axis=1,
        )
        shard_cols = attn_weight.shape[0]
        col_all = lax.all_to_all(
            weight_cols.reshape(own_rows, shards, shard_cols).transpose(1, 0, 2),
            "fsdp",
            split_axis=0,
            concat_axis=0,
            tiled=True,
        ).reshape(-1, shard_cols)
        limit = jnp.clip((HQ + 2 * KVH) * HD - shard * shard_cols, 0, shard_cols)
        attn_grad = weight_grad(col_all, limit, normed_pieces, attn_pieces)
        gain_grad = jnp.stack(
            [
                jnp.sum(gain_pre_attn, axis=0),
                jnp.sum(gain_post_attn, axis=0),
                jnp.sum(gain_pre_ffn, axis=0),
                gain_last,
            ]
        )
        return attn_grad, gain_grad, token_grad

    def nothing():
        return (
            jnp.zeros(attn_weight.shape, bf16),
            jnp.zeros((4, width), f32),
            jnp.zeros(tokens.shape, f32),
        )

    attn_grad, gain_grad, token_grad = lax.cond(
        shard < 2**20, attention_back, nothing
    )
    attn_grad, gate_grad, up_grad, down_grad = lax.optimization_barrier(
        (attn_grad, gate_grad, up_grad, down_grad)
    )
    attn_total = lax.psum(attn_grad, "seq").astype(f32)
    ffn_grad = widen_plane(down_grad, 2, 3, None)
    ffn_grad = widen_plane(gate_grad, 0, 3, ffn_grad)
    ffn_grad = widen_plane(up_grad, 1, 3, ffn_grad)
    ffn_grad = ffn_grad.transpose(1, 0, 2)
    gain_total = lax.dynamic_slice_in_dim(
        sum_everywhere(gain_grad, columns, shards),
        shard * norm_gains.shape[1],
        norm_gains.shape[1],
        1,
    )
    return (block_out, token_grad, attn_total, gain_total, ffn_grad)


def solution(mesh):
    in_specs = (
        P(None, ("seq", "fsdp"), None),
        P("fsdp", None),
        P(None, "fsdp"),
        P("fsdp", None, None),
        P(None, ("seq", "fsdp"), None),
    )
    out_specs = (
        P(None, ("seq", "fsdp"), None),
        P(None, ("seq", "fsdp"), None),
        P("fsdp", None),
        P(None, "fsdp"),
        P("fsdp", None, None),
    )
    return jax.shard_map(local, mesh=mesh, in_specs=in_specs, out_specs=out_specs, check_vma=False)
```

```python
import functools

import jax
import jax.numpy as jnp
import numpy as np
from jax import lax
from jax.experimental import pallas as pl
from jax.experimental.pallas import tpu as pltpu
from jax.sharding import PartitionSpec as P

HQ = 8
KVH = 4
HD = 256
GROUP = HQ // KVH
HALF = HD // 2

soft_cap = 50.0
norm_eps = 1e-06
bf16 = jnp.bfloat16
f32 = jnp.float32


def rms_scale(values, gain_row):
    return (
        values * lax.rsqrt(jnp.mean(values * values, axis=-1, keepdims=True) + norm_eps) * gain_row
    )


def norm_back(values, gain_row, cotangent):
    inverse = lax.rsqrt(jnp.mean(values * values, axis=-1, keepdims=True) + norm_eps)
    unit_rows = values * inverse
    scaled = cotangent * gain_row
    grad_values = inverse * (
        scaled - unit_rows * jnp.mean(scaled * unit_rows, axis=-1, keepdims=True)
    )
    return (grad_values, cotangent * unit_rows)


def gated_units(gate_proj, up_proj):
    return jax.nn.gelu(gate_proj, approximate=True) * up_proj


def dot_nt(a, b):
    return lax.dot_general(a, b, (((1,), (1,)), ((), ())), preferred_element_type=f32)


def dot_nn(a, b):
    return lax.dot_general(a, b, (((1,), (0,)), ((), ())), preferred_element_type=f32)


def dot_tn(a, b):
    return lax.dot_general(a, b, (((0,), (0,)), ((), ())), preferred_element_type=f32)


def stacked_heads(block):
    heads = block.shape[1] // HD
    return jnp.concatenate([block[:, h * HD : (h + 1) * HD] for h in range(heads)], axis=0)


def visible_of(block, own, shard, rows, keys, lines):
    shape = (lines, keys)
    row = lax.broadcasted_iota(jnp.int32, shape, 0) & (rows - 1)
    col = lax.broadcasted_iota(jnp.int32, shape, 1)
    return block * keys + col <= own * keys + shard * rows + row


def attend_kernel(shard_ref, q_ref, kv_ref, o_ref, lse_ref, score_ref):
    own = pl.program_id(1)
    shard = shard_ref[0]
    parts, _, _, rows, _ = kv_ref.shape
    keys = parts * rows
    queries = stacked_heads(q_ref[0, 0])
    lines = queries.shape[0]

    def score_step(block, top):
        key_block = kv_ref[:, block, 0, :, :HD].reshape(keys, HD)
        raw = dot_nt(queries, key_block) * HD ** (-0.5)
        capped = soft_cap * jnp.tanh(raw / soft_cap)
        capped = jnp.where(visible_of(block, own, shard, rows, keys, lines), capped, -1e30)
        score_ref[block] = capped
        return jnp.maximum(top, jnp.max(capped, axis=-1, keepdims=True))

    top = lax.fori_loop(0, own + 1, score_step, jnp.full((lines, 1), -3e38, f32))

    def sum_step(block, total):
        expanded = jnp.exp(score_ref[block] - top)
        score_ref[block] = expanded
        return total + jnp.sum(expanded, axis=-1, keepdims=True)

    total = lax.fori_loop(0, own + 1, sum_step, jnp.zeros((lines, 1), f32))
    inverse = 1.0 / total

    def mix_step(block, mixed):
        weights = (score_ref[block] * inverse).astype(bf16)
        value_block = kv_ref[:, block, 0, :, HD:].reshape(keys, HD)
        return mixed + dot_nn(weights, value_block)

    mixed = lax.fori_loop(0, own + 1, mix_step, jnp.zeros((lines, HD), f32))
    for h in range(lines // rows):
        o_ref[0, 0, :, h * HD : (h + 1) * HD] = mixed[h * rows : (h + 1) * rows].astype(bf16)
    lse_ref[0, 0] = jnp.broadcast_to(top + jnp.log(total), (lines, 128))


def attend_back_kernel(
    shard_ref, q_ref, do_ref, lse_ref, kv_ref, dq_ref, dkv_ref, weight_ref, dp_ref, acc_ref
):
    own = pl.program_id(1)
    shard = shard_ref[0]
    parts, blocks, _, rows, _ = kv_ref.shape
    keys = parts * rows
    queries = stacked_heads(q_ref[0, 0])
    grads = stacked_heads(do_ref[0, 0])
    lse = lse_ref[0, 0][:, :1]
    lines = queries.shape[0]

    @pl.when(own == 0)
    def _():
        acc_ref[...] = jnp.zeros_like(acc_ref)

    def first_step(block, delta):
        key_block = kv_ref[:, block, 0, :, :HD].reshape(keys, HD)
        value_block = kv_ref[:, block, 0, :, HD:].reshape(keys, HD)
        bounded = jnp.tanh(dot_nt(queries, key_block) * (HD ** (-0.5) / soft_cap))
        capped = jnp.where(
            visible_of(block, own, shard, rows, keys, lines), soft_cap * bounded, -1e30
        )
        weights = jnp.exp(capped - lse)
        grad_weights = dot_nt(grads, value_block)
        acc_ref[block, :, HD:] += dot_tn(weights.astype(bf16), grads)
        weight_ref[block] = weights * (1.0 - bounded * bounded)
        dp_ref[block] = grad_weights
        return delta + jnp.sum(weights * grad_weights, axis=-1, keepdims=True)

    delta = lax.fori_loop(0, own + 1, first_step, jnp.zeros((lines, 1), f32))

    def second_step(block, grad_query):
        key_block = kv_ref[:, block, 0, :, :HD].reshape(keys, HD)
        grad_raw = (weight_ref[block] * (dp_ref[block] - delta)).astype(bf16)
        acc_ref[block, :, :HD] += dot_tn(grad_raw, queries)
        return grad_query + dot_nn(grad_raw, key_block)

    grad_query = lax.fori_loop(
        0, own + 1, second_step, jnp.zeros((lines, HD), f32)
    ) * HD ** (-0.5)
    for h in range(lines // rows):
        dq_ref[0, 0, :, h * HD : (h + 1) * HD] = grad_query[h * rows : (h + 1) * rows].astype(bf16)

    @pl.when(own == blocks - 1)
    def _():
        for block in range(blocks):
            dkv_ref[:, block, 0, :, :HD] = (
                (acc_ref[block, :, :HD] * HD ** (-0.5)).astype(bf16).reshape(parts, rows, HD)
            )
            dkv_ref[:, block, 0, :, HD:] = (
                acc_ref[block, :, HD:].astype(bf16).reshape(parts, rows, HD)
            )


def attend(shard, queries, kv_all):
    blocks, seqs, rows, width = queries.shape
    lines = rows * width // HD
    parts = kv_all.shape[0]
    keys = parts * rows
    row_spec = pl.BlockSpec((1, 1, rows, width), lambda n, s, shard: (s, n, 0, 0))
    lse_spec = pl.BlockSpec((1, 1, lines, 128), lambda n, s, shard: (s, n, 0, 0))
    kv_spec = pl.BlockSpec((parts, blocks, 1, rows, 2 * HD), lambda n, s, shard: (0, 0, n, 0, 0))
    return pl.pallas_call(
        attend_kernel,
        grid_spec=pltpu.PrefetchScalarGridSpec(
            num_scalar_prefetch=1,
            grid=(seqs, blocks),
            in_specs=[row_spec, kv_spec],
            out_specs=[row_spec, lse_spec],
            scratch_shapes=[pltpu.VMEM((blocks, lines, keys), f32)],
        ),
        out_shape=[
            jax.ShapeDtypeStruct(queries.shape, bf16),
            jax.ShapeDtypeStruct((blocks, seqs, lines, 128), f32),
        ],
        compiler_params=pltpu.CompilerParams(vmem_limit_bytes=48 * 2**20),
        name="attend",
    )(shard, queries, kv_all)


def attend_back(shard, queries, grads, lse, kv_all):
    blocks, seqs, rows, width = queries.shape
    lines = rows * width // HD
    parts = kv_all.shape[0]
    keys = parts * rows
    row_spec = pl.BlockSpec((1, 1, rows, width), lambda n, s, shard: (s, n, 0, 0))
    lse_spec = pl.BlockSpec((1, 1, lines, 128), lambda n, s, shard: (s, n, 0, 0))
    deep = 2 if keys * blocks <= 4096 else 1
    kv_spec = pl.BlockSpec(
        (parts, blocks, 1, rows, 2 * HD),
        lambda n, s, shard: (0, 0, n, 0, 0),
        pipeline_mode=pl.Buffered(deep),
    )
    return pl.pallas_call(
        attend_back_kernel,
        grid_spec=pltpu.PrefetchScalarGridSpec(
            num_scalar_prefetch=1,
            grid=(seqs, blocks),
            in_specs=[row_spec, row_spec, lse_spec, kv_spec],
            out_specs=[row_spec, kv_spec],
            scratch_shapes=[
                pltpu.VMEM((blocks, lines, keys), f32),
                pltpu.VMEM((blocks, lines, keys), f32),
                pltpu.VMEM((blocks, keys, 2 * HD), f32),
            ],
        ),
        out_shape=[
            jax.ShapeDtypeStruct(queries.shape, bf16),
            jax.ShapeDtypeStruct(kv_all.shape, bf16),
        ],
        compiler_params=pltpu.CompilerParams(vmem_limit_bytes=56 * 2**20),
        name="attend_back",
    )(shard, queries, grads, lse, kv_all)


def widen_kernel(*refs):
    refs[-1][0] = refs[0][...].astype(f32)


def widen_plane(plane, index, planes, whole):
    rows, width = plane.shape
    step = rows // 4 if rows % 64 == 0 else rows
    specs = [pl.BlockSpec((step, width), lambda i: (i, 0))]
    args = [plane]
    aliases = {}
    if whole is not None:
        specs.append(pl.BlockSpec(memory_space=pl.ANY))
        args.append(whole)
        aliases = {1: 0}
    return pl.pallas_call(
        widen_kernel,
        grid=(rows // step,),
        in_specs=specs,
        out_specs=pl.BlockSpec((1, step, width), lambda i: (index, i, 0)),
        out_shape=jax.ShapeDtypeStruct((planes, rows, width), f32),
        input_output_aliases=aliases,
        compiler_params=pltpu.CompilerParams(vmem_limit_bytes=40 * 2**20),
        name="widen",
    )(*args)


def granules_of(column, columns):
    per = HQ // columns
    first = column * per
    return (
        [first + i for i in range(per)]
        + [HQ + first // GROUP, HQ + KVH + first // GROUP]
        + [HQ + 2 * KVH + first + i for i in range(per)]
    )


def route(columns, chips, per_chip):
    items = len(granules_of(0, columns))
    urgent = items - HQ // columns
    rank = [1] * (urgent - 2) + [0] * 2 + [2] * (items - urgent)
    source = [[g // per_chip for g in granules_of(c, columns)] for c in range(columns)]
    held = [[{k for k in range(items) if source[c][k] == z} for z in range(chips)] for c in range(columns)]
    steps = []
    urgent_steps = kv_steps = None
    while any(len(held[c][z]) < items for c in range(columns) for z in range(chips)):
        moves = {}
        for c in range(columns):
            for z in range(chips):
                for core, way in ((0, 1), (1, -1)):
                    if not 0 <= z + way < chips:
                        continue
                    ready = [
                        k
                        for k in held[c][z]
                        if k not in held[c][z + way] and (source[c][k] - z) * way <= 0
                    ]
                    if ready:
                        moves[c, z, core] = min(
                            ready, key=lambda k: (rank[k], abs(source[c][k] - z), k)
                        )
        for (c, z, core), k in moves.items():
            held[c][z + (1, -1)[core]].add(k)
        steps.append(moves)
        done = all(k in held[c][z] for c in range(columns) for z in range(chips) for k in range(urgent))
        if done and urgent_steps is None:
            urgent_steps = len(steps)
        done = all(
            k in held[c][z]
            for c in range(columns)
            for z in range(chips)
            for k in (urgent - 2, urgent - 1)
        )
        if done and kv_steps is None:
            kv_steps = len(steps)
    return steps, urgent_steps, kv_steps


def chosen(places, devices):
    names = []
    which = np.zeros((devices, len(places)), np.int32)
    slot = np.zeros((devices, len(places)), np.int32)
    for k, place in enumerate(places):
        for d in range(devices):
            name, at = place.get(d, ("mine", 0))
            if name not in names:
                names.append(name)
            which[d, k] = names.index(name)
            slot[d, k] = at
    return names, which, slot


def fetch(cands, which_ref, slot_ref, sources, place, buffer, sem):
    for code in cands[place]:

        @pl.when(which_ref[place] == code)
        def _(code=code):
            pltpu.make_async_copy(sources[code].at[slot_ref[place]], buffer, sem).start()


def pick_kernel(cands, which_ref, slot_ref, *refs):
    out_ref, buffers, in_sems, out_sems = refs[-4:]
    count, deep = len(cands), buffers.shape[0]

    def begin(k):
        at = k % deep
        fetch(cands, which_ref, slot_ref, refs, k, buffers.at[at], in_sems.at[at])

    def leaving(k):
        at = k % deep
        return pltpu.make_async_copy(buffers.at[at], out_ref.at[k], out_sems.at[at])

    for k in range(min(deep, count)):
        begin(k)
    for k in range(count):
        at = k % deep
        pltpu.make_async_copy(buffers.at[at], buffers.at[at], in_sems.at[at]).wait()
        leaving(k).start()
        again = k - deep // 2
        if again >= 0 and again + deep < count:
            leaving(again).wait()
            begin(again + deep)
    for k in range(max(0, count - deep), count):
        leaving(k).wait()


def project_kernel(cands, which_ref, slot_ref, rows_ref, *refs):
    out_ref, buffers, sems = refs[-3:]
    rows = buffers.shape[1]
    for k in range(len(cands)):
        fetch(cands, which_ref, slot_ref, refs, k, buffers.at[k], sems.at[k])
    for k in range(len(cands)):
        pltpu.make_async_copy(buffers.at[k], buffers.at[k], sems.at[k]).wait()
        out_ref[:, k * rows : (k + 1) * rows] = dot_nt(rows_ref[...], buffers[k]).astype(bf16)


def apply_kernel(cands, which_ref, slot_ref, rows_ref, *refs):
    out_ref, buffers, sems = refs[-3:]
    _, rows, width = buffers.shape
    for k in range(len(cands)):
        fetch(cands, which_ref, slot_ref, refs, k, buffers.at[k], sems.at[k])
    for k in range(len(cands)):
        pltpu.make_async_copy(buffers.at[k], buffers.at[k], sems.at[k]).wait()
    step = width // 3 if width % 384 == 0 else width
    for low in range(0, width, step):
        total = dot_nn(rows_ref[:, :rows], buffers[0, :, low : low + step])
        for k in range(1, len(cands)):
            total += dot_nn(
                rows_ref[:, k * rows : (k + 1) * rows], buffers[k, :, low : low + step]
            )
        out_ref[:, low : low + step] = total.astype(bf16)


def pick(places, sources, device, devices, kind="pick", rows_in=None):
    names, which, slot = chosen(places, devices)
    _, rows, width = sources["mine"].shape
    table = jnp.asarray(np.concatenate([which, slot], axis=1))[device]
    count = len(places)
    cands = [sorted(set(which[:, k].tolist())) for k in range(count)]
    kernel = {"pick": pick_kernel, "project": project_kernel, "apply": apply_kernel}[kind]
    args = [sources[name] for name in names]
    in_specs = [pl.BlockSpec(memory_space=pl.ANY)] * len(names)
    if kind == "pick":
        deep = min(count, 8)
        out_spec = pl.BlockSpec(memory_space=pl.ANY)
        out_shape = (count, rows, width)
        sems = [pltpu.SemaphoreType.DMA((deep,)), pltpu.SemaphoreType.DMA((deep,))]
    else:
        deep = count
        args = [rows_in] + args
        in_specs = [pl.BlockSpec(memory_space=pltpu.VMEM)] + in_specs
        out_spec = pl.BlockSpec(memory_space=pltpu.VMEM)
        out_shape = (rows_in.shape[0], count * rows if kind == "project" else width)
        sems = [pltpu.SemaphoreType.DMA((deep,))]
    return pl.pallas_call(
        functools.partial(kernel, cands),
        grid_spec=pltpu.PrefetchScalarGridSpec(
            num_scalar_prefetch=2,
            grid=(1,),
            in_specs=in_specs,
            out_specs=out_spec,
            scratch_shapes=[pltpu.VMEM((deep, rows, width), bf16)] + sems,
        ),
        out_shape=jax.ShapeDtypeStruct(out_shape, bf16),
        compiler_params=pltpu.CompilerParams(vmem_limit_bytes=58 * 2**20),
        name=kind,
    )(table[:count], table[count:], *args)


def routed_weights(attn_weight, column, shard, columns, shards, between):
    rows, width = attn_weight.shape
    count = rows // HD
    chips = shards // 2
    devices = columns * shards
    device = column * shards + shard
    swap = [(f, f ^ 1) for f in range(shards)]
    items = len(granules_of(0, columns))
    urgent = items - HQ // columns
    steps, urgent_steps, kv_steps = route(columns, chips, 2 * count)
    mine = attn_weight.reshape(count, HD, width)
    theirs = between("start", lax.ppermute(mine, "fsdp", swap))
    sources = {"mine": mine, "theirs": theirs}
    at = [{} for _ in range(items)]
    for c in range(columns):
        for f in range(shards):
            for k, g in enumerate(granules_of(c, columns)):
                if g // (2 * count) == f // 2:
                    at[k][c * shards + f] = ("mine" if g // count == f else "theirs", g % count)
    sends = []
    for number, moves in enumerate(steps):
        own, passed, pairs = {}, {}, []
        for (c, z, core), k in moves.items():
            here = c * shards + 2 * z + core
            to = here + (2, -2)[core]
            name, slot = at[k][here]
            if name in ("mine", "theirs"):
                own[here] = (name, slot)
            else:
                passed[here] = name
            pairs.append((here, to))
            at[k][to] = ("got%d" % number, 0)
            at[k][to ^ 1] = ("swapped%d" % number, 0)
        sends.append((own, passed, pairs))
    with_own = [n for n in range(1, len(sends)) if sends[n][0]]
    own_first = pick([sends[0][0]], sources, device, devices)
    own_later = None
    for number, (own, passed, pairs) in enumerate(sends):
        if number == 0:
            piece = own_first
        else:
            names = sorted(set(passed.values()))
            code = np.zeros((devices,), np.int32)
            for d, name in passed.items():
                code[d] = 1 + names.index(name)
            here = jnp.asarray(code)[device]
            piece = sources[names[-1]]
            for i, name in enumerate(names[:-1]):
                piece = jnp.where(here == 1 + i, sources[name], piece)
            if number in with_own:
                place = with_own.index(number)
                piece = jnp.where(here == 0, own_later[place : place + 1], piece)
        got = lax.ppermute(piece, ("seq", "fsdp"), pairs)
        if number == 0:
            own_later = pick([sends[n][0] for n in with_own], sources, device, devices)
            got, own_later = lax.optimization_barrier((got, own_later))
        if number < urgent_steps:
            got = between(number, got)
        if 0 < number < urgent_steps:
            before = "swapped%d" % (number - 1)
            got, sources[before] = lax.optimization_barrier((got, sources[before]))
        sources["got%d" % number] = got
        if number < urgent_steps:
            sources["swapped%d" % number] = lax.ppermute(got, "fsdp", swap)
        for name, wanted, count_of in (
            ("kv", (urgent - 2, urgent), kv_steps),
            ("q", (0, urgent - 2), urgent_steps),
        ):
            if number + 1 == count_of:
                ready = dict(sources)
                places = [dict(place) for place in at[slice(*wanted)]]
                between(
                    name,
                    lambda times, ready=ready, places=places: pick(
                        places, ready, device, devices, "project", times
                    ),
                )

    def first(after):
        held, after = lax.optimization_barrier((ready, after))
        return pick(at[:urgent], held, device, devices)

    held = None

    def times_rest(rows_in):
        nonlocal held
        held, rows_in = lax.optimization_barrier((sources, rows_in))
        for number in range(urgent_steps, len(steps)):
            held["swapped%d" % number] = lax.ppermute(held["got%d" % number], "fsdp", swap)
        return pick(at[urgent:], held, device, devices, "apply", rows_in)

    def others(after):
        kept, after = lax.optimization_barrier((held, after))
        return pick(at[urgent:], kept, device, devices)

    return first, times_rest, others


def column_weights(attn_weight, column, shard, columns, shards, between):
    rows, width = attn_weight.shape
    per = HQ // columns
    if rows % HD == 0 and shards == 8 and columns == 4:
        return routed_weights(attn_weight, column, shard, columns, shards, between)
    whole = lax.all_gather(attn_weight, "fsdp", axis=0, tiled=True).reshape(-1, HD, width)
    table = np.array([granules_of(c, columns) for c in range(columns)], np.int32)
    place = jnp.asarray(table)[column]
    taken = jnp.concatenate(
        [lax.dynamic_slice_in_dim(whole, place[k], 1, 0) for k in range(table.shape[1])], axis=0
    )
    for name, low, high in (("kv", per, per + 2), ("q", 0, per)):
        between(
            name,
            lambda times, low=low, high=high: dot_nt(
                times, taken[low:high].reshape(-1, width)
            ).astype(bf16),
        )
    return (
        lambda after: taken[: per + 2],
        lambda rows_in: dot_nn(rows_in, taken[per + 2 :].reshape(-1, width)).astype(bf16),
        lambda after: taken[per + 2 :],
    )


def ring_of(chips):
    return [0] + list(range(1, chips, 2)) + [z for z in range(chips - 1, 0, -1) if z % 2 == 0]


def ring_tables(shards):
    chips = shards // 2
    order = ring_of(chips)
    spot = {z: p for p, z in enumerate(order)}
    pairs = [
        (2 * z + c, 2 * order[(spot[z] + 1) % chips] + c) for z in range(chips) for c in range(2)
    ]
    behind = np.array(
        [[order[(spot[f // 2] - t) % chips] for t in range(chips + 1)] for f in range(shards)],
        np.int32,
    )
    return chips, pairs, behind


def ring_pieces(block, shard, shards, beside):
    chips, pairs, behind = ring_tables(shards)
    swap = [(f, f ^ 1) for f in range(shards)]
    source = jnp.asarray(behind)[shard]
    core = shard % 2
    pieces = []
    held = block
    for t in range(chips):
        if t:
            held = lax.ppermute(held, "fsdp", pairs)
            held = beside(t, held)
        pieces.append((held, 2 * source[t] + core))
        pieces.append((lax.ppermute(held, "fsdp", swap), 2 * source[t] + 1 - core))
    return pieces


def direct_pieces(block, shard, shards, wanted):
    chips = shards // 2
    swap = [(f, f ^ 1) for f in range(shards)]
    core = shard % 2
    come = [block] + [
        lax.ppermute(
            block,
            "fsdp",
            [
                (f, (f + 2 * hop) % shards)
                for f in range(shards)
                if (f + 2 * hop) % shards // 2 in wanted
            ],
        )
        for hop in range(1, chips)
    ]

    def finish(after):
        held, after = lax.optimization_barrier((come, after))
        pieces = []
        for hop, piece in enumerate(held):
            chip = (shard // 2 - hop) % chips
            pieces.append((piece, 2 * chip + core))
            pieces.append((lax.ppermute(piece, "fsdp", swap), 2 * chip + 1 - core))
        return pieces, after

    return finish


def weight_grad_kernel(half, place_ref, cols_ref, *refs):
    pieces = refs[: 2 * half]
    out_ref, rows_ref, turned_ref, sems = refs[2 * half :]
    lines = pieces[0].shape[0]
    for i, piece in enumerate(pieces):
        start = pl.multiple_of(place_ref[i] * lines, lines)
        pltpu.make_async_copy(
            piece, rows_ref.at[i // half, pl.ds(start, lines)], sems.at[i]
        ).start()
    limit = place_ref[2 * half]
    turned = cols_ref[...].T
    col = lax.broadcasted_iota(jnp.int32, turned.shape, 0)
    turned_ref[0] = jnp.where(col < limit, turned, 0)
    turned_ref[1] = jnp.where(col < limit, 0, turned)
    for i, piece in enumerate(pieces):
        pltpu.make_async_copy(piece, rows_ref.at[0, pl.ds(0, lines)], sems.at[i]).wait()
    width = out_ref.shape[1]
    step = width // 3 if width % 384 == 0 else width

    def chunk(n, carry):
        cut = pl.ds(pl.multiple_of(n * step, step), step)
        total = dot_nn(turned_ref[0], rows_ref[0, :, cut])
        total += dot_nn(turned_ref[1], rows_ref[1, :, cut])
        out_ref[:, cut] = total.astype(bf16)
        return carry

    lax.fori_loop(0, width // step, chunk, 0)


def weight_grad(cols, limit, first, second):
    lines, width = first[0][0].shape
    half = len(first)
    place = jnp.stack(
        [where.astype(jnp.int32) for _, where in first + second] + [limit.astype(jnp.int32)]
    )
    return pl.pallas_call(
        functools.partial(weight_grad_kernel, half),
        grid_spec=pltpu.PrefetchScalarGridSpec(
            num_scalar_prefetch=1,
            grid=(1,),
            in_specs=[pl.BlockSpec(memory_space=pltpu.VMEM)]
            + [pl.BlockSpec(memory_space=pl.ANY)] * (2 * half),
            out_specs=pl.BlockSpec(memory_space=pltpu.VMEM),
            scratch_shapes=[
                pltpu.VMEM((2, half * lines, width), bf16),
                pltpu.VMEM((2, cols.shape[1], cols.shape[0]), bf16),
                pltpu.SemaphoreType.DMA((2 * half,)),
            ],
        ),
        out_shape=jax.ShapeDtypeStruct((cols.shape[1], width), bf16),
        compiler_params=pltpu.CompilerParams(vmem_limit_bytes=58 * 2**20),
        name="weight_grad",
    )(place, cols, *[piece for piece, _ in first + second])


def ring_scatter(parts, shard, shards):
    chips, pairs, behind = ring_tables(shards)
    swap = [(f, f ^ 1) for f in range(shards)]
    target = jnp.asarray(behind)[shard]
    core = shard % 2
    paired = parts.reshape((chips, 2) + parts.shape[1:])
    mine = lax.dynamic_index_in_dim(paired, core, 1, keepdims=False)
    other = lax.ppermute(
        lax.dynamic_index_in_dim(paired, 1 - core, 1, keepdims=False), "fsdp", swap
    )

    def local_sum(t):
        return lax.dynamic_index_in_dim(mine, target[t], 0, keepdims=False).astype(
            f32
        ) + lax.dynamic_index_in_dim(other, target[t], 0, keepdims=False).astype(f32)

    total = local_sum(1)
    for t in range(1, chips):
        total = lax.ppermute(total.astype(bf16), "fsdp", pairs).astype(f32) + local_sum(t + 1)
    return total


def partners(columns, bit):
    return [(c, c ^ bit) for c in range(columns)]


def column_scatter(parts):
    half = parts.shape[-1] // 2
    done = []
    for first, second, cut in ((1, 2, slice(0, half)), (2, 1, slice(half, None))):
        low = parts[..., cut]
        got = lax.ppermute(
            jnp.concatenate([low[first : first + 1], low[3:]], axis=0), "seq", partners(4, first)
        )
        keep = low[0].astype(f32) + got[0].astype(f32)
        away = low[second].astype(f32) + got[1].astype(f32)
        done.append(
            keep + lax.ppermute(away.astype(bf16), "seq", partners(4, second)).astype(f32)
        )
    return jnp.concatenate(done, axis=-1)


def column_total(value, column, later):
    rows, width = value.shape
    step, half = rows // 4, width // 2
    parts = jnp.stack(
        [lax.dynamic_slice_in_dim(value, (column ^ k) * step, step, 0) for k in range(4)]
    )
    own = column_scatter(parts).astype(bf16)
    own, *later = lax.optimization_barrier((own, *later))
    pieces = (own[:, :half], own[:, half:])
    near = tuple(lax.ppermute(p, "seq", partners(4, bit)) for p, bit in zip(pieces, (1, 2)))
    near, *later = lax.optimization_barrier((near, *later))
    out = jnp.zeros((rows, width), f32)
    for first, second, low, piece, got in (
        (1, 2, 0, pieces[0], near[0]),
        (2, 1, half, pieces[1], near[1]),
    ):
        far = lax.ppermute(jnp.stack([piece, got]), "seq", partners(4, second))
        for k, block in ((0, piece), (first, got), (second, far[0]), (3, far[1])):
            out = lax.dynamic_update_slice(
                out, block.astype(f32), ((column ^ k) * step, low)
            )
    return (out, *later)


def sum_over(value, axis, count):
    bit = 1
    while bit < count:
        value = value + lax.ppermute(value, axis, [(c, c ^ bit) for c in range(count)])
        bit *= 2
    return value


def local(tokens, attn_weight, norm_gains, ffn_weight, out_grad):
    seqs, rows, width = tokens.shape
    columns = lax.axis_size("seq")
    shards = lax.axis_size("fsdp")
    column = lax.axis_index("seq")
    shard = lax.axis_index("fsdp")
    core = shard % 2
    per = HQ // columns
    own_rows = seqs * rows
    swap = [(f, f ^ 1) for f in range(shards)]
    shard_arg = shard.astype(jnp.int32).reshape(1)

    def core_half(granules):
        return lax.dynamic_index_in_dim(
            granules.reshape(-1, 2, HALF, width), core, 1, keepdims=False
        )

    def all_columns(own, other, begin, end):
        count = own.shape[1]
        sources = {
            "mine": own.reshape(columns * count, HALF, width),
            "other": other.reshape(columns * count, HALF, width),
        }
        places = [
            {
                c * shards + f: ("mine" if f % 2 == half else "other", home * count + k)
                for c in range(columns)
                for f in range(shards)
            }
            for home in range(columns)
            for k in range(begin, end)
            for half in range(2)
        ]
        device = column * shards + shard
        return pick(places, sources, device, columns * shards).reshape(-1, width)

    token_slices = lax.all_gather(tokens, "seq", axis=0)
    gain_rows = lax.all_gather(norm_gains, "fsdp", axis=1, tiled=True).astype(f32)
    normed_slices = rms_scale(
        token_slices.reshape(-1, width).astype(f32), gain_rows[0]
    ).astype(bf16)
    made = {}

    def between(step, value):
        nonlocal normed_slices, gain_rows
        if step == "start":
            value, gain_rows = lax.optimization_barrier((value, gain_rows))
            normed_slices = rms_scale(
                token_slices.reshape(-1, width).astype(f32), gain_rows[0]
            ).astype(bf16)
        if step == 1:
            value, normed_slices = lax.optimization_barrier((value, normed_slices))
        if step == 2:
            value, made["kv"] = lax.optimization_barrier((value, made["kv"]))
        if step in ("kv", "q"):
            made[step] = value(normed_slices)
        return value

    first_weights, times_out, out_weights = column_weights(
        attn_weight, column, shard, columns, shards, between
    )
    kv_all = lax.all_gather(made["kv"].reshape(columns, seqs, rows, 2 * HD), "fsdp", axis=0)
    queries = made["q"].reshape(columns, seqs, rows, per * HD)
    flat_tokens = tokens.reshape(-1, width).astype(f32)
    flat_cot = out_grad.reshape(-1, width).astype(f32)
    normed_own = rms_scale(flat_tokens, gain_rows[0]).astype(bf16)
    normed_own, kv_all = lax.optimization_barrier((normed_own, kv_all))
    mixed, lse = attend(shard_arg, queries, kv_all)
    kept = {"mixed": mixed}

    def beside(step, held):
        if step == 1:
            held, kept["mixed"] = lax.optimization_barrier((held, kept["mixed"]))
            if columns == 4:
                by_partner = jnp.concatenate(
                    [
                        lax.dynamic_slice_in_dim(kept["mixed"], column ^ k, 1, 0)
                        for k in range(columns)
                    ],
                    axis=0,
                )
                kept["part"] = times_out(by_partner.reshape(columns * own_rows, per * HD))
            else:
                kept["part"] = times_out(kept["mixed"].reshape(-1, per * HD))
        if step == 2:
            held, kept["part"] = lax.optimization_barrier((held, kept["part"]))
            if columns == 4:
                kept["out"] = column_scatter(kept["part"].reshape(columns, own_rows, width))
            else:
                kept["out"] = lax.psum_scatter(
                    kept["part"], "seq", scatter_dimension=0, tiled=True
                ).astype(f32)
        if step == 3:
            held, kept["out"] = lax.optimization_barrier((held, kept["out"]))
        return held

    normed_pieces = ring_pieces(normed_own, shard, shards, beside)
    mixed, attn_out = kept["mixed"], kept["out"]
    lanes = jnp.concatenate(
        [core_half(first_weights(mixed)), core_half(out_weights(mixed))], axis=0
    )
    attn_out, lanes = lax.optimization_barrier((attn_out, lanes))
    kept["lanes"] = lax.all_gather(lanes, "seq", axis=0)
    residual = flat_tokens + rms_scale(attn_out, gain_rows[1])
    normed_ffn = rms_scale(residual, gain_rows[2]).astype(bf16)

    chips, ring, _ = ring_tables(shards)
    weight_gate_up, weight_down = ffn_weight[:, :2], ffn_weight[:, 2]

    def pipeline(block, work, aside, before_last):
        held = block
        for t in range(chips):
            rows_here = jnp.concatenate([held, lax.ppermute(held, "fsdp", swap)], axis=0)
            if t + 1 < chips:
                held = lax.ppermute(held, "fsdp", ring)
            made = work(t, rows_here).astype(bf16)
            got = lax.ppermute(made[own_rows:], "fsdp", swap)
            pair = made[:own_rows].astype(f32) + got.astype(f32)
            if t == 0:
                first = pair
            else:
                total = pair if t == 1 else total + pair
            if t + 1 < chips:
                held, made = aside(t, *lax.optimization_barrier((held, made)))
            if t:
                total = total.astype(bf16)
                if t + 1 < chips:
                    held, total = lax.optimization_barrier((held, total))
                else:
                    total = before_last(total)
                total = lax.ppermute(total, "fsdp", ring).astype(f32)
        return total + first

    saved = []

    def forward(t, rows_here):
        gate_up = jnp.einsum(
            "td,fgd->tgf", rows_here, weight_gate_up, preferred_element_type=f32
        )
        hidden = gated_units(gate_up[:, 0], gate_up[:, 1]).astype(bf16)
        saved.append((rows_here, gate_up, hidden))
        return dot_nn(hidden, weight_down)

    ffn_out = pipeline(
        normed_ffn, forward, lambda t, held, made: (held, made), lambda total: total
    )
    result = residual + rms_scale(ffn_out, gain_rows[3])
    block_out = result.astype(bf16).reshape(tokens.shape)
    grad_ffn, gain_terms = norm_back(ffn_out, gain_rows[3], flat_cot)
    gain_last = jnp.sum(gain_terms, axis=0)

    back = []

    def backward(t, grads_here):
        grad_hidden = dot_nt(grads_here, weight_down)
        _, gate_up, _ = saved[t]
        unused, gated_pull = jax.vjp(gated_units, gate_up[:, 0], gate_up[:, 1])
        grad_gate, grad_up = gated_pull(grad_hidden)
        units = jnp.stack([grad_gate, grad_up], axis=1).astype(bf16)
        back.append((grads_here, units))
        return jnp.einsum("tgf,fgd->td", units, weight_gate_up, preferred_element_type=f32)

    def backward_aside(t, held, made):
        if t == chips - 2:
            held, made, kept["lanes"] = lax.optimization_barrier((held, made, kept["lanes"]))
        return held, made

    def units_after(total):
        total, units = lax.optimization_barrier((total, [part for _, part in back]))
        kept["units"] = units
        return total

    grad_normed_ffn = pipeline(grad_ffn.astype(bf16), backward, backward_aside, units_after)
    ffn_in = jnp.concatenate([rows_here for rows_here, _, _ in saved], axis=0)
    hidden = jnp.concatenate([units for _, _, units in saved], axis=0)
    grad_ffn_all = jnp.concatenate([grads_here for grads_here, _ in back], axis=0)
    units = jnp.concatenate(kept["units"], axis=0)
    gate_grad, up_grad, down_grad = lax.psum(
        (
            dot_tn(units[:, 0], ffn_in).astype(bf16),
            dot_tn(units[:, 1], ffn_in).astype(bf16),
            dot_tn(hidden, grad_ffn_all).astype(bf16),
        ),
        "seq",
    )

    def attention_back():
        other_lanes = lax.ppermute(kept["lanes"], "fsdp", swap)
        weight_in_all = all_columns(kept["lanes"], other_lanes, 0, per + 2)
        weight_out_all = all_columns(kept["lanes"], other_lanes, per + 2, 2 * per + 2)
        grad_mid, gain_pre_ffn = norm_back(residual, gain_rows[2], grad_normed_ffn)
        grad_residual = flat_cot + grad_mid
        grad_attn, gain_post_attn = norm_back(attn_out, gain_rows[1], grad_residual)
        grad_attn_low = grad_attn.astype(bf16)
        grad_mixed = (
            dot_nt(grad_attn_low, weight_out_all)
            .astype(bf16)
            .reshape(seqs, rows, columns, per * HD)
        )
        both = lax.all_to_all(
            jnp.concatenate([grad_mixed.transpose(2, 0, 1, 3), mixed], axis=-1),
            "seq",
            split_axis=0,
            concat_axis=0,
            tiled=True,
        )
        grad_heads = both[..., : per * HD]
        mixed_rows = both[..., per * HD :].transpose(1, 2, 0, 3).reshape(own_rows, HQ * HD)
        shard_cols = attn_weight.shape[0]
        first_owner = (HQ + 2 * KVH) * HD // shard_cols // 2
        later_pieces = direct_pieces(
            grad_attn_low, shard, shards, range(first_owner, shards // 2)
        )
        grad_queries, grad_kv = attend_back(shard_arg, queries, grad_heads, lse, kv_all)
        grad_kv_own = (
            ring_scatter(grad_kv.reshape(shards, columns * own_rows, 2 * HD), shard, shards)
            .astype(bf16)
            .reshape(columns, seqs, rows, 2 * HD)
        )
        grad_proj = lax.all_to_all(
            jnp.concatenate([grad_queries, grad_kv_own], axis=-1),
            "seq",
            split_axis=0,
            concat_axis=0,
            tiled=True,
        )
        attn_pieces, grad_proj = later_pieces(grad_proj)
        grad_rows = grad_proj.reshape(columns, own_rows, (per + 2) * HD).transpose(1, 0, 2)
        grad_normed = dot_nn(grad_rows.reshape(own_rows, -1), weight_in_all)
        grad_tokens, gain_pre_attn = norm_back(flat_tokens, gain_rows[0], grad_normed)
        token_grad = (grad_residual + grad_tokens).reshape(tokens.shape)

        def shared(copies):
            if columns == KVH:
                return copies.reshape(own_rows, -1)
            summed = copies.reshape(own_rows, KVH, columns // KVH, HD).astype(f32).sum(axis=2)
            return summed.astype(bf16).reshape(own_rows, -1)

        weight_cols = jnp.concatenate(
            [
                grad_rows[:, :, : per * HD].reshape(own_rows, -1),
                shared(grad_rows[:, :, per * HD : (per + 1) * HD]),
                shared(grad_rows[:, :, (per + 1) * HD :]),
                mixed_rows,
            ],
            axis=1,
        )
        col_all = lax.all_to_all(
            weight_cols.reshape(own_rows, shards, shard_cols).transpose(1, 0, 2),
            "fsdp",
            split_axis=0,
            concat_axis=0,
            tiled=True,
        ).reshape(-1, shard_cols)
        limit = jnp.clip((HQ + 2 * KVH) * HD - shard * shard_cols, 0, shard_cols)
        attn_grad = weight_grad(col_all, limit, normed_pieces, attn_pieces)
        gain_grad = jnp.stack(
            [
                jnp.sum(gain_pre_attn, axis=0),
                jnp.sum(gain_post_attn, axis=0),
                jnp.sum(gain_pre_ffn, axis=0),
                gain_last,
            ]
        )
        gain_grad = lax.dynamic_slice_in_dim(
            sum_over(gain_grad, "fsdp", shards),
            shard * norm_gains.shape[1],
            norm_gains.shape[1],
            1,
        )
        return attn_grad, gain_grad, token_grad

    def nothing():
        return (
            jnp.zeros(attn_weight.shape, bf16),
            jnp.zeros(norm_gains.shape, f32),
            jnp.zeros(tokens.shape, f32),
        )

    attn_grad, gain_grad, token_grad = lax.cond(
        shard < 2**20, attention_back, nothing
    )
    gain_total = sum_over(gain_grad, "seq", columns)
    if columns == 4:
        attn_total, gate_grad, up_grad, down_grad = column_total(
            attn_grad, column, (gate_grad, up_grad, down_grad)
        )
    else:
        attn_grad, gate_grad, up_grad, down_grad = lax.optimization_barrier(
            (attn_grad, gate_grad, up_grad, down_grad)
        )
        attn_total = lax.psum(attn_grad, "seq").astype(f32)
    ffn_grad = widen_plane(down_grad, 2, 3, None)
    ffn_grad = widen_plane(gate_grad, 0, 3, ffn_grad)
    ffn_grad = widen_plane(up_grad, 1, 3, ffn_grad)
    ffn_grad = ffn_grad.transpose(1, 0, 2)
    return (block_out, token_grad, attn_total, gain_total, ffn_grad)


def solution(mesh):
    in_specs = (
        P(None, ("seq", "fsdp"), None),
        P("fsdp", None),
        P(None, "fsdp"),
        P("fsdp", None, None),
        P(None, ("seq", "fsdp"), None),
    )
    out_specs = (
        P(None, ("seq", "fsdp"), None),
        P(None, ("seq", "fsdp"), None),
        P("fsdp", None),
        P(None, "fsdp"),
        P("fsdp", None, None),
    )
    return jax.shard_map(local, mesh=mesh, in_specs=in_specs, out_specs=out_specs, check_vma=False)
```

```python
import functools

import jax
import jax.numpy as jnp
import numpy as np
from jax import lax
from jax.experimental import pallas as pl
from jax.experimental.pallas import tpu as pltpu
from jax.sharding import PartitionSpec as P

HQ = 8
KVH = 4
HD = 256
GROUP = HQ // KVH
HALF = HD // 2

soft_cap = 50.0
norm_eps = 1e-06
bf16 = jnp.bfloat16
f32 = jnp.float32


def rms_scale(values, gain_row):
    return (
        values * lax.rsqrt(jnp.mean(values * values, axis=-1, keepdims=True) + norm_eps) * gain_row
    )


def norm_back(values, gain_row, cotangent):
    inverse = lax.rsqrt(jnp.mean(values * values, axis=-1, keepdims=True) + norm_eps)
    unit_rows = values * inverse
    scaled = cotangent * gain_row
    grad_values = inverse * (
        scaled - unit_rows * jnp.mean(scaled * unit_rows, axis=-1, keepdims=True)
    )
    return (grad_values, cotangent * unit_rows)


def gated_units(gate_proj, up_proj):
    return jax.nn.gelu(gate_proj, approximate=True) * up_proj


def dot_nt(a, b):
    return lax.dot_general(a, b, (((1,), (1,)), ((), ())), preferred_element_type=f32)


def dot_nn(a, b):
    return lax.dot_general(a, b, (((1,), (0,)), ((), ())), preferred_element_type=f32)


def dot_tn(a, b):
    return lax.dot_general(a, b, (((0,), (0,)), ((), ())), preferred_element_type=f32)


def stacked_heads(block):
    heads = block.shape[1] // HD
    return jnp.concatenate([block[:, h * HD : (h + 1) * HD] for h in range(heads)], axis=0)


def visible_of(shard, rows, keys, lines):
    shape = (lines, keys)
    row = lax.broadcasted_iota(jnp.int32, shape, 0) & (rows - 1)
    col = lax.broadcasted_iota(jnp.int32, shape, 1)
    return col <= shard * rows + row


def lane_sums(values):
    return sum(values[:, low : low + 128] for low in range(0, values.shape[1], 128))


def attend_kernel(shard_ref, q_ref, kv_ref, o_ref, lse_ref, weight_ref):
    own = pl.program_id(1)
    shard = shard_ref[0]
    parts, _, _, rows, _ = kv_ref.shape
    keys = parts * rows
    queries = stacked_heads(q_ref[0, 0])
    lines = queries.shape[0]

    def exponentials(block):
        key_block = kv_ref[:, block, 0, :, :HD].reshape(keys, HD)
        bounded = jnp.tanh(dot_nt(queries, key_block) * (HD ** (-0.5) / soft_cap))
        return jnp.exp(soft_cap * bounded)

    def score_step(block, total):
        expanded = exponentials(block)
        weight_ref[block] = expanded
        return total + lane_sums(expanded)

    total = lax.fori_loop(0, own, score_step, jnp.zeros((lines, 128), f32))
    expanded = jnp.where(visible_of(shard, rows, keys, lines), exponentials(own), 0.0)
    weight_ref[own] = expanded
    total = jnp.sum(total + lane_sums(expanded), axis=-1, keepdims=True)
    inverse = 1.0 / total

    def mix_step(block, mixed):
        weights = (weight_ref[block] * inverse).astype(bf16)
        value_block = kv_ref[:, block, 0, :, HD:].reshape(keys, HD)
        return mixed + dot_nn(weights, value_block)

    mixed = lax.fori_loop(0, own + 1, mix_step, jnp.zeros((lines, HD), f32))
    for h in range(lines // rows):
        o_ref[0, 0, :, h * HD : (h + 1) * HD] = mixed[h * rows : (h + 1) * rows].astype(bf16)
    lse_ref[0, 0] = jnp.broadcast_to(jnp.log(total), (lines, 128))


def attend_back_kernel(
    shard_ref, q_ref, do_ref, lse_ref, kv_ref, dq_ref, dkv_ref, weight_ref, dp_ref, acc_ref
):
    own = pl.program_id(1)
    shard = shard_ref[0]
    parts, blocks, _, rows, _ = kv_ref.shape
    keys = parts * rows
    queries = stacked_heads(q_ref[0, 0])
    grads = stacked_heads(do_ref[0, 0])
    lse = lse_ref[0, 0][:, :1]
    lines = queries.shape[0]

    @pl.when(own == 0)
    def _():
        acc_ref[...] = jnp.zeros_like(acc_ref)

    def first_part(block, masked):
        key_block = kv_ref[:, block, 0, :, :HD].reshape(keys, HD)
        value_block = kv_ref[:, block, 0, :, HD:].reshape(keys, HD)
        bounded = jnp.tanh(dot_nt(queries, key_block) * (HD ** (-0.5) / soft_cap))
        weights = jnp.exp(soft_cap * bounded - lse)
        if masked:
            weights = jnp.where(visible_of(shard, rows, keys, lines), weights, 0.0)
        grad_weights = dot_nt(grads, value_block)
        acc_ref[block, :, HD:] += dot_tn(weights.astype(bf16), grads)
        weight_ref[block] = weights * (1.0 - bounded * bounded)
        dp_ref[block] = grad_weights
        return lane_sums(weights * grad_weights)

    delta = lax.fori_loop(
        0,
        own,
        lambda block, delta: delta + first_part(block, False),
        jnp.zeros((lines, 128), f32),
    )
    delta = jnp.sum(delta + first_part(own, True), axis=-1, keepdims=True)

    def second_step(block, grad_query):
        key_block = kv_ref[:, block, 0, :, :HD].reshape(keys, HD)
        grad_raw = (weight_ref[block] * (dp_ref[block] - delta)).astype(bf16)
        acc_ref[block, :, :HD] += dot_tn(grad_raw, queries)
        return grad_query + dot_nn(grad_raw, key_block)

    grad_query = lax.fori_loop(0, own + 1, second_step, jnp.zeros((lines, HD), f32)) * HD ** (-0.5)
    for h in range(lines // rows):
        dq_ref[0, 0, :, h * HD : (h + 1) * HD] = grad_query[h * rows : (h + 1) * rows].astype(bf16)

    @pl.when(own == blocks - 1)
    def _():
        for block in range(blocks):
            dkv_ref[:, block, 0, :, :HD] = (
                (acc_ref[block, :, :HD] * HD ** (-0.5)).astype(bf16).reshape(parts, rows, HD)
            )
            dkv_ref[:, block, 0, :, HD:] = (
                acc_ref[block, :, HD:].astype(bf16).reshape(parts, rows, HD)
            )


def attend(shard, queries, kv_all):
    blocks, seqs, rows, width = queries.shape
    lines = rows * width // HD
    parts = kv_all.shape[0]
    keys = parts * rows
    row_spec = pl.BlockSpec((1, 1, rows, width), lambda n, s, shard: (s, n, 0, 0))
    lse_spec = pl.BlockSpec((1, 1, lines, 128), lambda n, s, shard: (s, n, 0, 0))
    kv_spec = pl.BlockSpec((parts, blocks, 1, rows, 2 * HD), lambda n, s, shard: (0, 0, n, 0, 0))
    return pl.pallas_call(
        attend_kernel,
        grid_spec=pltpu.PrefetchScalarGridSpec(
            num_scalar_prefetch=1,
            grid=(seqs, blocks),
            in_specs=[row_spec, kv_spec],
            out_specs=[row_spec, lse_spec],
            scratch_shapes=[pltpu.VMEM((blocks, lines, keys), f32)],
        ),
        out_shape=[
            jax.ShapeDtypeStruct(queries.shape, bf16),
            jax.ShapeDtypeStruct((blocks, seqs, lines, 128), f32),
        ],
        compiler_params=pltpu.CompilerParams(vmem_limit_bytes=48 * 2**20),
        name="attend",
    )(shard, queries, kv_all)


def attend_back(shard, queries, grads, lse, kv_all):
    blocks, seqs, rows, width = queries.shape
    lines = rows * width // HD
    parts = kv_all.shape[0]
    keys = parts * rows
    row_spec = pl.BlockSpec((1, 1, rows, width), lambda n, s, shard: (s, n, 0, 0))
    lse_spec = pl.BlockSpec((1, 1, lines, 128), lambda n, s, shard: (s, n, 0, 0))
    deep = 2 if keys * blocks <= 4096 else 1
    kv_spec = pl.BlockSpec(
        (parts, blocks, 1, rows, 2 * HD),
        lambda n, s, shard: (0, 0, n, 0, 0),
        pipeline_mode=pl.Buffered(deep),
    )
    return pl.pallas_call(
        attend_back_kernel,
        grid_spec=pltpu.PrefetchScalarGridSpec(
            num_scalar_prefetch=1,
            grid=(seqs, blocks),
            in_specs=[row_spec, row_spec, lse_spec, kv_spec],
            out_specs=[row_spec, kv_spec],
            scratch_shapes=[
                pltpu.VMEM((blocks, lines, keys), f32),
                pltpu.VMEM((blocks, lines, keys), f32),
                pltpu.VMEM((blocks, keys, 2 * HD), f32),
            ],
        ),
        out_shape=[
            jax.ShapeDtypeStruct(queries.shape, bf16),
            jax.ShapeDtypeStruct(kv_all.shape, bf16),
        ],
        compiler_params=pltpu.CompilerParams(vmem_limit_bytes=56 * 2**20),
        name="attend_back",
    )(shard, queries, grads, lse, kv_all)


def widen_kernel(*refs):
    refs[-1][0] = refs[0][...].astype(f32)


def widen_plane(plane, index, planes, whole):
    rows, width = plane.shape
    step = rows // 4 if rows % 64 == 0 else rows
    specs = [pl.BlockSpec((step, width), lambda i: (i, 0))]
    args = [plane]
    aliases = {}
    if whole is not None:
        specs.append(pl.BlockSpec(memory_space=pl.ANY))
        args.append(whole)
        aliases = {1: 0}
    return pl.pallas_call(
        widen_kernel,
        grid=(rows // step,),
        in_specs=specs,
        out_specs=pl.BlockSpec((1, step, width), lambda i: (index, i, 0)),
        out_shape=jax.ShapeDtypeStruct((planes, rows, width), f32),
        input_output_aliases=aliases,
        compiler_params=pltpu.CompilerParams(vmem_limit_bytes=40 * 2**20),
        name="widen",
    )(*args)


def granules_of(column, columns):
    per = HQ // columns
    first = column * per
    return (
        [first + i for i in range(per)]
        + [HQ + first // GROUP, HQ + KVH + first // GROUP]
        + [HQ + 2 * KVH + first + i for i in range(per)]
    )


def route(columns, chips, per_chip):
    items = len(granules_of(0, columns))
    urgent = items - HQ // columns
    rank = [1] * (urgent - 2) + [0] * 2 + [2] * (items - urgent)
    source = [[g // per_chip for g in granules_of(c, columns)] for c in range(columns)]
    held = [[{k for k in range(items) if source[c][k] == z} for z in range(chips)] for c in range(columns)]
    steps = []
    urgent_steps = kv_steps = None
    while any(len(held[c][z]) < items for c in range(columns) for z in range(chips)):
        moves = {}
        for c in range(columns):
            for z in range(chips):
                for core, way in ((0, 1), (1, -1)):
                    if not 0 <= z + way < chips:
                        continue
                    ready = [
                        k
                        for k in held[c][z]
                        if k not in held[c][z + way] and (source[c][k] - z) * way <= 0
                    ]
                    if ready:
                        moves[c, z, core] = min(
                            ready, key=lambda k: (rank[k], abs(source[c][k] - z), k)
                        )
        for (c, z, core), k in moves.items():
            held[c][z + (1, -1)[core]].add(k)
        steps.append(moves)
        done = all(k in held[c][z] for c in range(columns) for z in range(chips) for k in range(urgent))
        if done and urgent_steps is None:
            urgent_steps = len(steps)
        done = all(
            k in held[c][z]
            for c in range(columns)
            for z in range(chips)
            for k in (urgent - 2, urgent - 1)
        )
        if done and kv_steps is None:
            kv_steps = len(steps)
    return steps, urgent_steps, kv_steps


def chosen(places, devices):
    names = []
    which = np.zeros((devices, len(places)), np.int32)
    slot = np.zeros((devices, len(places)), np.int32)
    for k, place in enumerate(places):
        for d in range(devices):
            name, at = place.get(d, ("mine", 0))
            if name not in names:
                names.append(name)
            which[d, k] = names.index(name)
            slot[d, k] = at
    return names, which, slot


def fetch(cands, which_ref, slot_ref, sources, place, buffer, sem):
    for code in cands[place]:

        @pl.when(which_ref[place] == code)
        def _(code=code):
            pltpu.make_async_copy(sources[code].at[slot_ref[place]], buffer, sem).start()


def pick_kernel(cands, which_ref, slot_ref, *refs):
    out_ref, buffers, in_sems, out_sems = refs[-4:]
    count, deep = len(cands), buffers.shape[0]

    def begin(k):
        at = k % deep
        fetch(cands, which_ref, slot_ref, refs, k, buffers.at[at], in_sems.at[at])

    def leaving(k):
        at = k % deep
        return pltpu.make_async_copy(buffers.at[at], out_ref.at[k], out_sems.at[at])

    for k in range(min(deep, count)):
        begin(k)
    for k in range(count):
        at = k % deep
        pltpu.make_async_copy(buffers.at[at], buffers.at[at], in_sems.at[at]).wait()
        leaving(k).start()
        again = k - deep // 2
        if again >= 0 and again + deep < count:
            leaving(again).wait()
            begin(again + deep)
    for k in range(max(0, count - deep), count):
        leaving(k).wait()


def project_kernel(cands, which_ref, slot_ref, rows_ref, *refs):
    out_ref, buffers, sems = refs[-3:]
    rows = buffers.shape[1]
    for k in range(len(cands)):
        fetch(cands, which_ref, slot_ref, refs, k, buffers.at[k], sems.at[k])
    for k in range(len(cands)):
        pltpu.make_async_copy(buffers.at[k], buffers.at[k], sems.at[k]).wait()
        out_ref[:, k * rows : (k + 1) * rows] = dot_nt(rows_ref[...], buffers[k]).astype(bf16)


def apply_kernel(cands, which_ref, slot_ref, rows_ref, *refs):
    out_ref, buffers, sems = refs[-3:]
    _, rows, width = buffers.shape
    for k in range(len(cands)):
        fetch(cands, which_ref, slot_ref, refs, k, buffers.at[k], sems.at[k])
    for k in range(len(cands)):
        pltpu.make_async_copy(buffers.at[k], buffers.at[k], sems.at[k]).wait()
    step = width // 3 if width % 384 == 0 else width
    for low in range(0, width, step):
        total = dot_nn(rows_ref[:, :rows], buffers[0, :, low : low + step])
        for k in range(1, len(cands)):
            total += dot_nn(
                rows_ref[:, k * rows : (k + 1) * rows], buffers[k, :, low : low + step]
            )
        out_ref[:, low : low + step] = total.astype(bf16)


def pick(places, sources, device, devices, kind="pick", rows_in=None):
    names, which, slot = chosen(places, devices)
    _, rows, width = sources["mine"].shape
    table = jnp.asarray(np.concatenate([which, slot], axis=1))[device]
    count = len(places)
    cands = [sorted(set(which[:, k].tolist())) for k in range(count)]
    kernel = {"pick": pick_kernel, "project": project_kernel, "apply": apply_kernel}[kind]
    args = [sources[name] for name in names]
    in_specs = [pl.BlockSpec(memory_space=pl.ANY)] * len(names)
    if kind == "pick":
        deep = min(count, 8)
        out_spec = pl.BlockSpec(memory_space=pl.ANY)
        out_shape = (count, rows, width)
        sems = [pltpu.SemaphoreType.DMA((deep,)), pltpu.SemaphoreType.DMA((deep,))]
    else:
        deep = count
        args = [rows_in] + args
        in_specs = [pl.BlockSpec(memory_space=pltpu.VMEM)] + in_specs
        out_spec = pl.BlockSpec(memory_space=pltpu.VMEM)
        out_shape = (rows_in.shape[0], count * rows if kind == "project" else width)
        sems = [pltpu.SemaphoreType.DMA((deep,))]
    return pl.pallas_call(
        functools.partial(kernel, cands),
        grid_spec=pltpu.PrefetchScalarGridSpec(
            num_scalar_prefetch=2,
            grid=(1,),
            in_specs=in_specs,
            out_specs=out_spec,
            scratch_shapes=[pltpu.VMEM((deep, rows, width), bf16)] + sems,
        ),
        out_shape=jax.ShapeDtypeStruct(out_shape, bf16),
        compiler_params=pltpu.CompilerParams(vmem_limit_bytes=58 * 2**20),
        name=kind,
    )(table[:count], table[count:], *args)


def routed_weights(attn_weight, column, shard, columns, shards, between):
    rows, width = attn_weight.shape
    count = rows // HD
    chips = shards // 2
    devices = columns * shards
    device = column * shards + shard
    swap = [(f, f ^ 1) for f in range(shards)]
    items = len(granules_of(0, columns))
    urgent = items - HQ // columns
    steps, urgent_steps, kv_steps = route(columns, chips, 2 * count)
    mine = attn_weight.reshape(count, HD, width)
    theirs = between("start", lax.ppermute(mine, "fsdp", swap))
    sources = {"mine": mine, "theirs": theirs}
    at = [{} for _ in range(items)]
    for c in range(columns):
        for f in range(shards):
            for k, g in enumerate(granules_of(c, columns)):
                if g // (2 * count) == f // 2:
                    at[k][c * shards + f] = ("mine" if g // count == f else "theirs", g % count)
    sends = []
    for number, moves in enumerate(steps):
        own, passed, pairs = {}, {}, []
        for (c, z, core), k in moves.items():
            here = c * shards + 2 * z + core
            to = here + (2, -2)[core]
            name, slot = at[k][here]
            if name in ("mine", "theirs"):
                own[here] = (name, slot)
            else:
                passed[here] = name
            pairs.append((here, to))
            at[k][to] = ("got%d" % number, 0)
            at[k][to ^ 1] = ("swapped%d" % number, 0)
        sends.append((own, passed, pairs))
    with_own = [n for n in range(1, len(sends)) if sends[n][0]]
    own_first = pick([sends[0][0]], sources, device, devices)
    own_later = None
    for number, (own, passed, pairs) in enumerate(sends):
        if number == 0:
            piece = own_first
        else:
            names = sorted(set(passed.values()))
            code = np.zeros((devices,), np.int32)
            for d, name in passed.items():
                code[d] = 1 + names.index(name)
            here = jnp.asarray(code)[device]
            piece = sources[names[-1]]
            for i, name in enumerate(names[:-1]):
                piece = jnp.where(here == 1 + i, sources[name], piece)
            if number in with_own:
                place = with_own.index(number)
                piece = jnp.where(here == 0, own_later[place : place + 1], piece)
        got = lax.ppermute(piece, ("seq", "fsdp"), pairs)
        if number == 0:
            own_later = pick([sends[n][0] for n in with_own], sources, device, devices)
            got, own_later = lax.optimization_barrier((got, own_later))
        if number < urgent_steps:
            got = between(number, got)
        if 0 < number < urgent_steps:
            before = "swapped%d" % (number - 1)
            got, sources[before] = lax.optimization_barrier((got, sources[before]))
        sources["got%d" % number] = got
        if number < urgent_steps:
            sources["swapped%d" % number] = lax.ppermute(got, "fsdp", swap)
        for name, wanted, count_of in (
            ("kv", (urgent - 2, urgent), kv_steps),
            ("q", (0, urgent - 2), urgent_steps),
        ):
            if number + 1 == count_of:
                ready = dict(sources)
                places = [dict(place) for place in at[slice(*wanted)]]
                between(
                    name,
                    lambda times, ready=ready, places=places: pick(
                        places, ready, device, devices, "project", times
                    ),
                )

    def first(after):
        held, after = lax.optimization_barrier((ready, after))
        return pick(at[:urgent], held, device, devices)

    held = None

    def times_rest(rows_in):
        nonlocal held
        held, rows_in = lax.optimization_barrier((sources, rows_in))
        for number in range(urgent_steps, len(steps)):
            held["swapped%d" % number] = lax.ppermute(held["got%d" % number], "fsdp", swap)
        return pick(at[urgent:], held, device, devices, "apply", rows_in)

    def others(after):
        kept, after = lax.optimization_barrier((held, after))
        return pick(at[urgent:], kept, device, devices)

    return first, times_rest, others


def column_weights(attn_weight, column, shard, columns, shards, between):
    rows, width = attn_weight.shape
    per = HQ // columns
    if rows % HD == 0 and shards == 8 and columns == 4:
        return routed_weights(attn_weight, column, shard, columns, shards, between)
    whole = lax.all_gather(attn_weight, "fsdp", axis=0, tiled=True).reshape(-1, HD, width)
    table = np.array([granules_of(c, columns) for c in range(columns)], np.int32)
    place = jnp.asarray(table)[column]
    taken = jnp.concatenate(
        [lax.dynamic_slice_in_dim(whole, place[k], 1, 0) for k in range(table.shape[1])], axis=0
    )
    for name, low, high in (("kv", per, per + 2), ("q", 0, per)):
        between(
            name,
            lambda times, low=low, high=high: dot_nt(
                times, taken[low:high].reshape(-1, width)
            ).astype(bf16),
        )
    return (
        lambda after: taken[: per + 2],
        lambda rows_in: dot_nn(rows_in, taken[per + 2 :].reshape(-1, width)).astype(bf16),
        lambda after: taken[per + 2 :],
    )


def ring_of(chips):
    return [0] + list(range(1, chips, 2)) + [z for z in range(chips - 1, 0, -1) if z % 2 == 0]


def ring_tables(shards):
    chips = shards // 2
    order = ring_of(chips)
    spot = {z: p for p, z in enumerate(order)}
    pairs = [
        (2 * z + c, 2 * order[(spot[z] + 1) % chips] + c) for z in range(chips) for c in range(2)
    ]
    behind = np.array(
        [[order[(spot[f // 2] - t) % chips] for t in range(chips + 1)] for f in range(shards)],
        np.int32,
    )
    return chips, pairs, behind


def ring_pieces(block, shard, shards, beside):
    chips, pairs, behind = ring_tables(shards)
    swap = [(f, f ^ 1) for f in range(shards)]
    source = jnp.asarray(behind)[shard]
    core = shard % 2
    pieces = []
    held = block
    for t in range(chips):
        if t:
            held = lax.ppermute(held, "fsdp", pairs)
            held = beside(t, held)
        pieces.append((held, 2 * source[t] + core))
        pieces.append((lax.ppermute(held, "fsdp", swap), 2 * source[t] + 1 - core))
    return pieces


def direct_pieces(block, shard, shards, wanted):
    chips = shards // 2
    swap = [(f, f ^ 1) for f in range(shards)]
    core = shard % 2
    come = [block] + [
        lax.ppermute(
            block,
            "fsdp",
            [
                (f, (f + 2 * hop) % shards)
                for f in range(shards)
                if (f + 2 * hop) % shards // 2 in wanted
            ],
        )
        for hop in range(1, chips)
    ]

    def finish(after):
        held, after = lax.optimization_barrier((come, after))
        pieces = []
        for hop, piece in enumerate(held):
            chip = (shard // 2 - hop) % chips
            pieces.append((piece, 2 * chip + core))
            pieces.append((lax.ppermute(piece, "fsdp", swap), 2 * chip + 1 - core))
        return pieces, after

    return finish


def weight_grad_kernel(half, place_ref, cols_ref, *refs):
    pieces = refs[: 2 * half]
    out_ref, rows_ref, turned_ref, sems = refs[2 * half :]
    lines = pieces[0].shape[0]
    for i, piece in enumerate(pieces):
        start = pl.multiple_of(place_ref[i] * lines, lines)
        pltpu.make_async_copy(
            piece, rows_ref.at[i // half, pl.ds(start, lines)], sems.at[i]
        ).start()
    limit = place_ref[2 * half]
    turned_ref[...] = cols_ref[...].T
    for i, piece in enumerate(pieces):
        pltpu.make_async_copy(piece, rows_ref.at[0, pl.ds(0, lines)], sems.at[i]).wait()
    height, width = out_ref.shape
    step = width // 3 if width % 384 == 0 else width
    block = HD if height % HD == 0 else HALF

    def chunk(n, carry):
        cut = pl.ds(pl.multiple_of(n * step, step), step)
        for low in range(0, height, block):
            which = (low >= limit).astype(jnp.int32)
            out_ref[low : low + block, cut] = dot_nn(
                turned_ref[low : low + block], rows_ref[which, :, cut]
            ).astype(bf16)
        return carry

    lax.fori_loop(0, width // step, chunk, 0)


def weight_grad(cols, limit, first, second):
    lines, width = first[0][0].shape
    half = len(first)
    place = jnp.stack(
        [where.astype(jnp.int32) for _, where in first + second] + [limit.astype(jnp.int32)]
    )
    return pl.pallas_call(
        functools.partial(weight_grad_kernel, half),
        grid_spec=pltpu.PrefetchScalarGridSpec(
            num_scalar_prefetch=1,
            grid=(1,),
            in_specs=[pl.BlockSpec(memory_space=pltpu.VMEM)]
            + [pl.BlockSpec(memory_space=pl.ANY)] * (2 * half),
            out_specs=pl.BlockSpec(memory_space=pltpu.VMEM),
            scratch_shapes=[
                pltpu.VMEM((2, half * lines, width), bf16),
                pltpu.VMEM((cols.shape[1], cols.shape[0]), bf16),
                pltpu.SemaphoreType.DMA((2 * half,)),
            ],
        ),
        out_shape=jax.ShapeDtypeStruct((cols.shape[1], width), bf16),
        compiler_params=pltpu.CompilerParams(vmem_limit_bytes=58 * 2**20),
        name="weight_grad",
    )(place, cols, *[piece for piece, _ in first + second])


def ring_scatter(parts, shard, shards):
    chips, pairs, behind = ring_tables(shards)
    swap = [(f, f ^ 1) for f in range(shards)]
    target = jnp.asarray(behind)[shard]
    core = shard % 2
    paired = parts.reshape((chips, 2) + parts.shape[1:])
    mine = lax.dynamic_index_in_dim(paired, core, 1, keepdims=False)
    other = lax.ppermute(
        lax.dynamic_index_in_dim(paired, 1 - core, 1, keepdims=False), "fsdp", swap
    )

    def local_sum(t):
        return lax.dynamic_index_in_dim(mine, target[t], 0, keepdims=False).astype(
            f32
        ) + lax.dynamic_index_in_dim(other, target[t], 0, keepdims=False).astype(f32)

    total = local_sum(1)
    for t in range(1, chips):
        total = lax.ppermute(total.astype(bf16), "fsdp", pairs).astype(f32) + local_sum(t + 1)
    return total


def partners(columns, bit):
    return [(c, c ^ bit) for c in range(columns)]


def column_scatter(parts, beside=None):
    half = parts.shape[-1] // 2
    ways = ((1, 2, slice(0, half)), (2, 1, slice(half, None)))
    come = tuple(
        lax.ppermute(
            jnp.concatenate([parts[first : first + 1, ..., cut], parts[3:, ..., cut]], axis=0),
            "seq",
            partners(4, first),
        )
        for first, _, cut in ways
    )
    if beside:
        come = beside(come)
    done = []
    for (first, second, cut), got in zip(ways, come):
        keep = parts[0, ..., cut].astype(f32) + got[0].astype(f32)
        away = parts[second, ..., cut].astype(f32) + got[1].astype(f32)
        done.append(
            keep + lax.ppermute(away.astype(bf16), "seq", partners(4, second)).astype(f32)
        )
    return jnp.concatenate(done, axis=-1)


def column_total(value, column, beside, later):
    rows, width = value.shape
    step, half = rows // 4, width // 2
    parts = jnp.stack(
        [lax.dynamic_slice_in_dim(value, (column ^ k) * step, step, 0) for k in range(4)]
    )
    own, *later = beside(column_scatter(parts, beside).astype(bf16), *later)
    pieces = (own[:, :half], own[:, half:])
    near = tuple(lax.ppermute(p, "seq", partners(4, bit)) for p, bit in zip(pieces, (1, 2)))
    near, *later = lax.optimization_barrier((near, *later))
    out = jnp.zeros((rows, width), f32)
    for first, second, low, piece, got in (
        (1, 2, 0, pieces[0], near[0]),
        (2, 1, half, pieces[1], near[1]),
    ):
        far = lax.ppermute(jnp.stack([piece, got]), "seq", partners(4, second))
        for k, block in ((0, piece), (first, got), (second, far[0]), (3, far[1])):
            out = lax.dynamic_update_slice(
                out, block.astype(f32), ((column ^ k) * step, low)
            )
    return (out, *later)


def sum_over(value, axis, count):
    bit = 1
    while bit < count:
        value = value + lax.ppermute(value, axis, [(c, c ^ bit) for c in range(count)])
        bit *= 2
    return value


def local(tokens, attn_weight, norm_gains, ffn_weight, out_grad):
    seqs, rows, width = tokens.shape
    columns = lax.axis_size("seq")
    shards = lax.axis_size("fsdp")
    column = lax.axis_index("seq")
    shard = lax.axis_index("fsdp")
    core = shard % 2
    per = HQ // columns
    own_rows = seqs * rows
    swap = [(f, f ^ 1) for f in range(shards)]
    shard_arg = shard.astype(jnp.int32).reshape(1)

    def core_half(granules):
        return lax.dynamic_index_in_dim(
            granules.reshape(-1, 2, HALF, width), core, 1, keepdims=False
        )

    def all_columns(own, other, begin, end):
        count = own.shape[1]
        sources = {
            "mine": own.reshape(columns * count, HALF, width),
            "other": other.reshape(columns * count, HALF, width),
        }
        places = [
            {
                c * shards + f: ("mine" if f % 2 == half else "other", home * count + k)
                for c in range(columns)
                for f in range(shards)
            }
            for home in range(columns)
            for k in range(begin, end)
            for half in range(2)
        ]
        device = column * shards + shard
        return pick(places, sources, device, columns * shards).reshape(-1, width)

    token_slices = lax.all_gather(tokens, "seq", axis=0)
    gain_rows = lax.all_gather(norm_gains, "fsdp", axis=1, tiled=True).astype(f32)
    normed_slices = rms_scale(
        token_slices.reshape(-1, width).astype(f32), gain_rows[0]
    ).astype(bf16)
    made = {}

    def between(step, value):
        nonlocal normed_slices, gain_rows
        if step == "start":
            value, gain_rows = lax.optimization_barrier((value, gain_rows))
            normed_slices = rms_scale(
                token_slices.reshape(-1, width).astype(f32), gain_rows[0]
            ).astype(bf16)
        if step == 1:
            value, normed_slices = lax.optimization_barrier((value, normed_slices))
        if step == 2:
            value, made["kv"] = lax.optimization_barrier((value, made["kv"]))
        if step in ("kv", "q"):
            made[step] = value(normed_slices)
        return value

    first_weights, times_out, out_weights = column_weights(
        attn_weight, column, shard, columns, shards, between
    )
    kv_all = lax.all_gather(made["kv"].reshape(columns, seqs, rows, 2 * HD), "fsdp", axis=0)
    queries = made["q"].reshape(columns, seqs, rows, per * HD)
    flat_tokens = tokens.reshape(-1, width).astype(f32)
    flat_cot = out_grad.reshape(-1, width).astype(f32)
    normed_own = rms_scale(flat_tokens, gain_rows[0]).astype(bf16)
    normed_own, kv_all = lax.optimization_barrier((normed_own, kv_all))
    mixed, lse = attend(shard_arg, queries, kv_all)
    kept = {"mixed": mixed}

    def beside(step, held):
        if step == 1:
            held, kept["mixed"] = lax.optimization_barrier((held, kept["mixed"]))
            if columns == 4:
                by_partner = jnp.concatenate(
                    [
                        lax.dynamic_slice_in_dim(kept["mixed"], column ^ k, 1, 0)
                        for k in range(columns)
                    ],
                    axis=0,
                )
                kept["part"] = times_out(by_partner.reshape(columns * own_rows, per * HD))
            else:
                kept["part"] = times_out(kept["mixed"].reshape(-1, per * HD))
        if step == 2:
            held, kept["part"] = lax.optimization_barrier((held, kept["part"]))
            if columns == 4:
                kept["out"] = column_scatter(kept["part"].reshape(columns, own_rows, width))
            else:
                kept["out"] = lax.psum_scatter(
                    kept["part"], "seq", scatter_dimension=0, tiled=True
                ).astype(f32)
        if step == 3:
            held, kept["out"] = lax.optimization_barrier((held, kept["out"]))
        return held

    normed_pieces = ring_pieces(normed_own, shard, shards, beside)
    mixed, attn_out = kept["mixed"], kept["out"]
    lanes = jnp.concatenate(
        [core_half(first_weights(mixed)), core_half(out_weights(mixed))], axis=0
    )
    attn_out, lanes = lax.optimization_barrier((attn_out, lanes))
    kept["lanes"] = lax.all_gather(lanes, "seq", axis=0)
    residual = flat_tokens + rms_scale(attn_out, gain_rows[1])
    normed_ffn = rms_scale(residual, gain_rows[2]).astype(bf16)

    chips, ring, _ = ring_tables(shards)
    weight_gate_up, weight_down = ffn_weight[:, :2], ffn_weight[:, 2]

    def pipeline(block, work, aside, late):
        held = block
        pairs = []
        for t in range(chips):
            rows_here = jnp.concatenate([held, lax.ppermute(held, "fsdp", swap)], axis=0)
            if t + 1 < chips:
                held = lax.ppermute(held, "fsdp", ring)
            made = work(t, rows_here).astype(bf16)
            got = lax.ppermute(made[own_rows:], "fsdp", swap)
            pair = made[:own_rows].astype(f32) + got.astype(f32)
            pairs.append(pair)
            if t + 1 < chips:
                held, made = aside(t, *lax.optimization_barrier((held, made)))
            if t and not late:
                total = (pair if t == 1 else total + pair).astype(bf16)
                if t + 1 < chips:
                    held, total = lax.optimization_barrier((held, total))
                total = lax.ppermute(total, "fsdp", ring).astype(f32)
        if late:
            total, _ = lax.optimization_barrier((pairs[1].astype(bf16), held))
            total = lax.ppermute(total, "fsdp", ring).astype(f32)
            for pair in pairs[2:]:
                total = lax.ppermute((total + pair).astype(bf16), "fsdp", ring).astype(f32)
        return total + pairs[0]

    saved = []

    def forward(t, rows_here):
        gate_up = jnp.einsum(
            "td,fgd->tgf", rows_here, weight_gate_up, preferred_element_type=f32
        )
        hidden = gated_units(gate_up[:, 0], gate_up[:, 1]).astype(bf16)
        saved.append((rows_here, gate_up, hidden))
        return dot_nn(hidden, weight_down)

    ffn_out = pipeline(normed_ffn, forward, lambda t, held, made: (held, made), False)
    result = residual + rms_scale(ffn_out, gain_rows[3])
    block_out = result.astype(bf16).reshape(tokens.shape)
    grad_ffn, gain_terms = norm_back(ffn_out, gain_rows[3], flat_cot)
    gain_last = jnp.sum(gain_terms, axis=0)

    back = []

    def backward(t, grads_here):
        grad_hidden = dot_nt(grads_here, weight_down)
        _, gate_up, _ = saved[t]
        unused, gated_pull = jax.vjp(gated_units, gate_up[:, 0], gate_up[:, 1])
        grad_gate, grad_up = gated_pull(grad_hidden)
        units = jnp.stack([grad_gate, grad_up], axis=1).astype(bf16)
        back.append((grads_here, units))
        return jnp.einsum("tgf,fgd->td", units, weight_gate_up, preferred_element_type=f32)

    def backward_aside(t, held, made):
        if t == chips - 2:
            held, made, kept["lanes"] = lax.optimization_barrier((held, made, kept["lanes"]))
        return held, made

    grad_normed_ffn = pipeline(grad_ffn.astype(bf16), backward, backward_aside, True)
    ffn_in = jnp.concatenate([rows_here for rows_here, _, _ in saved], axis=0)
    hidden = jnp.concatenate([units for _, _, units in saved], axis=0)
    grad_ffn_all = jnp.concatenate([grads_here for grads_here, _ in back], axis=0)
    units = jnp.concatenate([part for _, part in back], axis=0)
    gate_grad, up_grad, down_grad = lax.psum(
        (
            dot_tn(units[:, 0], ffn_in).astype(bf16),
            dot_tn(units[:, 1], ffn_in).astype(bf16),
            dot_tn(hidden, grad_ffn_all).astype(bf16),
        ),
        "seq",
    )

    other_lanes = lax.ppermute(kept["lanes"], "fsdp", swap)
    weight_out_all = all_columns(kept["lanes"], other_lanes, per + 2, 2 * per + 2)
    grad_normed_ffn, weight_out_all = lax.optimization_barrier((grad_normed_ffn, weight_out_all))

    def attention_back():
        weight_in_all = all_columns(kept["lanes"], other_lanes, 0, per + 2)
        grad_mid, gain_pre_ffn = norm_back(residual, gain_rows[2], grad_normed_ffn)
        grad_residual = flat_cot + grad_mid
        grad_attn, gain_post_attn = norm_back(attn_out, gain_rows[1], grad_residual)
        grad_attn_low = grad_attn.astype(bf16)
        grad_mixed = (
            dot_nt(grad_attn_low, weight_out_all)
            .astype(bf16)
            .reshape(seqs, rows, columns, per * HD)
        )
        both = lax.all_to_all(
            jnp.concatenate([grad_mixed.transpose(2, 0, 1, 3), mixed], axis=-1),
            "seq",
            split_axis=0,
            concat_axis=0,
            tiled=True,
        )
        grad_heads = both[..., : per * HD]
        mixed_rows = both[..., per * HD :].transpose(1, 2, 0, 3).reshape(own_rows, HQ * HD)
        shard_cols = attn_weight.shape[0]
        first_owner = (HQ + 2 * KVH) * HD // shard_cols // 2
        later_pieces = direct_pieces(
            grad_attn_low, shard, shards, range(first_owner, shards // 2)
        )
        grad_queries, grad_kv = attend_back(shard_arg, queries, grad_heads, lse, kv_all)
        grad_kv_own = (
            ring_scatter(grad_kv.reshape(shards, columns * own_rows, 2 * HD), shard, shards)
            .astype(bf16)
            .reshape(columns, seqs, rows, 2 * HD)
        )
        grad_proj = lax.all_to_all(
            jnp.concatenate([grad_queries, grad_kv_own], axis=-1),
            "seq",
            split_axis=0,
            concat_axis=0,
            tiled=True,
        )
        attn_pieces, grad_proj = later_pieces(grad_proj)
        grad_rows = grad_proj.reshape(columns, own_rows, (per + 2) * HD).transpose(1, 0, 2)
        grad_normed = dot_nn(grad_rows.reshape(own_rows, -1), weight_in_all)
        grad_tokens, gain_pre_attn = norm_back(flat_tokens, gain_rows[0], grad_normed)
        token_grad = (grad_residual + grad_tokens).reshape(tokens.shape)

        def shared(copies):
            if columns == KVH:
                return copies.reshape(own_rows, -1)
            summed = copies.reshape(own_rows, KVH, columns // KVH, HD).astype(f32).sum(axis=2)
            return summed.astype(bf16).reshape(own_rows, -1)

        weight_cols = jnp.concatenate(
            [
                grad_rows[:, :, : per * HD].reshape(own_rows, -1),
                shared(grad_rows[:, :, per * HD : (per + 1) * HD]),
                shared(grad_rows[:, :, (per + 1) * HD :]),
                mixed_rows,
            ],
            axis=1,
        )
        col_all = lax.all_to_all(
            weight_cols.reshape(own_rows, shards, shard_cols).transpose(1, 0, 2),
            "fsdp",
            split_axis=0,
            concat_axis=0,
            tiled=True,
        ).reshape(-1, shard_cols)
        limit = jnp.clip((HQ + 2 * KVH) * HD - shard * shard_cols, 0, shard_cols)
        attn_grad = weight_grad(col_all, limit, normed_pieces, attn_pieces)
        gain_grad = jnp.stack(
            [
                jnp.sum(gain_pre_attn, axis=0),
                jnp.sum(gain_post_attn, axis=0),
                jnp.sum(gain_pre_ffn, axis=0),
                gain_last,
            ]
        )
        return attn_grad, gain_grad, token_grad

    def nothing():
        return (
            jnp.zeros(attn_weight.shape, bf16),
            jnp.zeros((norm_gains.shape[0], width), f32),
            jnp.zeros(tokens.shape, f32),
        )

    attn_grad, gain_grad, token_grad = lax.cond(
        shard < 2**20, attention_back, nothing
    )
    gain_grad = lax.dynamic_slice_in_dim(
        sum_over(gain_grad, "fsdp", shards),
        shard * norm_gains.shape[1],
        norm_gains.shape[1],
        1,
    )
    if columns == 4:

        def with_gains(*come):
            nonlocal gain_grad
            if len(come) == 1:
                gain_grad = sum_over(gain_grad, "seq", columns)
                come, gain_grad = lax.optimization_barrier((come[0], gain_grad))
                return come
            return lax.optimization_barrier(come)

        attn_total, gate_grad, up_grad, down_grad = column_total(
            attn_grad, column, with_gains, (gate_grad, up_grad, down_grad)
        )
    else:
        attn_grad, gate_grad, up_grad, down_grad = lax.optimization_barrier(
            (attn_grad, gate_grad, up_grad, down_grad)
        )
        attn_total = lax.psum(attn_grad, "seq").astype(f32)
        gain_grad = sum_over(gain_grad, "seq", columns)
    gain_total = gain_grad
    ffn_grad = widen_plane(down_grad, 2, 3, None)
    ffn_grad = widen_plane(gate_grad, 0, 3, ffn_grad)
    ffn_grad = widen_plane(up_grad, 1, 3, ffn_grad)
    ffn_grad = ffn_grad.transpose(1, 0, 2)
    return (block_out, token_grad, attn_total, gain_total, ffn_grad)


def solution(mesh):
    in_specs = (
        P(None, ("seq", "fsdp"), None),
        P("fsdp", None),
        P(None, "fsdp"),
        P("fsdp", None, None),
        P(None, ("seq", "fsdp"), None),
    )
    out_specs = (
        P(None, ("seq", "fsdp"), None),
        P(None, ("seq", "fsdp"), None),
        P("fsdp", None),
        P(None, "fsdp"),
        P("fsdp", None, None),
    )
    return jax.shard_map(local, mesh=mesh, in_specs=in_specs, out_specs=out_specs, check_vma=False)
```

```python
import functools

import jax
import jax.numpy as jnp
import numpy as np
from jax import lax
from jax.experimental import pallas as pl
from jax.experimental.pallas import tpu as pltpu
from jax.sharding import PartitionSpec as P

HQ = 8
KVH = 4
HD = 256
GROUP = HQ // KVH
HALF = HD // 2

soft_cap = 50.0
norm_eps = 1e-06
bf16 = jnp.bfloat16
f32 = jnp.float32


def rms_scale(values, gain_row):
    return (
        values * lax.rsqrt(jnp.mean(values * values, axis=-1, keepdims=True) + norm_eps) * gain_row
    )


def norm_back(values, gain_row, cotangent):
    inverse = lax.rsqrt(jnp.mean(values * values, axis=-1, keepdims=True) + norm_eps)
    unit_rows = values * inverse
    scaled = cotangent * gain_row
    grad_values = inverse * (
        scaled - unit_rows * jnp.mean(scaled * unit_rows, axis=-1, keepdims=True)
    )
    return (grad_values, cotangent * unit_rows)


def gated_units(gate_proj, up_proj):
    return jax.nn.gelu(gate_proj, approximate=True) * up_proj


def dot_nt(a, b):
    return lax.dot_general(a, b, (((1,), (1,)), ((), ())), preferred_element_type=f32)


def dot_nn(a, b):
    return lax.dot_general(a, b, (((1,), (0,)), ((), ())), preferred_element_type=f32)


def dot_tn(a, b):
    return lax.dot_general(a, b, (((0,), (0,)), ((), ())), preferred_element_type=f32)


def stacked_heads(block):
    heads = block.shape[1] // HD
    return jnp.concatenate([block[:, h * HD : (h + 1) * HD] for h in range(heads)], axis=0)


def visible_of(shard, rows, keys, lines):
    shape = (lines, keys)
    row = lax.broadcasted_iota(jnp.int32, shape, 0) & (rows - 1)
    col = lax.broadcasted_iota(jnp.int32, shape, 1)
    return col <= shard * rows + row


def lane_sums(values):
    return sum(values[:, low : low + 128] for low in range(0, values.shape[1], 128))


def attend_kernel(shard_ref, q_ref, kv_ref, o_ref, lse_ref, weight_ref):
    own = pl.program_id(1)
    shard = shard_ref[0]
    parts, _, _, rows, _ = kv_ref.shape
    keys = parts * rows
    queries = stacked_heads(q_ref[0, 0])
    lines = queries.shape[0]

    def exponentials(block):
        key_block = kv_ref[:, block, 0, :, :HD].reshape(keys, HD)
        bounded = jnp.tanh(dot_nt(queries, key_block) * (HD ** (-0.5) / soft_cap))
        return jnp.exp(soft_cap * bounded)

    def score_step(block, total):
        expanded = exponentials(block)
        weight_ref[block] = expanded
        return total + lane_sums(expanded)

    total = lax.fori_loop(0, own, score_step, jnp.zeros((lines, 128), f32))
    expanded = jnp.where(visible_of(shard, rows, keys, lines), exponentials(own), 0.0)
    weight_ref[own] = expanded
    total = jnp.sum(total + lane_sums(expanded), axis=-1, keepdims=True)
    inverse = 1.0 / total

    def mix_step(block, mixed):
        weights = (weight_ref[block] * inverse).astype(bf16)
        value_block = kv_ref[:, block, 0, :, HD:].reshape(keys, HD)
        return mixed + dot_nn(weights, value_block)

    mixed = lax.fori_loop(0, own + 1, mix_step, jnp.zeros((lines, HD), f32))
    for h in range(lines // rows):
        o_ref[0, 0, :, h * HD : (h + 1) * HD] = mixed[h * rows : (h + 1) * rows].astype(bf16)
    lse_ref[0, 0] = jnp.broadcast_to(jnp.log(total), (lines, 128))


def attend_back_kernel(
    shard_ref, q_ref, do_ref, lse_ref, kv_ref, dq_ref, dkv_ref, weight_ref, dp_ref, acc_ref
):
    own = pl.program_id(1)
    shard = shard_ref[0]
    parts, blocks, _, rows, _ = kv_ref.shape
    keys = parts * rows
    queries = stacked_heads(q_ref[0, 0])
    grads = stacked_heads(do_ref[0, 0])
    lse = lse_ref[0, 0][:, :1]
    lines = queries.shape[0]

    @pl.when(own == 0)
    def _():
        acc_ref[...] = jnp.zeros_like(acc_ref)

    def first_part(block, masked):
        key_block = kv_ref[:, block, 0, :, :HD].reshape(keys, HD)
        value_block = kv_ref[:, block, 0, :, HD:].reshape(keys, HD)
        bounded = jnp.tanh(dot_nt(queries, key_block) * (HD ** (-0.5) / soft_cap))
        weights = jnp.exp(soft_cap * bounded - lse)
        if masked:
            weights = jnp.where(visible_of(shard, rows, keys, lines), weights, 0.0)
        grad_weights = dot_nt(grads, value_block)
        acc_ref[block, :, HD:] += dot_tn(weights.astype(bf16), grads)
        weight_ref[block] = weights * (1.0 - bounded * bounded)
        dp_ref[block] = grad_weights
        return lane_sums(weights * grad_weights)

    delta = lax.fori_loop(
        0,
        own,
        lambda block, delta: delta + first_part(block, False),
        jnp.zeros((lines, 128), f32),
    )
    delta = jnp.sum(delta + first_part(own, True), axis=-1, keepdims=True)

    def second_step(block, grad_query):
        key_block = kv_ref[:, block, 0, :, :HD].reshape(keys, HD)
        grad_raw = (weight_ref[block] * (dp_ref[block] - delta)).astype(bf16)
        acc_ref[block, :, :HD] += dot_tn(grad_raw, queries)
        return grad_query + dot_nn(grad_raw, key_block)

    grad_query = lax.fori_loop(0, own + 1, second_step, jnp.zeros((lines, HD), f32)) * HD ** (-0.5)
    for h in range(lines // rows):
        dq_ref[0, 0, :, h * HD : (h + 1) * HD] = grad_query[h * rows : (h + 1) * rows].astype(bf16)

    @pl.when(own == blocks - 1)
    def _():
        for block in range(blocks):
            dkv_ref[:, block, 0, :, :HD] = (
                (acc_ref[block, :, :HD] * HD ** (-0.5)).astype(bf16).reshape(parts, rows, HD)
            )
            dkv_ref[:, block, 0, :, HD:] = (
                acc_ref[block, :, HD:].astype(bf16).reshape(parts, rows, HD)
            )


def attend(shard, queries, kv_all):
    blocks, seqs, rows, width = queries.shape
    lines = rows * width // HD
    parts = kv_all.shape[0]
    keys = parts * rows
    row_spec = pl.BlockSpec((1, 1, rows, width), lambda n, s, shard: (s, n, 0, 0))
    lse_spec = pl.BlockSpec((1, 1, lines, 128), lambda n, s, shard: (s, n, 0, 0))
    kv_spec = pl.BlockSpec((parts, blocks, 1, rows, 2 * HD), lambda n, s, shard: (0, 0, n, 0, 0))
    return pl.pallas_call(
        attend_kernel,
        grid_spec=pltpu.PrefetchScalarGridSpec(
            num_scalar_prefetch=1,
            grid=(seqs, blocks),
            in_specs=[row_spec, kv_spec],
            out_specs=[row_spec, lse_spec],
            scratch_shapes=[pltpu.VMEM((blocks, lines, keys), f32)],
        ),
        out_shape=[
            jax.ShapeDtypeStruct(queries.shape, bf16),
            jax.ShapeDtypeStruct((blocks, seqs, lines, 128), f32),
        ],
        compiler_params=pltpu.CompilerParams(vmem_limit_bytes=48 * 2**20),
        name="attend",
    )(shard, queries, kv_all)


def attend_back(shard, queries, grads, lse, kv_all):
    blocks, seqs, rows, width = queries.shape
    lines = rows * width // HD
    parts = kv_all.shape[0]
    keys = parts * rows
    row_spec = pl.BlockSpec((1, 1, rows, width), lambda n, s, shard: (s, n, 0, 0))
    lse_spec = pl.BlockSpec((1, 1, lines, 128), lambda n, s, shard: (s, n, 0, 0))
    deep = 2 if keys * blocks <= 4096 else 1
    kv_spec = pl.BlockSpec(
        (parts, blocks, 1, rows, 2 * HD),
        lambda n, s, shard: (0, 0, n, 0, 0),
        pipeline_mode=pl.Buffered(deep),
    )
    return pl.pallas_call(
        attend_back_kernel,
        grid_spec=pltpu.PrefetchScalarGridSpec(
            num_scalar_prefetch=1,
            grid=(seqs, blocks),
            in_specs=[row_spec, row_spec, lse_spec, kv_spec],
            out_specs=[row_spec, kv_spec],
            scratch_shapes=[
                pltpu.VMEM((blocks, lines, keys), f32),
                pltpu.VMEM((blocks, lines, keys), f32),
                pltpu.VMEM((blocks, keys, 2 * HD), f32),
            ],
        ),
        out_shape=[
            jax.ShapeDtypeStruct(queries.shape, bf16),
            jax.ShapeDtypeStruct(kv_all.shape, bf16),
        ],
        compiler_params=pltpu.CompilerParams(vmem_limit_bytes=56 * 2**20),
        name="attend_back",
    )(shard, queries, grads, lse, kv_all)


def widen_kernel(*refs):
    refs[-1][0] = refs[0][...].astype(f32)


def widen_plane(plane, index, planes, whole):
    rows, width = plane.shape
    step = rows // 4 if rows % 64 == 0 else rows
    specs = [pl.BlockSpec((step, width), lambda i: (i, 0))]
    args = [plane]
    aliases = {}
    if whole is not None:
        specs.append(pl.BlockSpec(memory_space=pl.ANY))
        args.append(whole)
        aliases = {1: 0}
    return pl.pallas_call(
        widen_kernel,
        grid=(rows // step,),
        in_specs=specs,
        out_specs=pl.BlockSpec((1, step, width), lambda i: (index, i, 0)),
        out_shape=jax.ShapeDtypeStruct((planes, rows, width), f32),
        input_output_aliases=aliases,
        compiler_params=pltpu.CompilerParams(vmem_limit_bytes=40 * 2**20),
        name="widen",
    )(*args)


def granules_of(column, columns):
    per = HQ // columns
    first = column * per
    return (
        [first + i for i in range(per)]
        + [HQ + first // GROUP, HQ + KVH + first // GROUP]
        + [HQ + 2 * KVH + first + i for i in range(per)]
    )


def route(columns, chips, per_chip):
    items = len(granules_of(0, columns))
    urgent = items - HQ // columns
    rank = [1] * (urgent - 2) + [0] * 2 + [2] * (items - urgent)
    source = [[g // per_chip for g in granules_of(c, columns)] for c in range(columns)]
    held = [[{k for k in range(items) if source[c][k] == z} for z in range(chips)] for c in range(columns)]
    steps = []
    urgent_steps = kv_steps = None
    while any(len(held[c][z]) < items for c in range(columns) for z in range(chips)):
        moves = {}
        for c in range(columns):
            for z in range(chips):
                for core, way in ((0, 1), (1, -1)):
                    if not 0 <= z + way < chips:
                        continue
                    ready = [
                        k
                        for k in held[c][z]
                        if k not in held[c][z + way] and (source[c][k] - z) * way <= 0
                    ]
                    if ready:
                        moves[c, z, core] = min(
                            ready, key=lambda k: (rank[k], abs(source[c][k] - z), k)
                        )
        for (c, z, core), k in moves.items():
            held[c][z + (1, -1)[core]].add(k)
        steps.append(moves)
        done = all(k in held[c][z] for c in range(columns) for z in range(chips) for k in range(urgent))
        if done and urgent_steps is None:
            urgent_steps = len(steps)
        done = all(
            k in held[c][z]
            for c in range(columns)
            for z in range(chips)
            for k in (urgent - 2, urgent - 1)
        )
        if done and kv_steps is None:
            kv_steps = len(steps)
    return steps, urgent_steps, kv_steps


def chosen(places, devices):
    names = []
    which = np.zeros((devices, len(places)), np.int32)
    slot = np.zeros((devices, len(places)), np.int32)
    for k, place in enumerate(places):
        for d in range(devices):
            name, at = place.get(d, ("mine", 0))
            if name not in names:
                names.append(name)
            which[d, k] = names.index(name)
            slot[d, k] = at
    return names, which, slot


def fetch(cands, which_ref, slot_ref, sources, place, buffer, sem):
    for code in cands[place]:

        @pl.when(which_ref[place] == code)
        def _(code=code):
            pltpu.make_async_copy(sources[code].at[slot_ref[place]], buffer, sem).start()


def pick_kernel(cands, which_ref, slot_ref, *refs):
    out_ref, buffers, in_sems, out_sems = refs[-4:]
    count, deep = len(cands), buffers.shape[0]

    def begin(k):
        at = k % deep
        fetch(cands, which_ref, slot_ref, refs, k, buffers.at[at], in_sems.at[at])

    def leaving(k):
        at = k % deep
        return pltpu.make_async_copy(buffers.at[at], out_ref.at[k], out_sems.at[at])

    for k in range(min(deep, count)):
        begin(k)
    for k in range(count):
        at = k % deep
        pltpu.make_async_copy(buffers.at[at], buffers.at[at], in_sems.at[at]).wait()
        leaving(k).start()
        again = k - deep // 2
        if again >= 0 and again + deep < count:
            leaving(again).wait()
            begin(again + deep)
    for k in range(max(0, count - deep), count):
        leaving(k).wait()


def project_kernel(cands, which_ref, slot_ref, rows_ref, *refs):
    out_ref, buffers, sems = refs[-3:]
    rows = buffers.shape[1]
    for k in range(len(cands)):
        fetch(cands, which_ref, slot_ref, refs, k, buffers.at[k], sems.at[k])
    for k in range(len(cands)):
        pltpu.make_async_copy(buffers.at[k], buffers.at[k], sems.at[k]).wait()
        out_ref[:, k * rows : (k + 1) * rows] = dot_nt(rows_ref[...], buffers[k]).astype(bf16)


def apply_kernel(cands, which_ref, slot_ref, rows_ref, *refs):
    out_ref, buffers, sems = refs[-3:]
    _, rows, width = buffers.shape
    for k in range(len(cands)):
        fetch(cands, which_ref, slot_ref, refs, k, buffers.at[k], sems.at[k])
    for k in range(len(cands)):
        pltpu.make_async_copy(buffers.at[k], buffers.at[k], sems.at[k]).wait()
    step = width // 3 if width % 384 == 0 else width
    for low in range(0, width, step):
        total = dot_nn(rows_ref[:, :rows], buffers[0, :, low : low + step])
        for k in range(1, len(cands)):
            total += dot_nn(
                rows_ref[:, k * rows : (k + 1) * rows], buffers[k, :, low : low + step]
            )
        out_ref[:, low : low + step] = total.astype(bf16)


def pick(places, sources, device, devices, kind="pick", rows_in=None):
    names, which, slot = chosen(places, devices)
    _, rows, width = sources["mine"].shape
    table = jnp.asarray(np.concatenate([which, slot], axis=1))[device]
    count = len(places)
    cands = [sorted(set(which[:, k].tolist())) for k in range(count)]
    kernel = {"pick": pick_kernel, "project": project_kernel, "apply": apply_kernel}[kind]
    args = [sources[name] for name in names]
    in_specs = [pl.BlockSpec(memory_space=pl.ANY)] * len(names)
    if kind == "pick":
        deep = min(count, 8)
        out_spec = pl.BlockSpec(memory_space=pl.ANY)
        out_shape = (count, rows, width)
        sems = [pltpu.SemaphoreType.DMA((deep,)), pltpu.SemaphoreType.DMA((deep,))]
    else:
        deep = count
        args = [rows_in] + args
        in_specs = [pl.BlockSpec(memory_space=pltpu.VMEM)] + in_specs
        out_spec = pl.BlockSpec(memory_space=pltpu.VMEM)
        out_shape = (rows_in.shape[0], count * rows if kind == "project" else width)
        sems = [pltpu.SemaphoreType.DMA((deep,))]
    return pl.pallas_call(
        functools.partial(kernel, cands),
        grid_spec=pltpu.PrefetchScalarGridSpec(
            num_scalar_prefetch=2,
            grid=(1,),
            in_specs=in_specs,
            out_specs=out_spec,
            scratch_shapes=[pltpu.VMEM((deep, rows, width), bf16)] + sems,
        ),
        out_shape=jax.ShapeDtypeStruct(out_shape, bf16),
        compiler_params=pltpu.CompilerParams(vmem_limit_bytes=58 * 2**20),
        name=kind,
    )(table[:count], table[count:], *args)


def routed_weights(attn_weight, column, shard, columns, shards, between):
    rows, width = attn_weight.shape
    count = rows // HD
    chips = shards // 2
    devices = columns * shards
    device = column * shards + shard
    swap = [(f, f ^ 1) for f in range(shards)]
    items = len(granules_of(0, columns))
    urgent = items - HQ // columns
    steps, urgent_steps, kv_steps = route(columns, chips, 2 * count)
    mine = attn_weight.reshape(count, HD, width)
    theirs = between("start", lax.ppermute(mine, "fsdp", swap))
    sources = {"mine": mine, "theirs": theirs}
    at = [{} for _ in range(items)]
    for c in range(columns):
        for f in range(shards):
            for k, g in enumerate(granules_of(c, columns)):
                if g // (2 * count) == f // 2:
                    at[k][c * shards + f] = ("mine" if g // count == f else "theirs", g % count)
    sends = []
    for number, moves in enumerate(steps):
        own, passed, pairs = {}, {}, []
        for (c, z, core), k in moves.items():
            here = c * shards + 2 * z + core
            to = here + (2, -2)[core]
            name, slot = at[k][here]
            if name in ("mine", "theirs"):
                own[here] = (name, slot)
            else:
                passed[here] = name
            pairs.append((here, to))
            at[k][to] = ("got%d" % number, 0)
            at[k][to ^ 1] = ("swapped%d" % number, 0)
        sends.append((own, passed, pairs))
    with_own = [n for n in range(1, len(sends)) if sends[n][0]]
    own_first = pick([sends[0][0]], sources, device, devices)
    own_later = None
    for number, (own, passed, pairs) in enumerate(sends):
        if number == 0:
            piece = own_first
        else:
            names = sorted(set(passed.values()))
            code = np.zeros((devices,), np.int32)
            for d, name in passed.items():
                code[d] = 1 + names.index(name)
            here = jnp.asarray(code)[device]
            piece = sources[names[-1]]
            for i, name in enumerate(names[:-1]):
                piece = jnp.where(here == 1 + i, sources[name], piece)
            if number in with_own:
                place = with_own.index(number)
                piece = jnp.where(here == 0, own_later[place : place + 1], piece)
        got = lax.ppermute(piece, ("seq", "fsdp"), pairs)
        if number == 0:
            own_later = pick([sends[n][0] for n in with_own], sources, device, devices)
            got, own_later = lax.optimization_barrier((got, own_later))
        if number < urgent_steps:
            got = between(number, got)
        if 0 < number < urgent_steps:
            before = "swapped%d" % (number - 1)
            got, sources[before] = lax.optimization_barrier((got, sources[before]))
        sources["got%d" % number] = got
        if number < urgent_steps:
            sources["swapped%d" % number] = lax.ppermute(got, "fsdp", swap)
        for name, wanted, count_of in (
            ("kv", (urgent - 2, urgent), kv_steps),
            ("q", (0, urgent - 2), urgent_steps),
        ):
            if number + 1 == count_of:
                ready = dict(sources)
                places = [dict(place) for place in at[slice(*wanted)]]
                between(
                    name,
                    lambda times, ready=ready, places=places: pick(
                        places, ready, device, devices, "project", times
                    ),
                )

    def first(after):
        held, after = lax.optimization_barrier((ready, after))
        return pick(at[:urgent], held, device, devices)

    held = None

    def times_rest(rows_in):
        nonlocal held
        held, rows_in = lax.optimization_barrier((sources, rows_in))
        for number in range(urgent_steps, len(steps)):
            held["swapped%d" % number] = lax.ppermute(held["got%d" % number], "fsdp", swap)
        return pick(at[urgent:], held, device, devices, "apply", rows_in)

    def others(after):
        kept, after = lax.optimization_barrier((held, after))
        return pick(at[urgent:], kept, device, devices)

    return first, times_rest, others


def column_weights(attn_weight, column, shard, columns, shards, between):
    rows, width = attn_weight.shape
    per = HQ // columns
    if rows % HD == 0 and shards == 8 and columns == 4:
        return routed_weights(attn_weight, column, shard, columns, shards, between)
    whole = lax.all_gather(attn_weight, "fsdp", axis=0, tiled=True).reshape(-1, HD, width)
    table = np.array([granules_of(c, columns) for c in range(columns)], np.int32)
    place = jnp.asarray(table)[column]
    taken = jnp.concatenate(
        [lax.dynamic_slice_in_dim(whole, place[k], 1, 0) for k in range(table.shape[1])], axis=0
    )
    for name, low, high in (("kv", per, per + 2), ("q", 0, per)):
        between(
            name,
            lambda times, low=low, high=high: dot_nt(
                times, taken[low:high].reshape(-1, width)
            ).astype(bf16),
        )
    return (
        lambda after: taken[: per + 2],
        lambda rows_in: dot_nn(rows_in, taken[per + 2 :].reshape(-1, width)).astype(bf16),
        lambda after: taken[per + 2 :],
    )


def ring_of(chips):
    return [0] + list(range(1, chips, 2)) + [z for z in range(chips - 1, 0, -1) if z % 2 == 0]


def ring_tables(shards):
    chips = shards // 2
    order = ring_of(chips)
    spot = {z: p for p, z in enumerate(order)}
    pairs = [
        (2 * z + c, 2 * order[(spot[z] + 1) % chips] + c) for z in range(chips) for c in range(2)
    ]
    behind = np.array(
        [[order[(spot[f // 2] - t) % chips] for t in range(chips + 1)] for f in range(shards)],
        np.int32,
    )
    return chips, pairs, behind


def ring_pieces(block, shard, shards, beside):
    chips, pairs, behind = ring_tables(shards)
    swap = [(f, f ^ 1) for f in range(shards)]
    source = jnp.asarray(behind)[shard]
    core = shard % 2
    pieces = []
    held = block
    for t in range(chips):
        if t:
            held = lax.ppermute(held, "fsdp", pairs)
            held = beside(t, held)
        pieces.append((held, 2 * source[t] + core))
        pieces.append((lax.ppermute(held, "fsdp", swap), 2 * source[t] + 1 - core))
    return pieces


def direct_pieces(block, shard, shards, wanted):
    chips = shards // 2
    swap = [(f, f ^ 1) for f in range(shards)]
    core = shard % 2
    come = [block] + [
        lax.ppermute(
            block,
            "fsdp",
            [
                (f, (f + 2 * hop) % shards)
                for f in range(shards)
                if (f + 2 * hop) % shards // 2 in wanted
            ],
        )
        for hop in range(1, chips)
    ]

    def finish(after):
        held, after = lax.optimization_barrier((come, after))
        pieces = []
        for hop, piece in enumerate(held):
            chip = (shard // 2 - hop) % chips
            pieces.append((piece, 2 * chip + core))
            pieces.append((lax.ppermute(piece, "fsdp", swap), 2 * chip + 1 - core))
        return pieces, after

    return finish


def weight_grad_kernel(half, place_ref, cols_ref, *refs):
    pieces = refs[: 2 * half]
    out_ref, rows_ref, turned_ref, sems = refs[2 * half :]
    lines = pieces[0].shape[0]
    for i, piece in enumerate(pieces):
        start = pl.multiple_of(place_ref[i] * lines, lines)
        pltpu.make_async_copy(
            piece, rows_ref.at[i // half, pl.ds(start, lines)], sems.at[i]
        ).start()
    limit = place_ref[2 * half]
    turned_ref[...] = cols_ref[...].T
    for i, piece in enumerate(pieces):
        pltpu.make_async_copy(piece, rows_ref.at[0, pl.ds(0, lines)], sems.at[i]).wait()
    height, width = out_ref.shape
    step = width // 3 if width % 384 == 0 else width
    block = HD if height % HD == 0 else HALF

    def chunk(n, carry):
        cut = pl.ds(pl.multiple_of(n * step, step), step)
        for low in range(0, height, block):
            which = (low >= limit).astype(jnp.int32)
            out_ref[low : low + block, cut] = dot_nn(
                turned_ref[low : low + block], rows_ref[which, :, cut]
            ).astype(bf16)
        return carry

    lax.fori_loop(0, width // step, chunk, 0)


def weight_grad(cols, limit, first, second):
    lines, width = first[0][0].shape
    half = len(first)
    place = jnp.stack(
        [where.astype(jnp.int32) for _, where in first + second] + [limit.astype(jnp.int32)]
    )
    return pl.pallas_call(
        functools.partial(weight_grad_kernel, half),
        grid_spec=pltpu.PrefetchScalarGridSpec(
            num_scalar_prefetch=1,
            grid=(1,),
            in_specs=[pl.BlockSpec(memory_space=pltpu.VMEM)]
            + [pl.BlockSpec(memory_space=pl.ANY)] * (2 * half),
            out_specs=pl.BlockSpec(memory_space=pltpu.VMEM),
            scratch_shapes=[
                pltpu.VMEM((2, half * lines, width), bf16),
                pltpu.VMEM((cols.shape[1], cols.shape[0]), bf16),
                pltpu.SemaphoreType.DMA((2 * half,)),
            ],
        ),
        out_shape=jax.ShapeDtypeStruct((cols.shape[1], width), bf16),
        compiler_params=pltpu.CompilerParams(vmem_limit_bytes=58 * 2**20),
        name="weight_grad",
    )(place, cols, *[piece for piece, _ in first + second])


def ring_scatter(parts, shard, shards):
    chips, pairs, behind = ring_tables(shards)
    swap = [(f, f ^ 1) for f in range(shards)]
    target = jnp.asarray(behind)[shard]
    core = shard % 2
    paired = parts.reshape((chips, 2) + parts.shape[1:])
    mine = lax.dynamic_index_in_dim(paired, core, 1, keepdims=False)
    other = lax.ppermute(
        lax.dynamic_index_in_dim(paired, 1 - core, 1, keepdims=False), "fsdp", swap
    )

    def local_sum(t):
        return lax.dynamic_index_in_dim(mine, target[t], 0, keepdims=False).astype(
            f32
        ) + lax.dynamic_index_in_dim(other, target[t], 0, keepdims=False).astype(f32)

    total = local_sum(1)
    for t in range(1, chips):
        total = lax.ppermute(total.astype(bf16), "fsdp", pairs).astype(f32) + local_sum(t + 1)
    return total


def partners(columns, bit):
    return [(c, c ^ bit) for c in range(columns)]


def column_scatter(parts, beside=None):
    half = parts.shape[-1] // 2
    ways = ((1, 2, slice(0, half)), (2, 1, slice(half, None)))
    come = tuple(
        lax.ppermute(
            jnp.concatenate([parts[first : first + 1, ..., cut], parts[3:, ..., cut]], axis=0),
            "seq",
            partners(4, first),
        )
        for first, _, cut in ways
    )
    if beside:
        come = beside(come)
    done = []
    for (first, second, cut), got in zip(ways, come):
        keep = parts[0, ..., cut].astype(f32) + got[0].astype(f32)
        away = parts[second, ..., cut].astype(f32) + got[1].astype(f32)
        done.append(
            keep + lax.ppermute(away.astype(bf16), "seq", partners(4, second)).astype(f32)
        )
    return jnp.concatenate(done, axis=-1)


def column_total(value, column, beside, later):
    rows, width = value.shape
    step, half = rows // 4, width // 2
    parts = jnp.stack(
        [lax.dynamic_slice_in_dim(value, (column ^ k) * step, step, 0) for k in range(4)]
    )
    own, *later = beside(column_scatter(parts, beside).astype(bf16), *later)
    pieces = (own[:, :half], own[:, half:])
    near = tuple(lax.ppermute(p, "seq", partners(4, bit)) for p, bit in zip(pieces, (1, 2)))
    near, *later = lax.optimization_barrier((near, *later))
    out = jnp.zeros((rows, width), f32)
    for first, second, low, piece, got in (
        (1, 2, 0, pieces[0], near[0]),
        (2, 1, half, pieces[1], near[1]),
    ):
        far = lax.ppermute(jnp.stack([piece, got]), "seq", partners(4, second))
        for k, block in ((0, piece), (first, got), (second, far[0]), (3, far[1])):
            out = lax.dynamic_update_slice(
                out, block.astype(f32), ((column ^ k) * step, low)
            )
    return (out, *later)


def sum_over(value, axis, count):
    bit = 1
    while bit < count:
        value = value + lax.ppermute(value, axis, [(c, c ^ bit) for c in range(count)])
        bit *= 2
    return value


def local(tokens, attn_weight, norm_gains, ffn_weight, out_grad):
    seqs, rows, width = tokens.shape
    columns = lax.axis_size("seq")
    shards = lax.axis_size("fsdp")
    column = lax.axis_index("seq")
    shard = lax.axis_index("fsdp")
    core = shard % 2
    per = HQ // columns
    own_rows = seqs * rows
    swap = [(f, f ^ 1) for f in range(shards)]
    shard_arg = shard.astype(jnp.int32).reshape(1)

    def core_half(granules):
        return lax.dynamic_index_in_dim(
            granules.reshape(-1, 2, HALF, width), core, 1, keepdims=False
        )

    def all_columns(own, other, begin, end):
        count = own.shape[1]
        sources = {
            "mine": own.reshape(columns * count, HALF, width),
            "other": other.reshape(columns * count, HALF, width),
        }
        places = [
            {
                c * shards + f: ("mine" if f % 2 == half else "other", home * count + k)
                for c in range(columns)
                for f in range(shards)
            }
            for home in range(columns)
            for k in range(begin, end)
            for half in range(2)
        ]
        device = column * shards + shard
        return pick(places, sources, device, columns * shards).reshape(-1, width)

    token_slices = lax.all_gather(tokens, "seq", axis=0)
    gain_rows = lax.all_gather(norm_gains, "fsdp", axis=1, tiled=True).astype(f32)
    normed_slices = rms_scale(
        token_slices.reshape(-1, width).astype(f32), gain_rows[0]
    ).astype(bf16)
    made = {}

    def between(step, value):
        nonlocal normed_slices, gain_rows
        if step == "start":
            value, gain_rows = lax.optimization_barrier((value, gain_rows))
            normed_slices = rms_scale(
                token_slices.reshape(-1, width).astype(f32), gain_rows[0]
            ).astype(bf16)
        if step == 1:
            value, normed_slices = lax.optimization_barrier((value, normed_slices))
        if step == 2:
            value, made["kv"] = lax.optimization_barrier((value, made["kv"]))
        if step in ("kv", "q"):
            made[step] = value(normed_slices)
        return value

    first_weights, times_out, out_weights = column_weights(
        attn_weight, column, shard, columns, shards, between
    )
    kv_all = lax.all_gather(made["kv"].reshape(columns, seqs, rows, 2 * HD), "fsdp", axis=0)
    queries = made["q"].reshape(columns, seqs, rows, per * HD)
    flat_tokens = tokens.reshape(-1, width).astype(f32)
    flat_cot = out_grad.reshape(-1, width).astype(f32)
    normed_own = rms_scale(flat_tokens, gain_rows[0]).astype(bf16)
    normed_own, kv_all = lax.optimization_barrier((normed_own, kv_all))
    mixed, lse = attend(shard_arg, queries, kv_all)
    kept = {"mixed": mixed}

    def beside(step, held):
        if step == 1:
            held, kept["mixed"] = lax.optimization_barrier((held, kept["mixed"]))
            if columns == 4:
                by_partner = jnp.concatenate(
                    [
                        lax.dynamic_slice_in_dim(kept["mixed"], column ^ k, 1, 0)
                        for k in range(columns)
                    ],
                    axis=0,
                )
                kept["part"] = times_out(by_partner.reshape(columns * own_rows, per * HD))
            else:
                kept["part"] = times_out(kept["mixed"].reshape(-1, per * HD))
        if step == 2:
            held, kept["part"] = lax.optimization_barrier((held, kept["part"]))
            if columns == 4:
                kept["out"] = column_scatter(kept["part"].reshape(columns, own_rows, width))
            else:
                kept["out"] = lax.psum_scatter(
                    kept["part"], "seq", scatter_dimension=0, tiled=True
                ).astype(f32)
        if step == 3:
            held, kept["out"] = lax.optimization_barrier((held, kept["out"]))
        return held

    normed_pieces = ring_pieces(normed_own, shard, shards, beside)
    mixed, attn_out = kept["mixed"], kept["out"]
    lanes = jnp.concatenate(
        [core_half(first_weights(mixed)), core_half(out_weights(mixed))], axis=0
    )
    attn_out, lanes = lax.optimization_barrier((attn_out, lanes))
    kept["lanes"] = lax.all_gather(lanes, "seq", axis=0)
    residual = flat_tokens + rms_scale(attn_out, gain_rows[1])
    normed_ffn = rms_scale(residual, gain_rows[2]).astype(bf16)

    chips, ring, _ = ring_tables(shards)
    weight_gate_up, weight_down = ffn_weight[:, :2], ffn_weight[:, 2]

    def pipeline(block, work, aside, late):
        held = block
        pairs = []
        for t in range(chips):
            rows_here = jnp.concatenate([held, lax.ppermute(held, "fsdp", swap)], axis=0)
            if t + 1 < chips:
                held = lax.ppermute(held, "fsdp", ring)
            made = work(t, rows_here).astype(bf16)
            got = lax.ppermute(made[own_rows:], "fsdp", swap)
            pair = made[:own_rows].astype(f32) + got.astype(f32)
            pairs.append(pair)
            if t + 1 < chips:
                held, made = aside(t, *lax.optimization_barrier((held, made)))
            if t and not late:
                total = (pair if t == 1 else total + pair).astype(bf16)
                if t + 1 < chips:
                    held, total = lax.optimization_barrier((held, total))
                total = lax.ppermute(total, "fsdp", ring).astype(f32)
        if late:
            total, _ = lax.optimization_barrier((pairs[1].astype(bf16), held))
            total = lax.ppermute(total, "fsdp", ring).astype(f32)
            for pair in pairs[2:]:
                total = (total + pair).astype(bf16)
                total, pairs[-1] = lax.optimization_barrier((total, pairs[-1]))
                total = lax.ppermute(total, "fsdp", ring).astype(f32)
        return total + pairs[0]

    saved = []

    def forward(t, rows_here):
        gate_up = jnp.einsum(
            "td,fgd->tgf", rows_here, weight_gate_up, preferred_element_type=f32
        )
        hidden = gated_units(gate_up[:, 0], gate_up[:, 1]).astype(bf16)
        saved.append((rows_here, gate_up, hidden))
        return dot_nn(hidden, weight_down)

    ffn_out = pipeline(normed_ffn, forward, lambda t, held, made: (held, made), False)
    result = residual + rms_scale(ffn_out, gain_rows[3])
    block_out = result.astype(bf16).reshape(tokens.shape)
    grad_ffn, gain_terms = norm_back(ffn_out, gain_rows[3], flat_cot)
    gain_last = jnp.sum(gain_terms, axis=0)

    back = []

    def backward(t, grads_here):
        grad_hidden = dot_nt(grads_here, weight_down)
        _, gate_up, _ = saved[t]
        unused, gated_pull = jax.vjp(gated_units, gate_up[:, 0], gate_up[:, 1])
        grad_gate, grad_up = gated_pull(grad_hidden)
        units = jnp.stack([grad_gate, grad_up], axis=1).astype(bf16)
        back.append((grads_here, units))
        return jnp.einsum("tgf,fgd->td", units, weight_gate_up, preferred_element_type=f32)

    def backward_aside(t, held, made):
        if t == chips - 2:
            held, made, kept["lanes"] = lax.optimization_barrier((held, made, kept["lanes"]))
        return held, made

    grad_normed_ffn = pipeline(grad_ffn.astype(bf16), backward, backward_aside, True)
    ffn_in = jnp.concatenate([rows_here for rows_here, _, _ in saved], axis=0)
    hidden = jnp.concatenate([units for _, _, units in saved], axis=0)
    grad_ffn_all = jnp.concatenate([grads_here for grads_here, _ in back], axis=0)
    units = jnp.concatenate([part for _, part in back], axis=0)
    gate_grad, up_grad, down_grad = lax.psum(
        (
            dot_tn(units[:, 0], ffn_in).astype(bf16),
            dot_tn(units[:, 1], ffn_in).astype(bf16),
            dot_tn(hidden, grad_ffn_all).astype(bf16),
        ),
        "seq",
    )

    other_lanes = lax.ppermute(kept["lanes"], "fsdp", swap)
    weight_out_all = all_columns(kept["lanes"], other_lanes, per + 2, 2 * per + 2)
    grad_normed_ffn, weight_out_all = lax.optimization_barrier((grad_normed_ffn, weight_out_all))

    def attention_back():
        weight_in_all = all_columns(kept["lanes"], other_lanes, 0, per + 2)
        grad_mid, gain_pre_ffn = norm_back(residual, gain_rows[2], grad_normed_ffn)
        grad_residual = flat_cot + grad_mid
        grad_attn, gain_post_attn = norm_back(attn_out, gain_rows[1], grad_residual)
        grad_attn_low = grad_attn.astype(bf16)
        grad_mixed = (
            dot_nt(grad_attn_low, weight_out_all)
            .astype(bf16)
            .reshape(seqs, rows, columns, per * HD)
        )
        grad_heads = lax.all_to_all(
            grad_mixed.transpose(2, 0, 1, 3), "seq", split_axis=0, concat_axis=0, tiled=True
        )
        mixed_rows = lax.all_to_all(mixed, "seq", split_axis=0, concat_axis=0, tiled=True)
        mixed_rows = mixed_rows.transpose(1, 2, 0, 3).reshape(own_rows, HQ * HD)
        shard_cols = attn_weight.shape[0]
        first_owner = (HQ + 2 * KVH) * HD // shard_cols // 2
        later_pieces = direct_pieces(
            grad_attn_low, shard, shards, range(first_owner, shards // 2)
        )
        grad_queries, grad_kv = attend_back(shard_arg, queries, grad_heads, lse, kv_all)
        grad_kv_own = (
            ring_scatter(grad_kv.reshape(shards, columns * own_rows, 2 * HD), shard, shards)
            .astype(bf16)
            .reshape(columns, seqs, rows, 2 * HD)
        )
        grad_proj = lax.all_to_all(
            jnp.concatenate([grad_queries, grad_kv_own], axis=-1),
            "seq",
            split_axis=0,
            concat_axis=0,
            tiled=True,
        )
        attn_pieces, grad_proj = later_pieces(grad_proj)
        grad_rows = grad_proj.reshape(columns, own_rows, (per + 2) * HD).transpose(1, 0, 2)
        grad_normed = dot_nn(grad_rows.reshape(own_rows, -1), weight_in_all)
        grad_tokens, gain_pre_attn = norm_back(flat_tokens, gain_rows[0], grad_normed)
        token_grad = (grad_residual + grad_tokens).reshape(tokens.shape)

        def shared(copies):
            if columns == KVH:
                return copies.reshape(own_rows, -1)
            summed = copies.reshape(own_rows, KVH, columns // KVH, HD).astype(f32).sum(axis=2)
            return summed.astype(bf16).reshape(own_rows, -1)

        weight_cols = jnp.concatenate(
            [
                grad_rows[:, :, : per * HD].reshape(own_rows, -1),
                shared(grad_rows[:, :, per * HD : (per + 1) * HD]),
                shared(grad_rows[:, :, (per + 1) * HD :]),
                mixed_rows,
            ],
            axis=1,
        )
        col_all = lax.all_to_all(
            weight_cols.reshape(own_rows, shards, shard_cols).transpose(1, 0, 2),
            "fsdp",
            split_axis=0,
            concat_axis=0,
            tiled=True,
        ).reshape(-1, shard_cols)
        limit = jnp.clip((HQ + 2 * KVH) * HD - shard * shard_cols, 0, shard_cols)
        attn_grad = weight_grad(col_all, limit, normed_pieces, attn_pieces)
        gain_grad = jnp.stack(
            [
                jnp.sum(gain_pre_attn, axis=0),
                jnp.sum(gain_post_attn, axis=0),
                jnp.sum(gain_pre_ffn, axis=0),
                gain_last,
            ]
        )
        return attn_grad, gain_grad, token_grad

    def nothing():
        return (
            jnp.zeros(attn_weight.shape, bf16),
            jnp.zeros((norm_gains.shape[0], width), f32),
            jnp.zeros(tokens.shape, f32),
        )

    attn_grad, gain_grad, token_grad = lax.cond(
        shard < 2**20, attention_back, nothing
    )
    gain_grad = lax.dynamic_slice_in_dim(
        sum_over(gain_grad, "fsdp", shards),
        shard * norm_gains.shape[1],
        norm_gains.shape[1],
        1,
    )
    if columns == 4:

        def with_gains(*come):
            nonlocal gain_grad
            if len(come) == 1:
                gain_grad = sum_over(gain_grad, "seq", columns)
                come, gain_grad = lax.optimization_barrier((come[0], gain_grad))
                return come
            return lax.optimization_barrier(come)

        attn_total, gate_grad, up_grad, down_grad = column_total(
            attn_grad, column, with_gains, (gate_grad, up_grad, down_grad)
        )
    else:
        attn_grad, gate_grad, up_grad, down_grad = lax.optimization_barrier(
            (attn_grad, gate_grad, up_grad, down_grad)
        )
        attn_total = lax.psum(attn_grad, "seq").astype(f32)
        gain_grad = sum_over(gain_grad, "seq", columns)
    gain_total = gain_grad
    ffn_grad = widen_plane(down_grad, 2, 3, None)
    ffn_grad = widen_plane(gate_grad, 0, 3, ffn_grad)
    ffn_grad = widen_plane(up_grad, 1, 3, ffn_grad)
    ffn_grad = ffn_grad.transpose(1, 0, 2)
    return (block_out, token_grad, attn_total, gain_total, ffn_grad)


def solution(mesh):
    in_specs = (
        P(None, ("seq", "fsdp"), None),
        P("fsdp", None),
        P(None, "fsdp"),
        P("fsdp", None, None),
        P(None, ("seq", "fsdp"), None),
    )
    out_specs = (
        P(None, ("seq", "fsdp"), None),
        P(None, ("seq", "fsdp"), None),
        P("fsdp", None),
        P(None, "fsdp"),
        P("fsdp", None, None),
    )
    return jax.shard_map(local, mesh=mesh, in_specs=in_specs, out_specs=out_specs, check_vma=False)
```

```python
import functools

import jax
import jax.numpy as jnp
import numpy as np
from jax import lax
from jax.experimental import pallas as pl
from jax.experimental.pallas import tpu as pltpu
from jax.sharding import PartitionSpec as P

HQ = 8
KVH = 4
HD = 256
GROUP = HQ // KVH
HALF = HD // 2

soft_cap = 50.0
norm_eps = 1e-06
bf16 = jnp.bfloat16
f32 = jnp.float32


def rms_scale(values, gain_row):
    return (
        values * lax.rsqrt(jnp.mean(values * values, axis=-1, keepdims=True) + norm_eps) * gain_row
    )


def norm_back(values, gain_row, cotangent):
    inverse = lax.rsqrt(jnp.mean(values * values, axis=-1, keepdims=True) + norm_eps)
    unit_rows = values * inverse
    scaled = cotangent * gain_row
    grad_values = inverse * (
        scaled - unit_rows * jnp.mean(scaled * unit_rows, axis=-1, keepdims=True)
    )
    return (grad_values, cotangent * unit_rows)


def gated_units(gate_proj, up_proj):
    return jax.nn.gelu(gate_proj, approximate=True) * up_proj


def dot_nt(a, b):
    return lax.dot_general(a, b, (((1,), (1,)), ((), ())), preferred_element_type=f32)


def dot_nn(a, b):
    return lax.dot_general(a, b, (((1,), (0,)), ((), ())), preferred_element_type=f32)


def dot_tn(a, b):
    return lax.dot_general(a, b, (((0,), (0,)), ((), ())), preferred_element_type=f32)


def stacked_heads(block):
    heads = block.shape[1] // HD
    return jnp.concatenate([block[:, h * HD : (h + 1) * HD] for h in range(heads)], axis=0)


def visible_of(shard, rows, keys, lines):
    shape = (lines, keys)
    row = lax.broadcasted_iota(jnp.int32, shape, 0) & (rows - 1)
    col = lax.broadcasted_iota(jnp.int32, shape, 1)
    return col <= shard * rows + row


def lane_sums(values):
    return sum(values[:, low : low + 128] for low in range(0, values.shape[1], 128))


def attend_kernel(shard_ref, q_ref, kv_ref, o_ref, lse_ref, weight_ref):
    own = pl.program_id(1)
    shard = shard_ref[0]
    parts, _, _, rows, _ = kv_ref.shape
    keys = parts * rows
    queries = stacked_heads(q_ref[0, 0])
    lines = queries.shape[0]

    def exponentials(block):
        key_block = kv_ref[:, block, 0, :, :HD].reshape(keys, HD)
        bounded = jnp.tanh(dot_nt(queries, key_block) * (HD ** (-0.5) / soft_cap))
        return jnp.exp(soft_cap * bounded)

    def score_step(block, total):
        expanded = exponentials(block)
        weight_ref[block] = expanded
        return total + lane_sums(expanded)

    total = lax.fori_loop(0, own, score_step, jnp.zeros((lines, 128), f32))
    expanded = jnp.where(visible_of(shard, rows, keys, lines), exponentials(own), 0.0)
    weight_ref[own] = expanded
    total = jnp.sum(total + lane_sums(expanded), axis=-1, keepdims=True)
    inverse = 1.0 / total

    def mix_step(block, mixed):
        weights = (weight_ref[block] * inverse).astype(bf16)
        value_block = kv_ref[:, block, 0, :, HD:].reshape(keys, HD)
        return mixed + dot_nn(weights, value_block)

    mixed = lax.fori_loop(0, own + 1, mix_step, jnp.zeros((lines, HD), f32))
    for h in range(lines // rows):
        o_ref[0, 0, :, h * HD : (h + 1) * HD] = mixed[h * rows : (h + 1) * rows].astype(bf16)
    lse_ref[0, 0] = jnp.broadcast_to(jnp.log(total), (lines, 128))


def attend_back_kernel(
    shard_ref, q_ref, do_ref, lse_ref, kv_ref, dq_ref, dkv_ref, weight_ref, dp_ref, acc_ref
):
    own = pl.program_id(1)
    shard = shard_ref[0]
    parts, blocks, _, rows, _ = kv_ref.shape
    keys = parts * rows
    queries = stacked_heads(q_ref[0, 0])
    grads = stacked_heads(do_ref[0, 0])
    lse = lse_ref[0, 0][:, :1]
    lines = queries.shape[0]

    @pl.when(own == 0)
    def _():
        acc_ref[...] = jnp.zeros_like(acc_ref)

    def first_part(block, masked):
        key_block = kv_ref[:, block, 0, :, :HD].reshape(keys, HD)
        value_block = kv_ref[:, block, 0, :, HD:].reshape(keys, HD)
        bounded = jnp.tanh(dot_nt(queries, key_block) * (HD ** (-0.5) / soft_cap))
        weights = jnp.exp(soft_cap * bounded - lse)
        if masked:
            weights = jnp.where(visible_of(shard, rows, keys, lines), weights, 0.0)
        grad_weights = dot_nt(grads, value_block)
        acc_ref[block, :, HD:] += dot_tn(weights.astype(bf16), grads)
        weight_ref[block] = weights * (1.0 - bounded * bounded)
        dp_ref[block] = grad_weights
        return lane_sums(weights * grad_weights)

    delta = lax.fori_loop(
        0,
        own,
        lambda block, delta: delta + first_part(block, False),
        jnp.zeros((lines, 128), f32),
    )
    delta = jnp.sum(delta + first_part(own, True), axis=-1, keepdims=True)

    def second_step(block, grad_query):
        key_block = kv_ref[:, block, 0, :, :HD].reshape(keys, HD)
        grad_raw = (weight_ref[block] * (dp_ref[block] - delta)).astype(bf16)
        acc_ref[block, :, :HD] += dot_tn(grad_raw, queries)
        return grad_query + dot_nn(grad_raw, key_block)

    grad_query = lax.fori_loop(0, own + 1, second_step, jnp.zeros((lines, HD), f32)) * HD ** (-0.5)
    for h in range(lines // rows):
        dq_ref[0, 0, :, h * HD : (h + 1) * HD] = grad_query[h * rows : (h + 1) * rows].astype(bf16)

    @pl.when(own == blocks - 1)
    def _():
        for block in range(blocks):
            dkv_ref[:, block, 0, :, :HD] = (
                (acc_ref[block, :, :HD] * HD ** (-0.5)).astype(bf16).reshape(parts, rows, HD)
            )
            dkv_ref[:, block, 0, :, HD:] = (
                acc_ref[block, :, HD:].astype(bf16).reshape(parts, rows, HD)
            )


def attend(shard, queries, kv_all):
    blocks, seqs, rows, width = queries.shape
    lines = rows * width // HD
    parts = kv_all.shape[0]
    keys = parts * rows
    row_spec = pl.BlockSpec((1, 1, rows, width), lambda n, s, shard: (s, n, 0, 0))
    lse_spec = pl.BlockSpec((1, 1, lines, 128), lambda n, s, shard: (s, n, 0, 0))
    kv_spec = pl.BlockSpec((parts, blocks, 1, rows, 2 * HD), lambda n, s, shard: (0, 0, n, 0, 0))
    return pl.pallas_call(
        attend_kernel,
        grid_spec=pltpu.PrefetchScalarGridSpec(
            num_scalar_prefetch=1,
            grid=(seqs, blocks),
            in_specs=[row_spec, kv_spec],
            out_specs=[row_spec, lse_spec],
            scratch_shapes=[pltpu.VMEM((blocks, lines, keys), f32)],
        ),
        out_shape=[
            jax.ShapeDtypeStruct(queries.shape, bf16),
            jax.ShapeDtypeStruct((blocks, seqs, lines, 128), f32),
        ],
        compiler_params=pltpu.CompilerParams(vmem_limit_bytes=48 * 2**20),
        name="attend",
    )(shard, queries, kv_all)


def attend_back(shard, queries, grads, lse, kv_all):
    blocks, seqs, rows, width = queries.shape
    lines = rows * width // HD
    parts = kv_all.shape[0]
    keys = parts * rows
    row_spec = pl.BlockSpec((1, 1, rows, width), lambda n, s, shard: (s, n, 0, 0))
    lse_spec = pl.BlockSpec((1, 1, lines, 128), lambda n, s, shard: (s, n, 0, 0))
    deep = 2 if keys * blocks <= 4096 else 1
    kv_spec = pl.BlockSpec(
        (parts, blocks, 1, rows, 2 * HD),
        lambda n, s, shard: (0, 0, n, 0, 0),
        pipeline_mode=pl.Buffered(deep),
    )
    return pl.pallas_call(
        attend_back_kernel,
        grid_spec=pltpu.PrefetchScalarGridSpec(
            num_scalar_prefetch=1,
            grid=(seqs, blocks),
            in_specs=[row_spec, row_spec, lse_spec, kv_spec],
            out_specs=[row_spec, kv_spec],
            scratch_shapes=[
                pltpu.VMEM((blocks, lines, keys), f32),
                pltpu.VMEM((blocks, lines, keys), f32),
                pltpu.VMEM((blocks, keys, 2 * HD), f32),
            ],
        ),
        out_shape=[
            jax.ShapeDtypeStruct(queries.shape, bf16),
            jax.ShapeDtypeStruct(kv_all.shape, bf16),
        ],
        compiler_params=pltpu.CompilerParams(vmem_limit_bytes=56 * 2**20),
        name="attend_back",
    )(shard, queries, grads, lse, kv_all)


def widen_kernel(*refs):
    refs[-1][0] = refs[0][...].astype(f32)


def widen_plane(plane, index, planes, whole):
    rows, width = plane.shape
    step = rows // 4 if rows % 64 == 0 else rows
    specs = [pl.BlockSpec((step, width), lambda i: (i, 0))]
    args = [plane]
    aliases = {}
    if whole is not None:
        specs.append(pl.BlockSpec(memory_space=pl.ANY))
        args.append(whole)
        aliases = {1: 0}
    return pl.pallas_call(
        widen_kernel,
        grid=(rows // step,),
        in_specs=specs,
        out_specs=pl.BlockSpec((1, step, width), lambda i: (index, i, 0)),
        out_shape=jax.ShapeDtypeStruct((planes, rows, width), f32),
        input_output_aliases=aliases,
        compiler_params=pltpu.CompilerParams(vmem_limit_bytes=40 * 2**20),
        name="widen",
    )(*args)


def granules_of(column, columns):
    per = HQ // columns
    first = column * per
    return (
        [first + i for i in range(per)]
        + [HQ + first // GROUP, HQ + KVH + first // GROUP]
        + [HQ + 2 * KVH + first + i for i in range(per)]
    )


def route(columns, chips, per_chip):
    items = len(granules_of(0, columns))
    urgent = items - HQ // columns
    rank = [1] * (urgent - 2) + [0] * 2 + [2] * (items - urgent)
    source = [[g // per_chip for g in granules_of(c, columns)] for c in range(columns)]
    held = [[{k for k in range(items) if source[c][k] == z} for z in range(chips)] for c in range(columns)]
    steps = []
    urgent_steps = kv_steps = None
    while any(len(held[c][z]) < items for c in range(columns) for z in range(chips)):
        moves = {}
        for c in range(columns):
            for z in range(chips):
                for core, way in ((0, 1), (1, -1)):
                    if not 0 <= z + way < chips:
                        continue
                    ready = [
                        k
                        for k in held[c][z]
                        if k not in held[c][z + way] and (source[c][k] - z) * way <= 0
                    ]
                    if ready:
                        moves[c, z, core] = min(
                            ready, key=lambda k: (rank[k], abs(source[c][k] - z), k)
                        )
        for (c, z, core), k in moves.items():
            held[c][z + (1, -1)[core]].add(k)
        steps.append(moves)
        done = all(k in held[c][z] for c in range(columns) for z in range(chips) for k in range(urgent))
        if done and urgent_steps is None:
            urgent_steps = len(steps)
        done = all(
            k in held[c][z]
            for c in range(columns)
            for z in range(chips)
            for k in (urgent - 2, urgent - 1)
        )
        if done and kv_steps is None:
            kv_steps = len(steps)
    return steps, urgent_steps, kv_steps


def chosen(places, devices):
    names = []
    which = np.zeros((devices, len(places)), np.int32)
    slot = np.zeros((devices, len(places)), np.int32)
    for k, place in enumerate(places):
        for d in range(devices):
            name, at = place.get(d, ("mine", 0))
            if name not in names:
                names.append(name)
            which[d, k] = names.index(name)
            slot[d, k] = at
    return names, which, slot


def fetch(cands, which_ref, slot_ref, sources, place, buffer, sem):
    for code in cands[place]:

        @pl.when(which_ref[place] == code)
        def _(code=code):
            pltpu.make_async_copy(sources[code].at[slot_ref[place]], buffer, sem).start()


def pick_kernel(cands, which_ref, slot_ref, *refs):
    out_ref, buffers, in_sems, out_sems = refs[-4:]
    count, deep = len(cands), buffers.shape[0]

    def begin(k):
        at = k % deep
        fetch(cands, which_ref, slot_ref, refs, k, buffers.at[at], in_sems.at[at])

    def leaving(k):
        at = k % deep
        return pltpu.make_async_copy(buffers.at[at], out_ref.at[k], out_sems.at[at])

    for k in range(min(deep, count)):
        begin(k)
    for k in range(count):
        at = k % deep
        pltpu.make_async_copy(buffers.at[at], buffers.at[at], in_sems.at[at]).wait()
        leaving(k).start()
        again = k - deep // 2
        if again >= 0 and again + deep < count:
            leaving(again).wait()
            begin(again + deep)
    for k in range(max(0, count - deep), count):
        leaving(k).wait()


def project_kernel(cands, which_ref, slot_ref, rows_ref, *refs):
    out_ref, buffers, sems = refs[-3:]
    rows = buffers.shape[1]
    for k in range(len(cands)):
        fetch(cands, which_ref, slot_ref, refs, k, buffers.at[k], sems.at[k])
    for k in range(len(cands)):
        pltpu.make_async_copy(buffers.at[k], buffers.at[k], sems.at[k]).wait()
        out_ref[:, k * rows : (k + 1) * rows] = dot_nt(rows_ref[...], buffers[k]).astype(bf16)


def apply_kernel(cands, which_ref, slot_ref, rows_ref, *refs):
    out_ref, buffers, sems = refs[-3:]
    _, rows, width = buffers.shape
    for k in range(len(cands)):
        fetch(cands, which_ref, slot_ref, refs, k, buffers.at[k], sems.at[k])
    for k in range(len(cands)):
        pltpu.make_async_copy(buffers.at[k], buffers.at[k], sems.at[k]).wait()
    step = width // 3 if width % 384 == 0 else width
    for low in range(0, width, step):
        total = dot_nn(rows_ref[:, :rows], buffers[0, :, low : low + step])
        for k in range(1, len(cands)):
            total += dot_nn(
                rows_ref[:, k * rows : (k + 1) * rows], buffers[k, :, low : low + step]
            )
        out_ref[:, low : low + step] = total.astype(bf16)


def pick(places, sources, device, devices, kind="pick", rows_in=None):
    names, which, slot = chosen(places, devices)
    _, rows, width = sources["mine"].shape
    table = jnp.asarray(np.concatenate([which, slot], axis=1))[device]
    count = len(places)
    cands = [sorted(set(which[:, k].tolist())) for k in range(count)]
    kernel = {"pick": pick_kernel, "project": project_kernel, "apply": apply_kernel}[kind]
    args = [sources[name] for name in names]
    in_specs = [pl.BlockSpec(memory_space=pl.ANY)] * len(names)
    if kind == "pick":
        deep = min(count, 8)
        out_spec = pl.BlockSpec(memory_space=pl.ANY)
        out_shape = (count, rows, width)
        sems = [pltpu.SemaphoreType.DMA((deep,)), pltpu.SemaphoreType.DMA((deep,))]
    else:
        deep = count
        args = [rows_in] + args
        in_specs = [pl.BlockSpec(memory_space=pltpu.VMEM)] + in_specs
        out_spec = pl.BlockSpec(memory_space=pltpu.VMEM)
        out_shape = (rows_in.shape[0], count * rows if kind == "project" else width)
        sems = [pltpu.SemaphoreType.DMA((deep,))]
    return pl.pallas_call(
        functools.partial(kernel, cands),
        grid_spec=pltpu.PrefetchScalarGridSpec(
            num_scalar_prefetch=2,
            grid=(1,),
            in_specs=in_specs,
            out_specs=out_spec,
            scratch_shapes=[pltpu.VMEM((deep, rows, width), bf16)] + sems,
        ),
        out_shape=jax.ShapeDtypeStruct(out_shape, bf16),
        compiler_params=pltpu.CompilerParams(vmem_limit_bytes=58 * 2**20),
        name=kind,
    )(table[:count], table[count:], *args)


def routed_weights(attn_weight, column, shard, columns, shards, between):
    rows, width = attn_weight.shape
    count = rows // HD
    chips = shards // 2
    devices = columns * shards
    device = column * shards + shard
    swap = [(f, f ^ 1) for f in range(shards)]
    items = len(granules_of(0, columns))
    urgent = items - HQ // columns
    steps, urgent_steps, kv_steps = route(columns, chips, 2 * count)
    mine = attn_weight.reshape(count, HD, width)
    theirs = between("start", lax.ppermute(mine, "fsdp", swap))
    sources = {"mine": mine, "theirs": theirs}
    at = [{} for _ in range(items)]
    for c in range(columns):
        for f in range(shards):
            for k, g in enumerate(granules_of(c, columns)):
                if g // (2 * count) == f // 2:
                    at[k][c * shards + f] = ("mine" if g // count == f else "theirs", g % count)
    sends = []
    for number, moves in enumerate(steps):
        own, passed, pairs = {}, {}, []
        for (c, z, core), k in moves.items():
            here = c * shards + 2 * z + core
            to = here + (2, -2)[core]
            name, slot = at[k][here]
            if name in ("mine", "theirs"):
                own[here] = (name, slot)
            else:
                passed[here] = name
            pairs.append((here, to))
            at[k][to] = ("got%d" % number, 0)
            at[k][to ^ 1] = ("swapped%d" % number, 0)
        sends.append((own, passed, pairs))
    with_own = [n for n in range(1, len(sends)) if sends[n][0]]
    own_first = pick([sends[0][0]], sources, device, devices)
    own_later = None
    for number, (own, passed, pairs) in enumerate(sends):
        if number == 0:
            piece = own_first
        else:
            names = sorted(set(passed.values()))
            code = np.zeros((devices,), np.int32)
            for d, name in passed.items():
                code[d] = 1 + names.index(name)
            here = jnp.asarray(code)[device]
            piece = sources[names[-1]]
            for i, name in enumerate(names[:-1]):
                piece = jnp.where(here == 1 + i, sources[name], piece)
            if number in with_own:
                place = with_own.index(number)
                piece = jnp.where(here == 0, own_later[place : place + 1], piece)
        got = lax.ppermute(piece, ("seq", "fsdp"), pairs)
        if number == 0:
            own_later = pick([sends[n][0] for n in with_own], sources, device, devices)
            got, own_later = lax.optimization_barrier((got, own_later))
        if number < urgent_steps:
            got = between(number, got)
        if 0 < number < urgent_steps:
            before = "swapped%d" % (number - 1)
            got, sources[before] = lax.optimization_barrier((got, sources[before]))
        sources["got%d" % number] = got
        if number < urgent_steps:
            sources["swapped%d" % number] = lax.ppermute(got, "fsdp", swap)
        for name, wanted, count_of in (
            ("kv", (urgent - 2, urgent), kv_steps),
            ("q", (0, urgent - 2), urgent_steps),
        ):
            if number + 1 == count_of:
                ready = dict(sources)
                places = [dict(place) for place in at[slice(*wanted)]]
                between(
                    name,
                    lambda times, ready=ready, places=places: pick(
                        places, ready, device, devices, "project", times
                    ),
                )

    def first(after):
        held, after = lax.optimization_barrier((ready, after))
        return pick(at[:urgent], held, device, devices)

    held = None

    def times_rest(rows_in):
        nonlocal held
        held, rows_in = lax.optimization_barrier((sources, rows_in))
        for number in range(urgent_steps, len(steps)):
            held["swapped%d" % number] = lax.ppermute(held["got%d" % number], "fsdp", swap)
        return pick(at[urgent:], held, device, devices, "apply", rows_in)

    def others(after):
        kept, after = lax.optimization_barrier((held, after))
        return pick(at[urgent:], kept, device, devices)

    return first, times_rest, others


def column_weights(attn_weight, column, shard, columns, shards, between):
    rows, width = attn_weight.shape
    per = HQ // columns
    if rows % HD == 0 and shards == 8 and columns == 4:
        return routed_weights(attn_weight, column, shard, columns, shards, between)
    whole = lax.all_gather(attn_weight, "fsdp", axis=0, tiled=True).reshape(-1, HD, width)
    table = np.array([granules_of(c, columns) for c in range(columns)], np.int32)
    place = jnp.asarray(table)[column]
    taken = jnp.concatenate(
        [lax.dynamic_slice_in_dim(whole, place[k], 1, 0) for k in range(table.shape[1])], axis=0
    )
    for name, low, high in (("kv", per, per + 2), ("q", 0, per)):
        between(
            name,
            lambda times, low=low, high=high: dot_nt(
                times, taken[low:high].reshape(-1, width)
            ).astype(bf16),
        )
    return (
        lambda after: taken[: per + 2],
        lambda rows_in: dot_nn(rows_in, taken[per + 2 :].reshape(-1, width)).astype(bf16),
        lambda after: taken[per + 2 :],
    )


def ring_of(chips):
    return [0] + list(range(1, chips, 2)) + [z for z in range(chips - 1, 0, -1) if z % 2 == 0]


def ring_tables(shards):
    chips = shards // 2
    order = ring_of(chips)
    spot = {z: p for p, z in enumerate(order)}
    pairs = [
        (2 * z + c, 2 * order[(spot[z] + 1) % chips] + c) for z in range(chips) for c in range(2)
    ]
    behind = np.array(
        [[order[(spot[f // 2] - t) % chips] for t in range(chips + 1)] for f in range(shards)],
        np.int32,
    )
    return chips, pairs, behind


def ring_pieces(block, shard, shards, beside):
    chips, pairs, behind = ring_tables(shards)
    swap = [(f, f ^ 1) for f in range(shards)]
    source = jnp.asarray(behind)[shard]
    core = shard % 2
    pieces = []
    held = block
    for t in range(chips):
        if t:
            held = lax.ppermute(held, "fsdp", pairs)
            held = beside(t, held)
        pieces.append((held, 2 * source[t] + core))
        pieces.append((lax.ppermute(held, "fsdp", swap), 2 * source[t] + 1 - core))
    return pieces


def direct_pieces(block, shard, shards, wanted):
    chips = shards // 2
    swap = [(f, f ^ 1) for f in range(shards)]
    core = shard % 2
    come = [block] + [
        lax.ppermute(
            block,
            "fsdp",
            [
                (f, (f + 2 * hop) % shards)
                for f in range(shards)
                if (f + 2 * hop) % shards // 2 in wanted
            ],
        )
        for hop in range(1, chips)
    ]

    def finish(after):
        held, after = lax.optimization_barrier((come, after))
        pieces = []
        for hop, piece in enumerate(held):
            chip = (shard // 2 - hop) % chips
            pieces.append((piece, 2 * chip + core))
            pieces.append((lax.ppermute(piece, "fsdp", swap), 2 * chip + 1 - core))
        return pieces, after

    return finish


def weight_grad_kernel(half, place_ref, cols_ref, *refs):
    pieces = refs[: 2 * half]
    out_ref, rows_ref, turned_ref, sems = refs[2 * half :]
    lines = pieces[0].shape[0]
    for i, piece in enumerate(pieces):
        start = pl.multiple_of(place_ref[i] * lines, lines)
        pltpu.make_async_copy(
            piece, rows_ref.at[i // half, pl.ds(start, lines)], sems.at[i]
        ).start()
    limit = place_ref[2 * half]
    turned_ref[...] = cols_ref[...].T
    for i, piece in enumerate(pieces):
        pltpu.make_async_copy(piece, rows_ref.at[0, pl.ds(0, lines)], sems.at[i]).wait()
    height, width = out_ref.shape
    step = width // 3 if width % 384 == 0 else width
    block = HD if height % HD == 0 else HALF

    def chunk(n, carry):
        cut = pl.ds(pl.multiple_of(n * step, step), step)
        for low in range(0, height, block):
            which = (low >= limit).astype(jnp.int32)
            out_ref[low : low + block, cut] = dot_nn(
                turned_ref[low : low + block], rows_ref[which, :, cut]
            ).astype(bf16)
        return carry

    lax.fori_loop(0, width // step, chunk, 0)


def weight_grad(cols, limit, first, second):
    lines, width = first[0][0].shape
    half = len(first)
    place = jnp.stack(
        [where.astype(jnp.int32) for _, where in first + second] + [limit.astype(jnp.int32)]
    )
    return pl.pallas_call(
        functools.partial(weight_grad_kernel, half),
        grid_spec=pltpu.PrefetchScalarGridSpec(
            num_scalar_prefetch=1,
            grid=(1,),
            in_specs=[pl.BlockSpec(memory_space=pltpu.VMEM)]
            + [pl.BlockSpec(memory_space=pl.ANY)] * (2 * half),
            out_specs=pl.BlockSpec(memory_space=pltpu.VMEM),
            scratch_shapes=[
                pltpu.VMEM((2, half * lines, width), bf16),
                pltpu.VMEM((cols.shape[1], cols.shape[0]), bf16),
                pltpu.SemaphoreType.DMA((2 * half,)),
            ],
        ),
        out_shape=jax.ShapeDtypeStruct((cols.shape[1], width), bf16),
        compiler_params=pltpu.CompilerParams(vmem_limit_bytes=58 * 2**20),
        name="weight_grad",
    )(place, cols, *[piece for piece, _ in first + second])


def ring_scatter(parts, shard, shards):
    chips, pairs, behind = ring_tables(shards)
    swap = [(f, f ^ 1) for f in range(shards)]
    target = jnp.asarray(behind)[shard]
    core = shard % 2
    paired = parts.reshape((chips, 2) + parts.shape[1:])
    mine = lax.dynamic_index_in_dim(paired, core, 1, keepdims=False)
    other = lax.ppermute(
        lax.dynamic_index_in_dim(paired, 1 - core, 1, keepdims=False), "fsdp", swap
    )

    def local_sum(t):
        return lax.dynamic_index_in_dim(mine, target[t], 0, keepdims=False).astype(
            f32
        ) + lax.dynamic_index_in_dim(other, target[t], 0, keepdims=False).astype(f32)

    total = local_sum(1)
    for t in range(1, chips):
        total = lax.ppermute(total.astype(bf16), "fsdp", pairs).astype(f32) + local_sum(t + 1)
    return total


def partners(columns, bit):
    return [(c, c ^ bit) for c in range(columns)]


def column_scatter(parts, beside=None):
    half = parts.shape[-1] // 2
    ways = ((1, 2, slice(0, half)), (2, 1, slice(half, None)))
    come = tuple(
        lax.ppermute(
            jnp.concatenate([parts[first : first + 1, ..., cut], parts[3:, ..., cut]], axis=0),
            "seq",
            partners(4, first),
        )
        for first, _, cut in ways
    )
    if beside:
        come = beside(come)
    done = []
    for (first, second, cut), got in zip(ways, come):
        keep = parts[0, ..., cut].astype(f32) + got[0].astype(f32)
        away = parts[second, ..., cut].astype(f32) + got[1].astype(f32)
        done.append(
            keep + lax.ppermute(away.astype(bf16), "seq", partners(4, second)).astype(f32)
        )
    return jnp.concatenate(done, axis=-1)


def column_total(value, column, beside, later):
    rows, width = value.shape
    step, half = rows // 4, width // 2
    parts = jnp.stack(
        [lax.dynamic_slice_in_dim(value, (column ^ k) * step, step, 0) for k in range(4)]
    )
    own, *later = beside(column_scatter(parts, beside).astype(bf16), *later)
    pieces = (own[:, :half], own[:, half:])
    near = tuple(lax.ppermute(p, "seq", partners(4, bit)) for p, bit in zip(pieces, (1, 2)))
    near, *later = lax.optimization_barrier((near, *later))
    out = jnp.zeros((rows, width), f32)
    for first, second, low, piece, got in (
        (1, 2, 0, pieces[0], near[0]),
        (2, 1, half, pieces[1], near[1]),
    ):
        far = lax.ppermute(jnp.stack([piece, got]), "seq", partners(4, second))
        for k, block in ((0, piece), (first, got), (second, far[0]), (3, far[1])):
            out = lax.dynamic_update_slice(
                out, block.astype(f32), ((column ^ k) * step, low)
            )
    return (out, *later)


def sum_over(value, axis, count):
    bit = 1
    while bit < count:
        value = value + lax.ppermute(value, axis, [(c, c ^ bit) for c in range(count)])
        bit *= 2
    return value


def local(tokens, attn_weight, norm_gains, ffn_weight, out_grad):
    seqs, rows, width = tokens.shape
    columns = lax.axis_size("seq")
    shards = lax.axis_size("fsdp")
    column = lax.axis_index("seq")
    shard = lax.axis_index("fsdp")
    core = shard % 2
    per = HQ // columns
    own_rows = seqs * rows
    swap = [(f, f ^ 1) for f in range(shards)]
    shard_arg = shard.astype(jnp.int32).reshape(1)

    def core_half(granules):
        return lax.dynamic_index_in_dim(
            granules.reshape(-1, 2, HALF, width), core, 1, keepdims=False
        )

    def all_columns(own, other, begin, end):
        count = own.shape[1]
        sources = {
            "mine": own.reshape(columns * count, HALF, width),
            "other": other.reshape(columns * count, HALF, width),
        }
        places = [
            {
                c * shards + f: ("mine" if f % 2 == half else "other", home * count + k)
                for c in range(columns)
                for f in range(shards)
            }
            for home in range(columns)
            for k in range(begin, end)
            for half in range(2)
        ]
        device = column * shards + shard
        return pick(places, sources, device, columns * shards).reshape(-1, width)

    token_slices = lax.all_gather(tokens, "seq", axis=0)
    gain_rows = lax.all_gather(norm_gains, "fsdp", axis=1, tiled=True).astype(f32)
    normed_slices = rms_scale(
        token_slices.reshape(-1, width).astype(f32), gain_rows[0]
    ).astype(bf16)
    made = {}

    def between(step, value):
        nonlocal normed_slices, gain_rows
        if step == "start":
            value, gain_rows = lax.optimization_barrier((value, gain_rows))
            normed_slices = rms_scale(
                token_slices.reshape(-1, width).astype(f32), gain_rows[0]
            ).astype(bf16)
        if step == 1:
            value, normed_slices = lax.optimization_barrier((value, normed_slices))
        if step == 2:
            value, made["kv"] = lax.optimization_barrier((value, made["kv"]))
        if step in ("kv", "q"):
            made[step] = value(normed_slices)
        return value

    first_weights, times_out, out_weights = column_weights(
        attn_weight, column, shard, columns, shards, between
    )
    kv_all = lax.all_gather(made["kv"].reshape(columns, seqs, rows, 2 * HD), "fsdp", axis=0)
    queries = made["q"].reshape(columns, seqs, rows, per * HD)
    flat_tokens = tokens.reshape(-1, width).astype(f32)
    flat_cot = out_grad.reshape(-1, width).astype(f32)
    normed_own = rms_scale(flat_tokens, gain_rows[0]).astype(bf16)
    normed_own, kv_all = lax.optimization_barrier((normed_own, kv_all))
    mixed, lse = attend(shard_arg, queries, kv_all)
    kept = {"mixed": mixed}

    def beside(step, held):
        if step == 1:
            held, kept["mixed"] = lax.optimization_barrier((held, kept["mixed"]))
            if columns == 4:
                by_partner = jnp.concatenate(
                    [
                        lax.dynamic_slice_in_dim(kept["mixed"], column ^ k, 1, 0)
                        for k in range(columns)
                    ],
                    axis=0,
                )
                kept["part"] = times_out(by_partner.reshape(columns * own_rows, per * HD))
            else:
                kept["part"] = times_out(kept["mixed"].reshape(-1, per * HD))
        if step == 2:
            held, kept["part"] = lax.optimization_barrier((held, kept["part"]))
            if columns == 4:
                kept["out"] = column_scatter(kept["part"].reshape(columns, own_rows, width))
            else:
                kept["out"] = lax.psum_scatter(
                    kept["part"], "seq", scatter_dimension=0, tiled=True
                ).astype(f32)
        if step == 3:
            held, kept["out"] = lax.optimization_barrier((held, kept["out"]))
        return held

    normed_pieces = ring_pieces(normed_own, shard, shards, beside)
    mixed, attn_out = kept["mixed"], kept["out"]
    lanes = jnp.concatenate(
        [core_half(first_weights(mixed)), core_half(out_weights(mixed))], axis=0
    )
    attn_out, lanes = lax.optimization_barrier((attn_out, lanes))
    kept["lanes"] = lax.all_gather(lanes, "seq", axis=0)
    residual = flat_tokens + rms_scale(attn_out, gain_rows[1])
    normed_ffn = rms_scale(residual, gain_rows[2]).astype(bf16)

    chips, ring, _ = ring_tables(shards)
    weight_gate_up, weight_down = ffn_weight[:, :2], ffn_weight[:, 2]

    def pipeline(block, work, aside, late):
        held = block
        pairs = []
        for t in range(chips):
            rows_here = jnp.concatenate([held, lax.ppermute(held, "fsdp", swap)], axis=0)
            if t + 1 < chips:
                held = lax.ppermute(held, "fsdp", ring)
            made = work(t, rows_here).astype(bf16)
            got = lax.ppermute(made[own_rows:], "fsdp", swap)
            pair = made[:own_rows].astype(f32) + got.astype(f32)
            pairs.append(pair)
            if t + 1 < chips:
                held, made = aside(t, *lax.optimization_barrier((held, made)))
            if t and not late:
                total = (pair if t == 1 else total + pair).astype(bf16)
                if t + 1 < chips:
                    held, total = lax.optimization_barrier((held, total))
                total = lax.ppermute(total, "fsdp", ring).astype(f32)
        if late:
            total, _ = lax.optimization_barrier((pairs[1].astype(bf16), held))
            total = lax.ppermute(total, "fsdp", ring).astype(f32)
            for pair in pairs[2:]:
                total = (total + pair).astype(bf16)
                total, pairs[-1] = lax.optimization_barrier((total, pairs[-1]))
                total = lax.ppermute(total, "fsdp", ring).astype(f32)
        return total + pairs[0]

    saved = []

    def forward(t, rows_here):
        gate_up = jnp.einsum(
            "td,fgd->tgf", rows_here, weight_gate_up, preferred_element_type=f32
        )
        hidden = gated_units(gate_up[:, 0], gate_up[:, 1]).astype(bf16)
        saved.append((rows_here, gate_up, hidden))
        return dot_nn(hidden, weight_down)

    ffn_out = pipeline(normed_ffn, forward, lambda t, held, made: (held, made), False)
    result = residual + rms_scale(ffn_out, gain_rows[3])
    block_out = result.astype(bf16).reshape(tokens.shape)
    grad_ffn, gain_terms = norm_back(ffn_out, gain_rows[3], flat_cot)
    gain_last = jnp.sum(gain_terms, axis=0)

    back = []

    def backward(t, grads_here):
        grad_hidden = dot_nt(grads_here, weight_down)
        _, gate_up, _ = saved[t]
        unused, gated_pull = jax.vjp(gated_units, gate_up[:, 0], gate_up[:, 1])
        grad_gate, grad_up = gated_pull(grad_hidden)
        units = jnp.stack([grad_gate, grad_up], axis=1).astype(bf16)
        back.append((grads_here, units))
        return jnp.einsum("tgf,fgd->td", units, weight_gate_up, preferred_element_type=f32)

    def backward_aside(t, held, made):
        if t == chips - 2:
            held, made, kept["lanes"] = lax.optimization_barrier((held, made, kept["lanes"]))
        return held, made

    grad_normed_ffn = pipeline(grad_ffn.astype(bf16), backward, backward_aside, True)
    ffn_in = jnp.concatenate([rows_here for rows_here, _, _ in saved], axis=0)
    hidden = jnp.concatenate([units for _, _, units in saved], axis=0)
    grad_ffn_all = jnp.concatenate([grads_here for grads_here, _ in back], axis=0)
    units = jnp.concatenate([part for _, part in back], axis=0)
    gate_grad, up_grad, down_grad = lax.psum(
        (
            dot_tn(units[:, 0], ffn_in).astype(bf16),
            dot_tn(units[:, 1], ffn_in).astype(bf16),
            dot_tn(hidden, grad_ffn_all).astype(bf16),
        ),
        "seq",
    )

    other_lanes = lax.ppermute(kept["lanes"], "fsdp", swap)
    weight_out_all = all_columns(kept["lanes"], other_lanes, per + 2, 2 * per + 2)
    grad_normed_ffn, weight_out_all = lax.optimization_barrier((grad_normed_ffn, weight_out_all))

    def attention_back():
        weight_in_all = all_columns(kept["lanes"], other_lanes, 0, per + 2)
        grad_mid, gain_pre_ffn = norm_back(residual, gain_rows[2], grad_normed_ffn)
        grad_residual = flat_cot + grad_mid
        grad_attn, gain_post_attn = norm_back(attn_out, gain_rows[1], grad_residual)
        grad_attn_low = grad_attn.astype(bf16)
        grad_mixed = (
            dot_nt(grad_attn_low, weight_out_all)
            .astype(bf16)
            .reshape(seqs, rows, columns, per * HD)
        )
        grad_heads = lax.all_to_all(
            grad_mixed.transpose(2, 0, 1, 3), "seq", split_axis=0, concat_axis=0, tiled=True
        )
        mixed_rows = lax.all_to_all(mixed, "seq", split_axis=0, concat_axis=0, tiled=True)
        mixed_rows = mixed_rows.transpose(1, 2, 0, 3).reshape(own_rows, HQ * HD)
        shard_cols = attn_weight.shape[0]
        made = {"heads": grad_heads}

        def beside_back(step, held):
            if step == 1:
                held, made["heads"] = lax.optimization_barrier((held, made["heads"]))
                made["queries"], made["kv"] = attend_back(
                    shard_arg, queries, made["heads"], lse, kv_all
                )
            if step == 2:
                held, made["kv"] = lax.optimization_barrier((held, made["kv"]))
                grad_kv_own = (
                    ring_scatter(
                        made["kv"].reshape(shards, columns * own_rows, 2 * HD), shard, shards
                    )
                    .astype(bf16)
                    .reshape(columns, seqs, rows, 2 * HD)
                )
                made["proj"] = lax.all_to_all(
                    jnp.concatenate([made["queries"], grad_kv_own], axis=-1),
                    "seq",
                    split_axis=0,
                    concat_axis=0,
                    tiled=True,
                )
            if step == 3:
                held, made["proj"] = lax.optimization_barrier((held, made["proj"]))
            return held

        attn_pieces = ring_pieces(grad_attn_low, shard, shards, beside_back)
        grad_proj = made["proj"]
        grad_rows = grad_proj.reshape(columns, own_rows, (per + 2) * HD).transpose(1, 0, 2)
        grad_normed = dot_nn(grad_rows.reshape(own_rows, -1), weight_in_all)
        grad_tokens, gain_pre_attn = norm_back(flat_tokens, gain_rows[0], grad_normed)
        token_grad = (grad_residual + grad_tokens).reshape(tokens.shape)

        def shared(copies):
            if columns == KVH:
                return copies.reshape(own_rows, -1)
            summed = copies.reshape(own_rows, KVH, columns // KVH, HD).astype(f32).sum(axis=2)
            return summed.astype(bf16).reshape(own_rows, -1)

        weight_cols = jnp.concatenate(
            [
                grad_rows[:, :, : per * HD].reshape(own_rows, -1),
                shared(grad_rows[:, :, per * HD : (per + 1) * HD]),
                shared(grad_rows[:, :, (per + 1) * HD :]),
                mixed_rows,
            ],
            axis=1,
        )
        col_all = lax.all_to_all(
            weight_cols.reshape(own_rows, shards, shard_cols).transpose(1, 0, 2),
            "fsdp",
            split_axis=0,
            concat_axis=0,
            tiled=True,
        ).reshape(-1, shard_cols)
        limit = jnp.clip((HQ + 2 * KVH) * HD - shard * shard_cols, 0, shard_cols)
        attn_grad = weight_grad(col_all, limit, normed_pieces, attn_pieces)
        gain_grad = jnp.stack(
            [
                jnp.sum(gain_pre_attn, axis=0),
                jnp.sum(gain_post_attn, axis=0),
                jnp.sum(gain_pre_ffn, axis=0),
                gain_last,
            ]
        )
        return attn_grad, gain_grad, token_grad

    def nothing():
        return (
            jnp.zeros(attn_weight.shape, bf16),
            jnp.zeros((norm_gains.shape[0], width), f32),
            jnp.zeros(tokens.shape, f32),
        )

    attn_grad, gain_grad, token_grad = lax.cond(
        shard < 2**20, attention_back, nothing
    )
    gain_grad = lax.dynamic_slice_in_dim(
        sum_over(gain_grad, "fsdp", shards),
        shard * norm_gains.shape[1],
        norm_gains.shape[1],
        1,
    )
    if columns == 4:

        def with_gains(*come):
            nonlocal gain_grad
            if len(come) == 1:
                gain_grad = sum_over(gain_grad, "seq", columns)
                come, gain_grad = lax.optimization_barrier((come[0], gain_grad))
                return come
            return lax.optimization_barrier(come)

        attn_total, gate_grad, up_grad, down_grad = column_total(
            attn_grad, column, with_gains, (gate_grad, up_grad, down_grad)
        )
    else:
        attn_grad, gate_grad, up_grad, down_grad = lax.optimization_barrier(
            (attn_grad, gate_grad, up_grad, down_grad)
        )
        attn_total = lax.psum(attn_grad, "seq").astype(f32)
        gain_grad = sum_over(gain_grad, "seq", columns)
    gain_total = gain_grad
    ffn_grad = widen_plane(down_grad, 2, 3, None)
    ffn_grad = widen_plane(gate_grad, 0, 3, ffn_grad)
    ffn_grad = widen_plane(up_grad, 1, 3, ffn_grad)
    ffn_grad = ffn_grad.transpose(1, 0, 2)
    return (block_out, token_grad, attn_total, gain_total, ffn_grad)


def solution(mesh):
    in_specs = (
        P(None, ("seq", "fsdp"), None),
        P("fsdp", None),
        P(None, "fsdp"),
        P("fsdp", None, None),
        P(None, ("seq", "fsdp"), None),
    )
    out_specs = (
        P(None, ("seq", "fsdp"), None),
        P(None, ("seq", "fsdp"), None),
        P("fsdp", None),
        P(None, "fsdp"),
        P("fsdp", None, None),
    )
    return jax.shard_map(local, mesh=mesh, in_specs=in_specs, out_specs=out_specs, check_vma=False)
```
